32 devices in a mesh: blk: 8 (over z, x), rep: 4 (over y, core).
Axes of the slice: x: 2, y: 2, z: 4, core: 2. Of those that a mesh axis runs over, the one named last changes fastest.
Arguments:
- features: bfloat16 [8192, 256], P('blk'), may hold values from -6 to 6
- degree: int32 [8192], P('blk'), may hold values from 1 to 8
- order: int32 [8, 1024], P('blk'), may hold values from 0 to 1023, each once within a row
- tile_rows: int32 [8, 4, 48], P('blk', 'rep'), may hold values from 0 to 7
- tile_cols: int32 [8, 4, 48], P('blk', 'rep'), may hold values from 0 to 23
- tile_count: int32 [8, 4], P('blk', 'rep'), may hold values from 1 to 48, as said below
- tile_values: bfloat16 [8, 4, 48, 128, 128], P('blk', 'rep'), may hold values from -0.14941406 to 0.14941406
- w_self: bfloat16 [256, 256], replicated, may hold values from -0.375 to 0.375
- w_neigh: bfloat16 [256, 256], replicated, may hold values from -0.375 to 0.375
- out_grad: bfloat16 [8192, 256], P('blk'), may hold values from -6 to 6
Outputs:
- output: bfloat16 [8192, 256], P('blk')
- grad_features: bfloat16 [8192, 256], P('blk')
- grad_self: float32 [256, 256], replicated
- grad_neigh: float32 [256, 256], replicated
The draws below stay inside these ranges and needn't reach their ends.
Inputs may be any that keep to these rules, and one draw needn't show every extreme that they name: `tile_count`: some group of some block has all 48 slots live in every draw.
All inputs are finite; a program needn't handle non-finite values.
Results may differ from the reference program's by a relative error of at most 0.0095.
Values may be sent and summed in bfloat16 or wider, within the bound.
No kernel may reach another device: no remote copies, remote signals or barrier semaphores. Data moves between devices by JAX's collectives and lax.ppermute only.
A program may use at most 64 MiB of HBM per device.

```python
import jax
import jax.numpy as jnp
from jax import lax

F = 256
NB = 1024
TILES_DEV = 48
BLOCKS = 8
REPS = 4
N = 8192
RT = 8


def draw_tile_count(key, part):
    key = jax.random.fold_in(key, 7)
    first, second, third = jax.random.split(key, 3)
    busy = jax.random.randint(first, (BLOCKS, REPS), 0, 4) == 0
    light = jax.random.randint(second, (BLOCKS, REPS), 1, TILES_DEV // 2 + 1)
    counts = jnp.where(busy, TILES_DEV, light).reshape(-1)
    spot = jax.random.randint(third, (), 0, BLOCKS * REPS)
    counts = jnp.where(jnp.arange(BLOCKS * REPS) == spot, TILES_DEV, counts)
    return counts.reshape(BLOCKS, REPS).astype(jnp.int32)


def plant(entries, rng, smallest, largest):
    longest = entries.shape.index(max(entries.shape))
    spots = []
    for shift in (0, 1):
        where = [jax.random.randint(jax.random.fold_in(rng, axis), (), 0, length) for axis, length in enumerate(entries.shape)]
        where[longest] = (where[longest] + shift) % entries.shape[longest]
        spots.append(tuple(where))
    return entries.at[spots[0]].set(smallest).at[spots[1]].set(largest)


def steps_of(rng, extent, shards, least, top_value):
    def one(position, blocks):
        steps = jax.random.uniform(jax.random.fold_in(jax.random.fold_in(rng, 6), position), (blocks,), jnp.float32, least / len(shards), top_value / len(shards))
        return jnp.repeat(jnp.exp(steps), extent[position] // blocks).reshape((-1,) + (1,) * (len(extent) - position - 1))

    level = one(*shards[0])
    for cut in shards[1:]:
        level = level * one(*cut)
    return level


def noise(rng, extent, spread, limit, pieces=(), kind=jnp.bfloat16):
    entries = spread * jax.random.normal(rng, extent, jnp.float32)
    if pieces:
        entries = entries * steps_of(rng, extent, pieces, -0.22, 0.18)
    return jnp.clip(entries, -limit, limit).astype(kind)


def setup_inputs(seed: int = 0) -> dict:
    splits = jax.random.split(jax.random.key(seed), 11)
    return {
        "features": noise(splits[0], (N, F), 1.0, 6.0, ((0, 8),)),
        "degree": plant(jax.random.randint(splits[1], (N,), 1, 9), jax.random.fold_in(splits[1], 1), 1, 8).astype(jnp.int32),
        "order": jax.vmap(lambda own: jax.random.permutation(own, NB))(jax.random.split(splits[2], BLOCKS)).reshape((BLOCKS, NB)).astype(jnp.int32),
        "tile_rows": plant(jax.random.randint(splits[3], (BLOCKS, REPS, TILES_DEV), 0, RT), jax.random.fold_in(splits[3], 1), 0, RT - 1).astype(jnp.int32),
        "tile_cols": plant(jax.random.randint(splits[4], (BLOCKS, REPS, TILES_DEV), 0, 3 * RT), jax.random.fold_in(splits[4], 1), 0, (3 * RT) - 1).astype(jnp.int32),
        "tile_count": draw_tile_count(jax.random.fold_in(splits[10], 71), 0),
        "tile_values": noise(splits[6], (BLOCKS, REPS, TILES_DEV, 128, 128), 0.025, 0.14941406, ((0, 8), (1, 4))),
        "w_self": noise(splits[7], (F, F), F ** -0.5, 0.375),
        "w_neigh": noise(splits[8], (F, F), F ** -0.5, 0.375),
        "out_grad": noise(splits[9], (N, F), 1.0, 6.0, ((0, 8),)),
    }


def silu_pair(h):
    sig = jax.nn.sigmoid(h)
    return h * sig, sig * (1.0 + h * (1.0 - sig))


def reference(features, degree, order, tile_rows, tile_cols, tile_count, tile_values, w_self, w_neigh, out_grad):
    row_tiles = NB // 128
    slots = REPS * TILES_DEV
    perm = order[:, :, None]
    feats = jnp.take_along_axis(features.reshape(BLOCKS, NB, F), perm, axis=1)
    grads = jnp.take_along_axis(out_grad.reshape(BLOCKS, NB, F), perm, axis=1)
    scale = 1.0 / jnp.take_along_axis(degree.reshape(BLOCKS, NB), order, axis=1).astype(jnp.float32)
    rows_all = tile_rows.reshape(BLOCKS, slots)
    cols_all = tile_cols.reshape(BLOCKS, slots)
    live = (jnp.arange(TILES_DEV, dtype=jnp.int32)[None, None, :] < tile_count[:, :, None]).astype(jnp.float32)
    live = live.reshape(BLOCKS, slots)
    vals_all = tile_values.reshape(BLOCKS, slots, 128, 128)
    window = jnp.concatenate([jnp.roll(feats, 1, axis=0), feats, jnp.roll(feats, -1, axis=0)], axis=1)

    def gather_block(args):
        win, rows_i, cols_i, live_i, vals = args
        pick = win.reshape(3 * row_tiles, 128, F)[cols_i]
        prod = jnp.einsum("tab,tbf->taf", vals.astype(jnp.float32), pick.astype(jnp.float32),
                          precision=lax.Precision.HIGHEST)
        hot = (rows_i[None, :] == jnp.arange(row_tiles, dtype=jnp.int32)[:, None]).astype(jnp.float32) * live_i[None, :]
        return jnp.dot(hot, prod.reshape(slots, 128 * F), precision=lax.Precision.HIGHEST).reshape(NB, F)

    partial_value = lax.map(gather_block, (window, rows_all, cols_all, live, vals_all))
    agg = (partial_value * scale[:, :, None]).astype(jnp.bfloat16).reshape(N, F)
    flat_x = feats.reshape(N, F)
    h = jnp.dot(flat_x, w_self, preferred_element_type=jnp.float32) + jnp.dot(agg, w_neigh, preferred_element_type=jnp.float32)
    act, slope = silu_pair(h)
    act = act.astype(jnp.bfloat16)
    gp = (grads.reshape(N, F).astype(jnp.float32) * slope).astype(jnp.bfloat16)
    grad_self = jnp.dot(flat_x.T, gp, preferred_element_type=jnp.float32)
    grad_neigh = jnp.dot(agg.T, gp, preferred_element_type=jnp.float32)
    sback = (jnp.dot(gp, w_neigh.T, preferred_element_type=jnp.float32) * scale.reshape(N)[:, None]).astype(jnp.bfloat16)
    dself = jnp.dot(gp, w_self.T, preferred_element_type=jnp.float32).reshape(BLOCKS, NB, F)

    def return_block(args):
        s_blk, rows_i, cols_i, live_i, vals = args
        pick = s_blk.reshape(row_tiles, 128, F)[rows_i]
        back = jnp.einsum("tab,taf->tbf", vals.astype(jnp.float32), pick.astype(jnp.float32),
                          precision=lax.Precision.HIGHEST)
        hot = (cols_i[None, :] == jnp.arange(3 * row_tiles, dtype=jnp.int32)[:, None]).astype(jnp.float32) * live_i[None, :]
        return jnp.dot(hot, back.reshape(slots, 128 * F), precision=lax.Precision.HIGHEST).reshape(3, NB, F)

    parts = lax.map(return_block, (sback.reshape(BLOCKS, NB, F), rows_all, cols_all, live, vals_all))
    total = dself + parts[:, 1] + jnp.roll(parts[:, 0], -1, axis=0) + jnp.roll(parts[:, 2], 1, axis=0)
    grad_perm = total.astype(jnp.bfloat16)
    inverse = jnp.argsort(order, axis=1).astype(jnp.int32)[:, :, None]
    output = jnp.take_along_axis(act.reshape(BLOCKS, NB, F), inverse, axis=1).reshape(N, F)
    grad_features = jnp.take_along_axis(grad_perm, inverse, axis=1).reshape(N, F)
    return output, grad_features, grad_self, grad_neigh
```

```python
import jax
import jax.numpy as jnp
from jax import lax
from jax.experimental import pallas as pl
from jax.experimental.pallas import tpu as pltpu
from jax.sharding import PartitionSpec as P

BF = jnp.bfloat16
F32 = jnp.float32
T = 128


def mm(a, b):
    return jnp.dot(a, b, preferred_element_type=F32)


def mm_nt(a, b):
    return lax.dot_general(a, b, (((1,), (1,)), ((), ())), preferred_element_type=F32)


def mm_tn(a, b):
    return lax.dot_general(a, b, (((0,), (0,)), ((), ())), preferred_element_type=F32)


def core_of():
    return lax.rem(lax.axis_index("rep"), 2)


def y_of():
    return lax.div(lax.axis_index("rep"), 2)


def onehot_rows(order_row, count):
    column = jnp.transpose(jnp.broadcast_to(order_row, (T, T)))
    lane = lax.broadcasted_iota(jnp.int32, (T, T), 1).astype(F32)
    cuts = [
        jnp.where(column == lane + float(j * T), 1.0, 0.0).astype(BF) for j in range(count // T)
    ]
    return jnp.concatenate(cuts, axis=1)


def onehot_inverse(order_row, first, rows):
    wide = (rows, order_row.shape[1])
    at = lax.broadcasted_iota(jnp.int32, wide, 0) + first
    return jnp.where(jnp.broadcast_to(order_row, wide) == at, 1.0, 0.0).astype(BF)


def half_lanes(index):
    return pl.ds(pl.multiple_of(index * T, T), T)


def reorder_kernel(order_ref, x_ref, out_ref):
    c = core_of()
    rows = out_ref.shape[0]
    x = x_ref[:, half_lanes(c)]
    for i in range(rows // T):
        hot = onehot_rows(order_ref[i : i + 1, :].astype(F32), rows)
        out_ref[i * T : (i + 1) * T, :] = mm(hot, x).astype(BF)


def prepare_kernel(order_ref, degree_ref, x_ref, g_ref, w_ref, xh_ref, gh_ref, hs_ref, sc_ref, sr_ref):
    c = core_of()
    rows = x_ref.shape[0]
    tiles = rows // T // 2
    deg = jnp.broadcast_to(degree_ref[...].astype(F32), (8, rows)).astype(BF)
    for i in range(tiles):
        hot = onehot_rows(order_ref[pl.ds(c * tiles + i, 1), :].astype(F32), rows)
        here = slice(i * T, (i + 1) * T)
        xt = mm(hot, x_ref[...]).astype(BF)
        xh_ref[here, :] = xt
        gh_ref[here, :] = mm(hot, g_ref[...]).astype(BF)
        hs_ref[here, :] = mm(xt, w_ref[...])
        scale = 1.0 / mm_nt(deg, hot)
        sr_ref[:, here] = scale
        sc_ref[here, :] = jnp.transpose(jnp.broadcast_to(scale[0:1, :], (T, T)))


def gather_kernel(
    ra_ref, ca_ref, na_ref, rb_ref, cb_ref, nb_ref,
    prev_ref, own_ref, next_ref, va_ref, vb_ref,
    here_ref, other_ref, win, acc,
):
    c = core_of()
    rows = own_ref.shape[0]
    tiles = rows // T
    half = rows // 2
    win[0:rows, :] = prev_ref[...]
    win[rows : 2 * rows, :] = own_ref[...]
    win[2 * rows : 3 * rows, :] = next_ref[...]
    acc[...] = jnp.zeros_like(acc)
    slots = va_ref.shape[0]
    for t in range(slots):
        for r_ref, c_ref, n_ref, v_ref in (
            (ra_ref, ca_ref, na_ref, va_ref),
            (rb_ref, cb_ref, nb_ref, vb_ref),
        ):
            r = jnp.where(t < n_ref[0], r_ref[t], tiles)
            prod = mm(v_ref[t], win[pl.ds(pl.multiple_of(c_ref[t] * T, T), T), :])
            acc[r] += prod
    for i in range(tiles // 2):
        here_ref[i * T : (i + 1) * T, :] = acc[c * (tiles // 2) + i].astype(BF)
        other_ref[i * T : (i + 1) * T, :] = acc[(1 - c) * (tiles // 2) + i].astype(BF)


def dense_kernel(
    own_ref, core_ref, y_ref, diag_ref, hs_ref, gh_ref, sc_ref, sr_ref, wn_ref,
    act_ref, gp_ref, agg_ref, keep_ref, send_ref,
):
    c = core_of()
    scale = sc_ref[...]
    agg_ref[:, half_lanes(c)] = (
        (own_ref[...].astype(F32) + y_ref[...].astype(F32)) * scale
    ).astype(BF)
    agg_ref[:, half_lanes(1 - c)] = (
        (core_ref[...].astype(F32) + diag_ref[...].astype(F32)) * scale
    ).astype(BF)
    h = hs_ref[...] + mm(agg_ref[...], wn_ref[...])
    sig = jax.nn.sigmoid(h)
    act_ref[...] = (h * sig).astype(BF)
    gp = (gh_ref[...].astype(F32) * (sig * (1.0 + h * (1.0 - sig)))).astype(BF)
    gp_ref[...] = gp
    row = sr_ref[0:1, :]
    keep_ref[...] = (mm_nt(wn_ref[pl.ds(pl.multiple_of(c * T, T), T), :], gp) * row).astype(BF)
    send_ref[...] = (mm_nt(wn_ref[pl.ds(pl.multiple_of((1 - c) * T, T), T), :], gp) * row).astype(BF)


def terms_kernel(xh_ref, agg_ref, gp_ref, ws_ref, keep_ref, send_ref, mine_ref, theirs_ref):
    c, y = core_of(), y_of()
    gp = gp_ref[...]
    keep_ref[...] = mm_nt(ws_ref[pl.ds(pl.multiple_of(c * T, T), T), :], gp)
    send_ref[...] = mm_nt(ws_ref[pl.ds(pl.multiple_of((1 - c) * T, T), T), :], gp)
    mine_ref[...] = jnp.zeros_like(mine_ref)

    def term(lhs_ref):
        mine_ref[...] = mm_tn(lhs_ref[:, half_lanes(c)], gp)
        theirs_ref[...] = mm_tn(lhs_ref[:, half_lanes(1 - c)], gp)

    @pl.when(y == 0)
    def _():
        term(xh_ref)

    @pl.when(y != 0)
    def _():
        term(agg_ref)


def scatter_kernel(
    ra_ref, ca_ref, na_ref, rb_ref, cb_ref, nb_ref,
    mine_ref, theirs_ref, va_ref, vb_ref,
    own_ref, ownx_ref, dn_ref, dnx_ref, up_ref, upx_ref, src, acc,
):
    c, y = core_of(), y_of()
    half = mine_ref.shape[1]
    tiles = 2 * half // T
    ht = tiles // 2
    for i in range(ht):
        cut = slice(i * T, (i + 1) * T)
        src[c * ht + i] = mine_ref[:, cut]
        src[(1 - c) * ht + i] = theirs_ref[:, cut]
    acc[...] = jnp.zeros_like(acc)
    slots = va_ref.shape[0]
    for t in range(slots):
        for r_ref, c_ref, n_ref, v_ref in (
            (ra_ref, ca_ref, na_ref, va_ref),
            (rb_ref, cb_ref, nb_ref, vb_ref),
        ):
            col = jnp.where(t < n_ref[0], c_ref[t], 3 * tiles)
            acc[col] += mm(src[r_ref[t]], v_ref[t])
    for i in range(ht):
        same, cross = y * ht + i, (1 - y) * ht + i
        own_ref[i] = acc[tiles + same]
        ownx_ref[i] = acc[tiles + cross].astype(BF)
        dn_ref[i] = acc[same].astype(BF)
        dnx_ref[i] = acc[cross].astype(BF)
        up_ref[i] = acc[2 * tiles + same].astype(BF)
        upx_ref[i] = acc[2 * tiles + cross].astype(BF)


def total_kernel(own_ref, y_ref, a_ref, b_ref, d_ref, e_ref, keep_ref, recv_ref, out_ref):
    c, y = core_of(), y_of()
    local = jnp.broadcast_to(c == y, keep_ref.shape)
    dself = jnp.where(local, keep_ref[...], recv_ref[...])
    for i in range(own_ref.shape[0]):
        total = own_ref[i] + dself[:, i * T : (i + 1) * T] + y_ref[i].astype(F32)
        total = total + a_ref[i].astype(F32) + b_ref[i].astype(F32)
        total = total + d_ref[i].astype(F32) + e_ref[i].astype(F32)
        out_ref[i] = total.astype(BF)


def restore_kernel(order_ref, own_ref, core_ref, y_ref, diag_ref, out_ref, full):
    c, y = core_of(), y_of()
    rows = out_ref.shape[0]
    ht = own_ref.shape[0]
    for i in range(ht):
        for ref, fh, rh in (
            (own_ref, c, y),
            (core_ref, 1 - c, y),
            (y_ref, c, 1 - y),
            (diag_ref, 1 - c, 1 - y),
        ):
            at = pl.ds(pl.multiple_of((rh * ht + i) * T, T), T)
            full[pl.ds(pl.multiple_of(fh * T, T), T), at] = ref[i]
    for j in range(rows // 256):
        hot = onehot_inverse(order_ref[...], j * 256, 256)
        out_ref[j * 256 : (j + 1) * 256, :] = mm_nt(hot, full[...]).astype(BF)


def output_kernel(order_ref, own_ref, core_ref, out_ref, full):
    c = core_of()
    half = own_ref.shape[0]
    rows = 2 * half
    full[pl.ds(pl.multiple_of(c * half, half), half), :] = own_ref[...]
    full[pl.ds(pl.multiple_of((1 - c) * half, half), half), :] = core_ref[...]
    for j in range(rows // 256):
        hot = onehot_inverse(order_ref[...], j * 256, 256)
        out_ref[j * 256 : (j + 1) * 256, :] = mm(hot, full[...]).astype(BF)


def call(kernel, outs, ins, smem=0, scratch=(), name=None, flops=0, moved=0):
    specs = [pl.BlockSpec(memory_space=pltpu.SMEM)] * smem
    specs += [pl.BlockSpec(memory_space=pltpu.VMEM)] * (len(ins) - smem)
    shapes = [jax.ShapeDtypeStruct(s, d) for s, d in outs]
    out_specs = [pl.BlockSpec(memory_space=pltpu.VMEM)] * len(outs)
    single = len(outs) == 1
    return pl.pallas_call(
        kernel,
        out_shape=shapes[0] if single else shapes,
        in_specs=specs,
        out_specs=out_specs[0] if single else out_specs,
        scratch_shapes=list(scratch),
        name=name,
        cost_estimate=pl.CostEstimate(flops=flops, bytes_accessed=moved, transcendentals=0),
    )(*ins)


def shards(
    features, degree, order, tile_rows, tile_cols, tile_count, tile_values, w_self, w_neigh, out_grad
):
    rows, width = features.shape
    half = rows // 2
    tiles = rows // T
    ht = tiles // 2
    blocks = lax.axis_size("blk")
    reps = lax.axis_size("rep")
    assert reps == 4 and width == 2 * T

    def hop(x, blk_step, rep_mask):
        pairs = [
            (b * reps + r, ((b + blk_step) % blocks) * reps + (r ^ rep_mask))
            for b in range(blocks)
            for r in range(reps)
        ]
        return lax.ppermute(x, ("blk", "rep"), pairs)

    def swap_core(x):
        return lax.ppermute(x, "rep", [(r, r ^ 1) for r in range(reps)])

    def swap_y(x):
        return lax.ppermute(x, "rep", [(r, r ^ 2) for r in range(reps)])

    def swap_diag(x):
        return lax.ppermute(x, "rep", [(r, r ^ 3) for r in range(reps)])

    order8 = order.reshape(tiles, T)
    deg = degree.reshape(1, rows)
    ra, ca, na = tile_rows[0, 0], tile_cols[0, 0], tile_count[0]
    va = tile_values[0, 0]

    feats_c = call(reorder_kernel, [((rows, T), BF)], [order8, features], name="reorder")
    prev = hop(feats_c, 1, 0)
    nxt = hop(feats_c, -1, 0)
    vb = swap_core(va)
    rb, cb, nb = swap_core(ra), swap_core(ca), swap_core(na)
    xh, gh, hs, sc, sr = call(
        prepare_kernel,
        [((half, width), BF), ((half, width), BF), ((half, width), F32), ((half, T), F32), ((8, half), F32)],
        [order8, deg, features, out_grad, w_self],
        name="prepare",
    )
    index = [ra, ca, na, rb, cb, nb]
    here, other = call(
        gather_kernel,
        [((half, T), BF), ((half, T), BF)],
        index + [prev, feats_c, nxt, va, vb],
        smem=6,
        scratch=[pltpu.VMEM((3 * rows, T), BF), pltpu.VMEM((tiles + 1, T, T), F32)],
        name="gather",
    )
    from_y = swap_y(here)
    from_diag = swap_diag(other)
    from_core = swap_core(other)
    act, gp, agg, s_keep, s_send = call(
        dense_kernel,
        [((half, width), BF), ((half, width), BF), ((half, width), BF), ((T, half), BF), ((T, half), BF)],
        [here, from_core, from_y, from_diag, hs, gh, sc, sr, w_neigh],
        name="dense",
    )
    s_other = swap_core(s_send)
    d_keep, d_send, g_mine, g_theirs = call(
        terms_kernel,
        [((T, half), F32), ((T, half), F32), ((T, width), F32), ((T, width), F32)],
        [xh, agg, gp, w_self],
        name="terms",
    )
    piece = (ht, T, T)
    own, ownx, dn, dnx, up, upx = call(
        scatter_kernel,
        [(piece, F32)] + [(piece, BF)] * 5,
        index + [s_keep, s_other, va, vb],
        smem=6,
        scratch=[pltpu.VMEM((tiles, T, T), BF), pltpu.VMEM((3 * tiles + 1, T, T), F32)],
        name="scatter",
    )
    r_a = hop(dn, -1, 0)
    r_b = hop(dnx, -1, 2)
    r_d = hop(up, 1, 0)
    r_e = hop(upx, 1, 2)
    r_y = swap_y(ownx)
    d_recv = swap_core(d_send)
    act_other = swap_core(act)
    output = call(
        output_kernel,
        [((rows, width), BF)],
        [order, act, act_other],
        scratch=[pltpu.VMEM((rows, width), BF)],
        name="output",
    )
    grad_piece = call(
        total_kernel, [(piece, BF)], [own, r_y, r_a, r_b, r_d, r_e, d_keep, d_recv], name="total"
    )
    g = g_mine + swap_core(g_theirs)
    step = 1
    while step < blocks:
        g = g + lax.ppermute(g, "blk", [(b, b ^ step) for b in range(blocks)])
        step *= 2
    g = g.astype(BF)
    p_y = swap_y(grad_piece)
    p_core = swap_core(grad_piece)
    p_diag = swap_core(p_y)
    grad_features = call(
        restore_kernel,
        [((rows, width), BF)],
        [order, grad_piece, p_core, p_y, p_diag],
        scratch=[pltpu.VMEM((width, rows), BF)],
        name="restore",
    )
    weights = lax.all_gather(g, "rep", axis=0, tiled=True).astype(F32)
    return output, grad_features, weights[:width], weights[width:]


def solution(mesh):
    return jax.shard_map(
        shards,
        mesh=mesh,
        in_specs=(
            P("blk", None),
            P("blk"),
            P("blk", None),
            P("blk", "rep", None),
            P("blk", "rep", None),
            P("blk", "rep"),
            P("blk", "rep", None, None, None),
            P(),
            P(),
            P("blk", None),
        ),
        out_specs=(P("blk", None), P("blk", None), P(), P()),
        check_vma=False,
    )
```

```python
import jax
import jax.numpy as jnp
from jax import lax
from jax.experimental import pallas as pl
from jax.experimental.pallas import tpu as pltpu
from jax.sharding import PartitionSpec as P

BF = jnp.bfloat16
F32 = jnp.float32
T = 128
VMEM = 16 * 2**20


def mm(a, b):
    return jnp.dot(a, b, preferred_element_type=F32)


def mm_nt(a, b):
    return lax.dot_general(a, b, (((1,), (1,)), ((), ())), preferred_element_type=F32)


def mm_tn(a, b):
    return lax.dot_general(a, b, (((0,), (0,)), ((), ())), preferred_element_type=F32)


def core_of():
    return lax.rem(lax.axis_index("rep"), 2)


def y_of():
    return lax.div(lax.axis_index("rep"), 2)


def onehot_rows(order_row, count):
    column = jnp.transpose(jnp.broadcast_to(order_row, (T, T)))
    lane = lax.broadcasted_iota(jnp.int32, (T, T), 1).astype(F32)
    cuts = [
        jnp.where(column == lane + float(j * T), 1.0, 0.0).astype(BF) for j in range(count // T)
    ]
    return jnp.concatenate(cuts, axis=1)


def onehot_inverse(order_row, first, rows):
    wide = (rows, order_row.shape[1])
    at = lax.broadcasted_iota(jnp.int32, wide, 0) + first
    return jnp.where(jnp.broadcast_to(order_row, wide) == at, 1.0, 0.0).astype(BF)


def half_lanes(index):
    return pl.ds(pl.multiple_of(index * T, T), T)


def reorder_kernel(order_ref, x_ref, out_ref):
    c = core_of()
    rows = out_ref.shape[0]
    x = x_ref[:, half_lanes(c)]
    for i in range(rows // T):
        hot = onehot_rows(order_ref[i : i + 1, :].astype(F32), rows)
        out_ref[i * T : (i + 1) * T, :] = mm(hot, x).astype(BF)


def prepare_kernel(order_ref, degree_ref, x_ref, g_ref, w_ref, xh_ref, gh_ref, hs_ref, sc_ref, sr_ref):
    c = core_of()
    rows = x_ref.shape[0]
    tiles = rows // T // 2
    deg = jnp.broadcast_to(degree_ref[...].astype(F32), (8, rows)).astype(BF)
    for i in range(tiles):
        hot = onehot_rows(order_ref[pl.ds(c * tiles + i, 1), :].astype(F32), rows)
        here = slice(i * T, (i + 1) * T)
        xt = mm(hot, x_ref[...]).astype(BF)
        xh_ref[here, :] = xt
        gh_ref[here, :] = mm(hot, g_ref[...]).astype(BF)
        hs_ref[here, :] = mm(xt, w_ref[...])
        scale = 1.0 / mm_nt(deg, hot)
        sr_ref[:, here] = scale
        sc_ref[here, :] = jnp.transpose(jnp.broadcast_to(scale[0:1, :], (T, T)))


def gather_kernel(
    ra_ref, ca_ref, na_ref, rb_ref, cb_ref, nb_ref,
    prev_ref, own_ref, next_ref, va_ref, vb_ref,
    here_ref, other_ref, win, acc,
):
    c = core_of()
    rows = own_ref.shape[0]
    tiles = rows // T
    half = rows // 2
    win[0:rows, :] = prev_ref[...]
    win[rows : 2 * rows, :] = own_ref[...]
    win[2 * rows : 3 * rows, :] = next_ref[...]
    acc[...] = jnp.zeros_like(acc)
    slots = va_ref.shape[0]
    for t in range(slots):
        for r_ref, c_ref, n_ref, v_ref in (
            (ra_ref, ca_ref, na_ref, va_ref),
            (rb_ref, cb_ref, nb_ref, vb_ref),
        ):
            r = jnp.where(t < n_ref[0], r_ref[t], tiles)
            prod = mm(v_ref[t], win[pl.ds(pl.multiple_of(c_ref[t] * T, T), T), :])
            acc[r] += prod
    for i in range(tiles // 2):
        here_ref[i * T : (i + 1) * T, :] = acc[c * (tiles // 2) + i].astype(BF)
        other_ref[i * T : (i + 1) * T, :] = acc[(1 - c) * (tiles // 2) + i].astype(BF)


def dense_kernel(
    own_ref, core_ref, y_ref, diag_ref, hs_ref, gh_ref, sc_ref, sr_ref, wn_ref,
    act_ref, gp_ref, agg_ref, keep_ref, send_ref,
):
    c = core_of()
    scale = sc_ref[...]
    agg_ref[:, half_lanes(c)] = (
        (own_ref[...].astype(F32) + y_ref[...].astype(F32)) * scale
    ).astype(BF)
    agg_ref[:, half_lanes(1 - c)] = (
        (core_ref[...].astype(F32) + diag_ref[...].astype(F32)) * scale
    ).astype(BF)
    h = hs_ref[...] + mm(agg_ref[...], wn_ref[...])
    sig = jax.nn.sigmoid(h)
    act_ref[...] = (h * sig).astype(BF)
    gp = (gh_ref[...].astype(F32) * (sig * (1.0 + h * (1.0 - sig)))).astype(BF)
    gp_ref[...] = gp
    row = sr_ref[0:1, :]
    keep_ref[...] = (mm_nt(wn_ref[pl.ds(pl.multiple_of(c * T, T), T), :], gp) * row).astype(BF)
    send_ref[...] = (mm_nt(wn_ref[pl.ds(pl.multiple_of((1 - c) * T, T), T), :], gp) * row).astype(BF)


def terms_kernel(xh_ref, agg_ref, gp_ref, ws_ref, keep_ref, send_ref, mine_ref, theirs_ref):
    c, y = core_of(), y_of()
    gp = gp_ref[...]
    keep_ref[...] = mm_nt(ws_ref[pl.ds(pl.multiple_of(c * T, T), T), :], gp)
    send_ref[...] = mm_nt(ws_ref[pl.ds(pl.multiple_of((1 - c) * T, T), T), :], gp)
    mine_ref[...] = jnp.zeros_like(mine_ref)

    def term(lhs_ref):
        mine_ref[...] = mm_tn(lhs_ref[:, half_lanes(c)], gp)
        theirs_ref[...] = mm_tn(lhs_ref[:, half_lanes(1 - c)], gp)

    @pl.when(y == 0)
    def _():
        term(xh_ref)

    @pl.when(y != 0)
    def _():
        term(agg_ref)


def scatter_kernel(
    ra_ref, ca_ref, na_ref, rb_ref, cb_ref, nb_ref,
    mine_ref, theirs_ref, va_ref, vb_ref,
    own_ref, ownx_ref, dn_ref, dnx_ref, up_ref, upx_ref, src, acc,
):
    c, y = core_of(), y_of()
    half = mine_ref.shape[1]
    tiles = 2 * half // T
    ht = tiles // 2
    for i in range(ht):
        cut = slice(i * T, (i + 1) * T)
        src[c * ht + i] = mine_ref[:, cut]
        src[(1 - c) * ht + i] = theirs_ref[:, cut]
    acc[...] = jnp.zeros_like(acc)
    slots = va_ref.shape[0]
    for t in range(slots):
        for r_ref, c_ref, n_ref, v_ref in (
            (ra_ref, ca_ref, na_ref, va_ref),
            (rb_ref, cb_ref, nb_ref, vb_ref),
        ):
            col = jnp.where(t < n_ref[0], c_ref[t], 3 * tiles)
            acc[col] += mm(src[r_ref[t]], v_ref[t])
    for i in range(ht):
        same, cross = y * ht + i, (1 - y) * ht + i
        own_ref[i] = acc[tiles + same]
        ownx_ref[i] = acc[tiles + cross].astype(BF)
        dn_ref[i] = acc[same].astype(BF)
        dnx_ref[i] = acc[cross].astype(BF)
        up_ref[i] = acc[2 * tiles + same].astype(BF)
        upx_ref[i] = acc[2 * tiles + cross].astype(BF)


def total_kernel(own_ref, y_ref, a_ref, b_ref, d_ref, e_ref, keep_ref, recv_ref, out_ref):
    c, y = core_of(), y_of()
    local = jnp.broadcast_to(c == y, keep_ref.shape)
    dself = jnp.where(local, keep_ref[...], recv_ref[...])
    for i in range(own_ref.shape[0]):
        total = own_ref[i] + dself[:, i * T : (i + 1) * T] + y_ref[i].astype(F32)
        total = total + a_ref[i].astype(F32) + b_ref[i].astype(F32)
        total = total + d_ref[i].astype(F32) + e_ref[i].astype(F32)
        out_ref[i] = total.astype(BF)


def restore_kernel(order_ref, own_ref, core_ref, y_ref, diag_ref, out_ref, full):
    c, y = core_of(), y_of()
    rows = out_ref.shape[0]
    ht = own_ref.shape[0]
    for i in range(ht):
        for ref, fh, rh in (
            (own_ref, c, y),
            (core_ref, 1 - c, y),
            (y_ref, c, 1 - y),
            (diag_ref, 1 - c, 1 - y),
        ):
            at = pl.ds(pl.multiple_of((rh * ht + i) * T, T), T)
            full[pl.ds(pl.multiple_of(fh * T, T), T), at] = ref[i]
    for j in range(rows // 256):
        hot = onehot_inverse(order_ref[...], j * 256, 256)
        out_ref[j * 256 : (j + 1) * 256, :] = mm_nt(hot, full[...]).astype(BF)


def output_kernel(order_ref, own_ref, core_ref, out_ref, full):
    c = core_of()
    half = own_ref.shape[0]
    rows = 2 * half
    full[pl.ds(pl.multiple_of(c * half, half), half), :] = own_ref[...]
    full[pl.ds(pl.multiple_of((1 - c) * half, half), half), :] = core_ref[...]
    for j in range(rows // 256):
        hot = onehot_inverse(order_ref[...], j * 256, 256)
        out_ref[j * 256 : (j + 1) * 256, :] = mm(hot, full[...]).astype(BF)


def call(kernel, outs, ins, smem=0, scratch=(), name=None, flops=0, moved=0):
    specs = [pl.BlockSpec(memory_space=pltpu.SMEM)] * smem
    specs += [pl.BlockSpec(memory_space=pltpu.VMEM)] * (len(ins) - smem)
    shapes = [jax.ShapeDtypeStruct(s, d) for s, d in outs]
    out_specs = [pl.BlockSpec(memory_space=pltpu.VMEM)] * len(outs)
    single = len(outs) == 1
    return pl.pallas_call(
        kernel,
        out_shape=shapes[0] if single else shapes,
        in_specs=specs,
        out_specs=out_specs[0] if single else out_specs,
        scratch_shapes=list(scratch),
        name=name,
        compiler_params=pltpu.CompilerParams(vmem_limit_bytes=VMEM),
        cost_estimate=pl.CostEstimate(flops=flops, bytes_accessed=moved, transcendentals=0),
    )(*ins)


def shards(
    features, degree, order, tile_rows, tile_cols, tile_count, tile_values, w_self, w_neigh, out_grad
):
    rows, width = features.shape
    half = rows // 2
    tiles = rows // T
    ht = tiles // 2
    blocks = lax.axis_size("blk")
    reps = lax.axis_size("rep")
    assert reps == 4 and width == 2 * T

    def hop(x, blk_step, rep_mask):
        pairs = [
            (b * reps + r, ((b + blk_step) % blocks) * reps + (r ^ rep_mask))
            for b in range(blocks)
            for r in range(reps)
        ]
        return lax.ppermute(x, ("blk", "rep"), pairs)

    def swap_core(x):
        return lax.ppermute(x, "rep", [(r, r ^ 1) for r in range(reps)])

    def swap_y(x):
        return lax.ppermute(x, "rep", [(r, r ^ 2) for r in range(reps)])

    def swap_diag(x):
        return lax.ppermute(x, "rep", [(r, r ^ 3) for r in range(reps)])

    order8 = order.reshape(tiles, T)
    deg = degree.reshape(1, rows)
    ra, ca, na = tile_rows[0, 0], tile_cols[0, 0], tile_count[0]
    va = tile_values[0, 0]

    feats_c = call(reorder_kernel, [((rows, T), BF)], [order8, features], name="reorder")
    prev = hop(feats_c, 1, 0)
    nxt = hop(feats_c, -1, 0)
    vb = swap_core(va)
    rb, cb, nb = swap_core(ra), swap_core(ca), swap_core(na)
    xh, gh, hs, sc, sr = call(
        prepare_kernel,
        [((half, width), BF), ((half, width), BF), ((half, width), F32), ((half, T), F32), ((8, half), F32)],
        [order8, deg, features, out_grad, w_self],
        name="prepare",
    )
    index = [ra, ca, na, rb, cb, nb]
    here, other = call(
        gather_kernel,
        [((half, T), BF), ((half, T), BF)],
        index + [prev, feats_c, nxt, va, vb],
        smem=6,
        scratch=[pltpu.VMEM((3 * rows, T), BF), pltpu.VMEM((tiles + 1, T, T), F32)],
        name="gather",
    )
    from_y = swap_y(here)
    from_diag = swap_diag(other)
    from_core = swap_core(other)
    act, gp, agg, s_keep, s_send = call(
        dense_kernel,
        [((half, width), BF), ((half, width), BF), ((half, width), BF), ((T, half), BF), ((T, half), BF)],
        [here, from_core, from_y, from_diag, hs, gh, sc, sr, w_neigh],
        name="dense",
    )
    s_other = swap_core(s_send)
    d_keep, d_send, g_mine, g_theirs = call(
        terms_kernel,
        [((T, half), F32), ((T, half), F32), ((T, width), F32), ((T, width), F32)],
        [xh, agg, gp, w_self],
        name="terms",
    )
    piece = (ht, T, T)
    own, ownx, dn, dnx, up, upx = call(
        scatter_kernel,
        [(piece, F32)] + [(piece, BF)] * 5,
        index + [s_keep, s_other, va, vb],
        smem=6,
        scratch=[pltpu.VMEM((tiles, T, T), BF), pltpu.VMEM((3 * tiles + 1, T, T), F32)],
        name="scatter",
    )
    r_a = hop(dn, -1, 0)
    r_b = hop(dnx, -1, 2)
    r_d = hop(up, 1, 0)
    r_e = hop(upx, 1, 2)
    r_y = swap_y(ownx)
    d_recv = swap_core(d_send)
    act_other = swap_core(act)
    output = call(
        output_kernel,
        [((rows, width), BF)],
        [order, act, act_other],
        scratch=[pltpu.VMEM((rows, width), BF)],
        name="output",
    )
    grad_piece = call(
        total_kernel, [(piece, BF)], [own, r_y, r_a, r_b, r_d, r_e, d_keep, d_recv], name="total"
    )
    g = g_mine + swap_core(g_theirs)
    step = 1
    while step < blocks:
        g = g + lax.ppermute(g, "blk", [(b, b ^ step) for b in range(blocks)])
        step *= 2
    g = g.astype(BF)
    p_y = swap_y(grad_piece)
    p_core = swap_core(grad_piece)
    p_diag = swap_core(p_y)
    grad_features = call(
        restore_kernel,
        [((rows, width), BF)],
        [order, grad_piece, p_core, p_y, p_diag],
        scratch=[pltpu.VMEM((width, rows), BF)],
        name="restore",
    )
    weights = lax.all_gather(g, "rep", axis=0, tiled=True).astype(F32)
    return output, grad_features, weights[:width], weights[width:]


def solution(mesh):
    return jax.shard_map(
        shards,
        mesh=mesh,
        in_specs=(
            P("blk", None),
            P("blk"),
            P("blk", None),
            P("blk", "rep", None),
            P("blk", "rep", None),
            P("blk", "rep"),
            P("blk", "rep", None, None, None),
            P(),
            P(),
            P("blk", None),
        ),
        out_specs=(P("blk", None), P("blk", None), P(), P()),
        check_vma=False,
    )
```

```python
import jax
import jax.numpy as jnp
from jax import lax
from jax.experimental import pallas as pl
from jax.experimental.pallas import tpu as pltpu
from jax.sharding import PartitionSpec as P

BF = jnp.bfloat16
F32 = jnp.float32
T = 128
VMEM = 16 * 2**20


def mm(a, b):
    return jnp.dot(a, b, preferred_element_type=F32)


def mm_nt(a, b):
    return lax.dot_general(a, b, (((1,), (1,)), ((), ())), preferred_element_type=F32)


def mm_tn(a, b):
    return lax.dot_general(a, b, (((0,), (0,)), ((), ())), preferred_element_type=F32)


def core_of():
    return lax.rem(lax.axis_index("rep"), 2)


def y_of():
    return lax.div(lax.axis_index("rep"), 2)


def order_column(order_row):
    return jnp.transpose(jnp.broadcast_to(order_row, (T, T)))


def onehot_rows(column, count):
    lane = lax.broadcasted_iota(jnp.int32, (T, T), 1).astype(F32)
    cuts = [
        jnp.where(column == lane + float(j * T), 1.0, 0.0).astype(BF) for j in range(count // T)
    ]
    return jnp.concatenate(cuts, axis=1)


def onehot_inverse(order_row, first, rows):
    wide = (rows, order_row.shape[1])
    at = lax.broadcasted_iota(jnp.int32, wide, 0) + first
    return jnp.where(jnp.broadcast_to(order_row, wide) == at, 1.0, 0.0).astype(BF)


def half_lanes(index):
    return pl.ds(pl.multiple_of(index * T, T), T)


def reorder_kernel(order_hbm, x_hbm, rows_hbm, cols_hbm, count_ref, out_ref, idx_ref, order, x, rows, cols, sems):
    c = core_of()
    total = out_ref.shape[0]
    copies = [
        pltpu.make_async_copy(src, dst, sems.at[i])
        for i, (src, dst) in enumerate(
            (
                (order_hbm, order),
                (x_hbm.at[:, half_lanes(c)], x),
                (rows_hbm, rows),
                (cols_hbm, cols),
            )
        )
    ]
    for copy in copies:
        copy.start()
    copies[0].wait()
    columns = [order_column(order[i : i + 1, :].astype(F32)) for i in range(total // T)]
    copies[1].wait()
    for i in range(total // T):
        out_ref[i * T : (i + 1) * T, :] = mm(onehot_rows(columns[i], total), x[...]).astype(BF)
    for copy in copies[2:]:
        copy.wait()
    slots = rows.shape[1]
    idx_ref[...] = jnp.zeros_like(idx_ref)
    idx_ref[0:1, 0:slots] = rows[...]
    idx_ref[1:2, 0:slots] = cols[...]
    idx_ref[2:3, :] = jnp.full((1, T), count_ref[0, 0], jnp.int32)


def pair_slots(mine, theirs, slots, row_tiles, pairs, out_ref, pending):
    dead = row_tiles
    nothing = 2 * slots
    beyond = 3 * row_tiles

    def clear(i, _):
        out_ref[0, i] = dead
        out_ref[1, i] = nothing
        out_ref[2, i] = nothing
        out_ref[3, i] = beyond
        out_ref[4, i] = beyond
        return 0

    lax.fori_loop(0, pairs, clear, 0)
    for r in range(row_tiles + 1):
        pending[0, r] = -1
        pending[1, r] = beyond

    def emit(n, r, a, b, col_a, col_b):
        out_ref[0, n] = r
        out_ref[1, n] = a
        out_ref[2, n] = b
        out_ref[3, n] = col_a
        out_ref[4, n] = col_b

    n = jnp.int32(0)
    for base, idx in ((0, mine), (slots, theirs)):
        count = idx[2, 0]

        def place(s, n, base=base, idx=idx, count=count):
            live = s < count
            r = jnp.where(live, idx[0, s], dead)
            col = jnp.where(live, idx[1, s], beyond)
            first = pending[0, r]
            whole = first >= 0

            @pl.when(whole)
            def _():
                emit(n, r, first, base + s, pending[1, r], col)
                pending[0, r] = -1

            @pl.when(jnp.logical_not(whole))
            def _():
                pending[0, r] = base + s
                pending[1, r] = col

            return n + whole.astype(jnp.int32)

        n = lax.fori_loop(0, slots, place, n)

    def rest(r, n):
        first = pending[0, r]
        left = first >= 0

        @pl.when(left)
        def _():
            emit(n, r, first, nothing, pending[1, r], beyond)

        return n + left.astype(jnp.int32)

    lax.fori_loop(0, row_tiles, rest, n)


def prepare_kernel(
    mine, theirs, va_any, vb_any, order_ref, degree_ref, x_ref, g_ref, w_ref,
    xh_ref, gh_ref, hs_ref, sc_ref, sr_ref, tiles_ref, pairs_ref, pending, sems,
):
    c = core_of()
    rows = x_ref.shape[0]
    slots = va_any.shape[0]
    copies = [
        pltpu.make_async_copy(va_any, tiles_ref.at[0:slots], sems.at[0]),
        pltpu.make_async_copy(vb_any, tiles_ref.at[slots : 2 * slots], sems.at[1]),
    ]
    for copy in copies:
        copy.start()
    tiles_ref[2 * slots] = jnp.zeros((T, T), BF)
    pair_slots(mine, theirs, slots, rows // T, slots + rows // T // 2, pairs_ref, pending)
    tiles = rows // T // 2
    deg = jnp.broadcast_to(degree_ref[...].astype(F32), (8, rows)).astype(BF)
    for i in range(tiles):
        column = order_column(order_ref[pl.ds(c * tiles + i, 1), :].astype(F32))
        hot = onehot_rows(column, rows)
        here = slice(i * T, (i + 1) * T)
        xt = mm(hot, x_ref[...]).astype(BF)
        xh_ref[here, :] = xt
        gh_ref[here, :] = mm(hot, g_ref[...]).astype(BF)
        hs_ref[here, :] = mm(xt, w_ref[...])
        scale = 1.0 / mm_nt(deg, hot)
        sr_ref[:, here] = scale
        sc_ref[here, :] = jnp.transpose(jnp.broadcast_to(scale[0:1, :], (T, T)))
    for copy in copies:
        copy.wait()


def gather_kernel(pairs_ref, prev_ref, own_ref, next_ref, tiles_ref, here_ref, other_ref, win, acc):
    c = core_of()
    rows = own_ref.shape[0]
    tiles = rows // T
    win[0:rows, :] = prev_ref[...]
    win[rows : 2 * rows, :] = own_ref[...]
    win[2 * rows : 3 * rows, :] = next_ref[...]
    win[3 * rows : 3 * rows + T, :] = jnp.zeros((T, T), BF)
    acc[...] = jnp.zeros_like(acc)

    def window(col):
        return win[pl.ds(pl.multiple_of(col * T, T), T), :]

    for p in range((tiles_ref.shape[0] - 1 + tiles) // 2):
        left = jnp.concatenate([tiles_ref[pairs_ref[1, p]], tiles_ref[pairs_ref[2, p]]], axis=1)
        right = jnp.concatenate([window(pairs_ref[3, p]), window(pairs_ref[4, p])], axis=0)
        acc[pairs_ref[0, p]] += mm(left, right)
    for i in range(tiles // 2):
        here_ref[i * T : (i + 1) * T, :] = acc[c * (tiles // 2) + i].astype(BF)
        other_ref[i * T : (i + 1) * T, :] = acc[(1 - c) * (tiles // 2) + i].astype(BF)


def dense_kernel(
    own_ref, core_ref, y_ref, diag_ref, hs_ref, gh_ref, sc_ref, sr_ref, wn_ref,
    act_ref, gp_ref, agg_ref, keep_ref, send_ref,
):
    c = core_of()
    scale = sc_ref[...]
    agg_ref[:, half_lanes(c)] = (
        (own_ref[...].astype(F32) + y_ref[...].astype(F32)) * scale
    ).astype(BF)
    agg_ref[:, half_lanes(1 - c)] = (
        (core_ref[...].astype(F32) + diag_ref[...].astype(F32)) * scale
    ).astype(BF)
    h = hs_ref[...] + mm(agg_ref[...], wn_ref[...])
    sig = jax.nn.sigmoid(h)
    act_ref[...] = (h * sig).astype(BF)
    gp = (gh_ref[...].astype(F32) * (sig * (1.0 + h * (1.0 - sig)))).astype(BF)
    gp_ref[...] = gp
    row = sr_ref[0:1, :]
    keep_ref[...] = (mm_nt(wn_ref[pl.ds(pl.multiple_of(c * T, T), T), :], gp) * row).astype(BF)
    send_ref[...] = (mm_nt(wn_ref[pl.ds(pl.multiple_of((1 - c) * T, T), T), :], gp) * row).astype(BF)


def terms_kernel(xh_ref, agg_ref, gp_ref, ws_ref, keep_ref, send_ref, mine_ref, theirs_ref):
    c, y = core_of(), y_of()
    gp = gp_ref[...]
    keep_ref[...] = mm_nt(ws_ref[pl.ds(pl.multiple_of(c * T, T), T), :], gp)
    send_ref[...] = mm_nt(ws_ref[pl.ds(pl.multiple_of((1 - c) * T, T), T), :], gp)

    def term(lhs_ref):
        mine_ref[...] = mm_tn(lhs_ref[:, half_lanes(c)], gp).astype(BF)
        theirs_ref[...] = mm_tn(lhs_ref[:, half_lanes(1 - c)], gp).astype(BF)

    @pl.when(y == 0)
    def _():
        term(xh_ref)

    @pl.when(y != 0)
    def _():
        term(agg_ref)


def scatter_kernel(
    pairs_ref, mine_ref, theirs_ref, tiles_ref,
    down_ref, own_ref, up_ref, src, acc,
):
    c = core_of()
    half = mine_ref.shape[1]
    tiles = 2 * half // T
    ht = tiles // 2
    for i in range(ht):
        cut = slice(i * T, (i + 1) * T)
        src[c * ht + i] = mine_ref[:, cut]
        src[(1 - c) * ht + i] = theirs_ref[:, cut]
    src[tiles] = jnp.zeros((T, T), BF)
    acc[...] = jnp.zeros_like(acc)
    for p in range((tiles_ref.shape[0] - 1 + tiles) // 2):
        right = jnp.concatenate([tiles_ref[pairs_ref[1, p]], tiles_ref[pairs_ref[2, p]]], axis=1)
        prod = mm(src[pairs_ref[0, p]], right)
        acc[pairs_ref[3, p]] += prod[:, :T]
        acc[pairs_ref[4, p]] += prod[:, T:]
    for i in range(tiles):
        down_ref[i] = acc[i].astype(BF)
        own_ref[i] = acc[tiles + i]
        up_ref[i] = acc[2 * tiles + i].astype(BF)


def chip_kernel(own_ref, a_ref, b_ref, g0_ref, g1_ref, g2_ref, g3_ref, out_ref):
    tiles = own_ref.shape[0]
    out_ref[0:tiles] = (own_ref[...] + (a_ref[...].astype(F32) + b_ref[...].astype(F32))).astype(BF)
    near = g0_ref[...].astype(F32) + g1_ref[...].astype(F32)
    weights = (near + (g2_ref[...].astype(F32) + g3_ref[...].astype(F32))).astype(BF)
    out_ref[tiles] = weights[:, :T]
    out_ref[tiles + 1] = weights[:, T:]


def total_kernel(mine_ref, theirs_ref, keep_ref, recv_ref, out_ref):
    c, y = core_of(), y_of()
    tiles = mine_ref.shape[0] - 2
    ht = tiles // 2
    for i in range(ht):
        cut = slice(i * T, (i + 1) * T)
        for first, ref in ((c * ht, keep_ref), ((1 - c) * ht, recv_ref)):
            both = mine_ref[first + i].astype(F32) + theirs_ref[first + i].astype(F32)
            out_ref[first + i] = (ref[:, cut] + both).astype(BF)
    for i in range(2):
        out_ref[tiles + 2 * y + i] = mine_ref[tiles + i]
        out_ref[tiles + 2 * (1 - y) + i] = theirs_ref[tiles + i]


def restore_kernel(order_ref, own_ref, core_ref, out_ref, self_ref, neigh_ref, full):
    c = core_of()
    rows = out_ref.shape[0]
    for side, ref in ((c, own_ref), (1 - c, core_ref)):
        at = pl.ds(pl.multiple_of(side * T, T), T)
        for i in range(2):
            cut = slice(i * T, (i + 1) * T)
            self_ref[at, cut] = ref[rows // T + i].astype(F32)
            neigh_ref[at, cut] = ref[rows // T + 2 + i].astype(F32)
    for i in range(rows // T):
        cut = slice(i * T, (i + 1) * T)
        full[pl.ds(pl.multiple_of(c * T, T), T), cut] = own_ref[i]
        full[pl.ds(pl.multiple_of((1 - c) * T, T), T), cut] = core_ref[i]
    for j in range(rows // 256):
        hot = onehot_inverse(order_ref[...], j * 256, 256)
        out_ref[j * 256 : (j + 1) * 256, :] = mm_nt(hot, full[...]).astype(BF)


def output_kernel(order_ref, own_ref, core_ref, out_ref, full):
    c = core_of()
    half = own_ref.shape[0]
    rows = 2 * half
    full[pl.ds(pl.multiple_of(c * half, half), half), :] = own_ref[...]
    full[pl.ds(pl.multiple_of((1 - c) * half, half), half), :] = core_ref[...]
    for j in range(rows // 256):
        hot = onehot_inverse(order_ref[...], j * 256, 256)
        out_ref[j * 256 : (j + 1) * 256, :] = mm(hot, full[...]).astype(BF)


def call(kernel, outs, ins, spaces=None, scratch=(), name=None, out_spaces=None):
    spaces = dict(spaces or {})
    out_spaces = dict(out_spaces or {})
    specs = [pl.BlockSpec(memory_space=spaces.get(i, pltpu.VMEM)) for i in range(len(ins))]
    shapes = [jax.ShapeDtypeStruct(s, d) for s, d in outs]
    out_specs = [pl.BlockSpec(memory_space=out_spaces.get(i, pltpu.VMEM)) for i in range(len(outs))]
    single = len(outs) == 1
    return pl.pallas_call(
        kernel,
        out_shape=shapes[0] if single else shapes,
        in_specs=specs,
        out_specs=out_specs[0] if single else out_specs,
        scratch_shapes=list(scratch),
        name=name,
        compiler_params=pltpu.CompilerParams(vmem_limit_bytes=VMEM),
        cost_estimate=pl.CostEstimate(flops=0, bytes_accessed=0, transcendentals=0),
    )(*ins)


def shards(
    features, degree, order, tile_rows, tile_cols, tile_count, tile_values, w_self, w_neigh, out_grad
):
    rows, width = features.shape
    half = rows // 2
    tiles = rows // T
    ht = tiles // 2
    blocks = lax.axis_size("blk")
    reps = lax.axis_size("rep")
    assert reps == 4 and width == 2 * T

    def hop(x, blk_step, rep_mask):
        pairs = [
            (b * reps + r, ((b + blk_step) % blocks) * reps + (r ^ rep_mask))
            for b in range(blocks)
            for r in range(reps)
        ]
        return lax.ppermute(x, ("blk", "rep"), pairs)

    def swap_core(x):
        return lax.ppermute(x, "rep", [(r, r ^ 1) for r in range(reps)])

    def swap_y(x):
        return lax.ppermute(x, "rep", [(r, r ^ 2) for r in range(reps)])

    def swap_diag(x):
        return lax.ppermute(x, "rep", [(r, r ^ 3) for r in range(reps)])

    def stay(x):
        return pltpu.with_memory_space_constraint(x, pltpu.MemorySpace.HBM)

    order8 = stay(order.reshape(tiles, T))
    deg = stay(degree.reshape(1, rows))
    features, out_grad = stay(features), stay(out_grad)
    va = tile_values[0, 0]
    slots = va.shape[0]
    hbm = pltpu.MemorySpace.HBM
    smem = pltpu.SMEM
    dma = pltpu.SemaphoreType.DMA

    feats_c, mine = call(
        reorder_kernel,
        [((rows, T), BF), ((8, T), jnp.int32)],
        [order8, features, stay(tile_rows[0]), stay(tile_cols[0]), tile_count],
        spaces={0: hbm, 1: hbm, 2: hbm, 3: hbm, 4: smem},
        scratch=[
            pltpu.VMEM((tiles, T), jnp.int32),
            pltpu.VMEM((rows, T), BF),
            pltpu.VMEM((1, slots), jnp.int32),
            pltpu.VMEM((1, slots), jnp.int32),
            dma((4,)),
        ],
        name="reorder",
    )
    prev = hop(feats_c, 1, 0)
    nxt = hop(feats_c, -1, 0)
    theirs = swap_core(mine)
    va, _ = lax.optimization_barrier((va, feats_c))
    vb = swap_core(va)
    va = stay(va)
    xh, gh, hs, sc, sr, both, pairs = call(
        prepare_kernel,
        [
            ((half, width), BF),
            ((half, width), BF),
            ((half, width), F32),
            ((half, T), F32),
            ((8, half), F32),
            ((2 * slots + 1, T, T), BF),
            ((8, T), jnp.int32),
        ],
        [mine, theirs, va, vb, order8, deg, features, out_grad, stay(w_self)],
        spaces={0: smem, 1: smem, 2: pl.ANY, 3: pl.ANY},
        out_spaces={6: smem},
        scratch=[pltpu.SMEM((2, 16), jnp.int32), dma((2,))],
        name="prepare",
    )
    here, other = call(
        gather_kernel,
        [((half, T), BF), ((half, T), BF)],
        [pairs, prev, feats_c, nxt, both],
        spaces={0: smem},
        scratch=[pltpu.VMEM((3 * rows + T, T), BF), pltpu.VMEM((tiles + 1, T, T), F32)],
        name="gather",
    )
    from_y = swap_y(here)
    from_diag = swap_diag(other)
    from_core = swap_core(other)
    act, gp, agg, s_keep, s_send = call(
        dense_kernel,
        [((half, width), BF), ((half, width), BF), ((half, width), BF), ((T, half), BF), ((T, half), BF)],
        [here, from_core, from_y, from_diag, hs, gh, sc, sr, w_neigh],
        name="dense",
    )
    s_other = swap_core(s_send)
    d_keep, d_send, g_mine, g_theirs = call(
        terms_kernel,
        [((T, half), F32), ((T, half), F32), ((T, width), BF), ((T, width), BF)],
        [xh, agg, gp, w_self],
        name="terms",
    )
    terms_in = [g_mine, swap_core(g_theirs)]
    if (blocks.bit_length() - 1) % 2:
        for x, mask in ((g_mine, 0), (g_theirs, 1)):
            pairs_of = [(b * reps + r, (b ^ 1) * reps + (r ^ mask)) for b in range(blocks) for r in range(reps)]
            terms_in.append(lax.ppermute(x, ("blk", "rep"), pairs_of))
    piece = (tiles, T, T)
    down, own, up = call(
        scatter_kernel,
        [(piece, BF), (piece, F32), (piece, BF)],
        [pairs, s_keep, s_other, both],
        spaces={0: smem},
        scratch=[pltpu.VMEM((tiles + 1, T, T), BF), pltpu.VMEM((3 * tiles + 1, T, T), F32)],
        name="scatter",
    )
    from_up = hop(down, -1, 0)
    from_down = hop(up, 1, 0)
    d_recv = swap_core(d_send)
    bits = blocks.bit_length() - 1
    assert blocks == 1 << bits and bits >= 2

    def from_block(x, mask):
        return lax.ppermute(x, "blk", [(b, b ^ mask) for b in range(blocks)])

    def four(p, q, r, s):
        near = p.astype(F32) + q.astype(F32)
        return (near + (r.astype(F32) + s.astype(F32))).astype(BF)

    at = bits % 2
    g = four(*terms_in) if at else (terms_in[0].astype(F32) + terms_in[1].astype(F32)).astype(BF)
    while True:
        parts = [g] + [from_block(g, k << at) for k in (1, 2, 3)]
        at += 2
        if at == bits:
            break
        g = four(*parts)
    chip = call(chip_kernel, [((tiles + 2, T, T), BF)], [own, from_up, from_down] + parts, name="chip")
    chip, act = lax.optimization_barrier((chip, act))
    chip_y = swap_y(chip)
    act_other = swap_core(act)
    output = call(
        output_kernel,
        [((rows, width), BF)],
        [order, act, act_other],
        scratch=[pltpu.VMEM((rows, width), BF)],
        name="output",
    )
    chip_y, output = lax.optimization_barrier((chip_y, output))
    total = call(total_kernel, [((tiles + 4, T, T), BF)], [chip, chip_y, d_keep, d_recv], name="total")
    total_core = swap_core(total)
    grad_features, grad_self, grad_neigh = call(
        restore_kernel,
        [((rows, width), BF), ((width, width), F32), ((width, width), F32)],
        [order, total, total_core],
        scratch=[pltpu.VMEM((width, rows), BF)],
        name="restore",
    )
    return output, grad_features, grad_self, grad_neigh


def solution(mesh):
    return jax.shard_map(
        shards,
        mesh=mesh,
        in_specs=(
            P("blk", None),
            P("blk"),
            P("blk", None),
            P("blk", "rep", None),
            P("blk", "rep", None),
            P("blk", "rep"),
            P("blk", "rep", None, None, None),
            P(),
            P(),
            P("blk", None),
        ),
        out_specs=(P("blk", None), P("blk", None), P(), P()),
        check_vma=False,
    )
```

```python
import jax
import jax.numpy as jnp
from jax import lax
from jax.experimental import pallas as pl
from jax.experimental.pallas import tpu as pltpu
from jax.sharding import PartitionSpec as P

BF = jnp.bfloat16
F32 = jnp.float32
T = 128
VMEM = 16 * 2**20


def mm(a, b):
    return jnp.dot(a, b, preferred_element_type=F32)


def mm_nt(a, b):
    return lax.dot_general(a, b, (((1,), (1,)), ((), ())), preferred_element_type=F32)


def mm_tn(a, b):
    return lax.dot_general(a, b, (((0,), (0,)), ((), ())), preferred_element_type=F32)


def core_of():
    return lax.rem(lax.axis_index("rep"), 2)


def y_of():
    return lax.div(lax.axis_index("rep"), 2)


def order_column(order_row):
    return jnp.transpose(jnp.broadcast_to(order_row, (T, T)))


def onehot_rows(column, count):
    lane = lax.broadcasted_iota(jnp.int32, (T, T), 1).astype(F32)
    cuts = [
        jnp.where(column == lane + float(j * T), 1.0, 0.0).astype(BF) for j in range(count // T)
    ]
    return jnp.concatenate(cuts, axis=1)


def onehot_inverse(order_row, first, rows):
    wide = (rows, order_row.shape[1])
    at = lax.broadcasted_iota(jnp.int32, wide, 0) + first
    return jnp.where(jnp.broadcast_to(order_row, wide) == at, 1.0, 0.0).astype(BF)


def half_lanes(index):
    return pl.ds(pl.multiple_of(index * T, T), T)


def reorder_kernel(order_hbm, x_hbm, rows_hbm, cols_hbm, count_ref, out_ref, idx_ref, order, x, rows, cols, sems):
    c = core_of()
    total = out_ref.shape[0]
    copies = [
        pltpu.make_async_copy(src, dst, sems.at[i])
        for i, (src, dst) in enumerate(
            (
                (order_hbm, order),
                (x_hbm.at[:, half_lanes(c)], x),
                (rows_hbm, rows),
                (cols_hbm, cols),
            )
        )
    ]
    for copy in copies:
        copy.start()
    copies[0].wait()
    columns = [order_column(order[i : i + 1, :].astype(F32)) for i in range(total // T)]
    copies[1].wait()
    for i in range(total // T):
        out_ref[i * T : (i + 1) * T, :] = mm(onehot_rows(columns[i], total), x[...]).astype(BF)
    for copy in copies[2:]:
        copy.wait()
    slots = rows.shape[1]
    idx_ref[...] = jnp.zeros_like(idx_ref)
    idx_ref[0:1, 0:slots] = rows[...]
    idx_ref[1:2, 0:slots] = cols[...]
    idx_ref[2:3, :] = jnp.full((1, T), count_ref[0, 0], jnp.int32)


def pair_slots(mine, theirs, slots, row_tiles, pairs, out_ref, pending):
    dead = row_tiles
    nothing = 2 * slots
    beyond = 3 * row_tiles

    def clear(i, _):
        out_ref[0, i] = dead
        out_ref[1, i] = nothing
        out_ref[2, i] = nothing
        out_ref[3, i] = beyond
        out_ref[4, i] = beyond
        return 0

    lax.fori_loop(0, pairs, clear, 0)
    for r in range(row_tiles + 1):
        pending[0, r] = -1
        pending[1, r] = beyond

    def emit(n, r, a, b, col_a, col_b):
        out_ref[0, n] = r
        out_ref[1, n] = a
        out_ref[2, n] = b
        out_ref[3, n] = col_a
        out_ref[4, n] = col_b

    n = jnp.int32(0)
    for base, idx in ((0, mine), (slots, theirs)):
        count = idx[2, 0]

        def place(s, n, base=base, idx=idx, count=count):
            live = s < count
            r = jnp.where(live, idx[0, s], dead)
            col = jnp.where(live, idx[1, s], beyond)
            first = pending[0, r]
            whole = first >= 0

            @pl.when(whole)
            def _():
                emit(n, r, first, base + s, pending[1, r], col)
                pending[0, r] = -1

            @pl.when(jnp.logical_not(whole))
            def _():
                pending[0, r] = base + s
                pending[1, r] = col

            return n + whole.astype(jnp.int32)

        n = lax.fori_loop(0, slots, place, n)

    def rest(r, n):
        first = pending[0, r]
        left = first >= 0

        @pl.when(left)
        def _():
            emit(n, r, first, nothing, pending[1, r], beyond)

        return n + left.astype(jnp.int32)

    lax.fori_loop(0, row_tiles, rest, n)


def prepare_kernel(
    mine, theirs, va_any, vb_any, order_ref, degree_ref, x_ref, g_ref, w_ref,
    xh_ref, gh_ref, hs_ref, sc_ref, sr_ref, tiles_ref, pairs_ref, pending, sems,
):
    c = core_of()
    rows = x_ref.shape[0]
    slots = va_any.shape[0]
    copies = [
        pltpu.make_async_copy(va_any, tiles_ref.at[0:slots], sems.at[0]),
        pltpu.make_async_copy(vb_any, tiles_ref.at[slots : 2 * slots], sems.at[1]),
    ]
    for copy in copies:
        copy.start()
    tiles_ref[2 * slots] = jnp.zeros((T, T), BF)
    pair_slots(mine, theirs, slots, rows // T, slots + rows // T // 2, pairs_ref, pending)
    tiles = rows // T // 2
    deg = jnp.broadcast_to(degree_ref[...].astype(F32), (8, rows)).astype(BF)
    for i in range(tiles):
        column = order_column(order_ref[pl.ds(c * tiles + i, 1), :].astype(F32))
        hot = onehot_rows(column, rows)
        here = slice(i * T, (i + 1) * T)
        xt = mm(hot, x_ref[...]).astype(BF)
        xh_ref[here, :] = xt
        gh_ref[here, :] = mm(hot, g_ref[...]).astype(BF)
        hs_ref[here, :] = mm(xt, w_ref[...])
        scale = 1.0 / mm_nt(deg, hot)
        sr_ref[:, here] = scale
        sc_ref[here, :] = jnp.transpose(jnp.broadcast_to(scale[0:1, :], (T, T)))
    for copy in copies:
        copy.wait()


def near_part():
    return 2 - 2 * lax.rem(lax.axis_index("blk"), 2)


def gather_kernel(pairs_ref, near_ref, own_ref, far_ref, tiles_ref, here_ref, other_ref, win, acc):
    c, near = core_of(), near_part()
    rows = own_ref.shape[0]
    tiles = rows // T
    win[pl.ds(pl.multiple_of(near * rows, rows), rows), :] = near_ref[...]
    win[rows : 2 * rows, :] = own_ref[...]
    win[pl.ds(pl.multiple_of((2 - near) * rows, rows), rows), :] = far_ref[...]
    win[3 * rows : 3 * rows + T, :] = jnp.zeros((T, T), BF)
    acc[...] = jnp.zeros_like(acc)

    def window(col):
        return win[pl.ds(pl.multiple_of(col * T, T), T), :]

    for p in range((tiles_ref.shape[0] - 1 + tiles) // 2):
        left = jnp.concatenate([tiles_ref[pairs_ref[1, p]], tiles_ref[pairs_ref[2, p]]], axis=1)
        right = jnp.concatenate([window(pairs_ref[3, p]), window(pairs_ref[4, p])], axis=0)
        acc[pairs_ref[0, p]] += mm(left, right)
    for i in range(tiles // 2):
        here_ref[i * T : (i + 1) * T, :] = acc[c * (tiles // 2) + i].astype(BF)
        other_ref[i * T : (i + 1) * T, :] = acc[(1 - c) * (tiles // 2) + i].astype(BF)


def dense_kernel(
    own_ref, core_ref, y_ref, diag_ref, hs_ref, gh_ref, sc_ref, sr_ref, wn_ref,
    act_ref, gp_ref, agg_ref, keep_ref, send_ref,
):
    c = core_of()
    scale = sc_ref[...]
    agg_ref[:, half_lanes(c)] = (
        (own_ref[...].astype(F32) + y_ref[...].astype(F32)) * scale
    ).astype(BF)
    agg_ref[:, half_lanes(1 - c)] = (
        (core_ref[...].astype(F32) + diag_ref[...].astype(F32)) * scale
    ).astype(BF)
    h = hs_ref[...] + mm(agg_ref[...], wn_ref[...])
    sig = jax.nn.sigmoid(h)
    act_ref[...] = (h * sig).astype(BF)
    gp = (gh_ref[...].astype(F32) * (sig * (1.0 + h * (1.0 - sig)))).astype(BF)
    gp_ref[...] = gp
    row = sr_ref[0:1, :]
    keep_ref[...] = (mm_nt(wn_ref[pl.ds(pl.multiple_of(c * T, T), T), :], gp) * row).astype(BF)
    send_ref[...] = (mm_nt(wn_ref[pl.ds(pl.multiple_of((1 - c) * T, T), T), :], gp) * row).astype(BF)


def terms_kernel(xh_ref, agg_ref, gp_ref, ws_ref, keep_ref, send_ref, *refs):
    c, y = core_of(), y_of()
    term_refs, full_ref = refs[:4], refs[4]
    gp = gp_ref[...]
    keep_ref[...] = mm_nt(ws_ref[pl.ds(pl.multiple_of(c * T, T), T), :], gp)
    send_ref[...] = mm_nt(ws_ref[pl.ds(pl.multiple_of((1 - c) * T, T), T), :], gp)

    half = T // 2
    x = lax.rem(lax.axis_index("blk"), 2)

    def term(lhs_ref):
        for side, (keep, send) in ((c, term_refs[:2]), (1 - c, term_refs[2:])):
            full_ref[...] = mm_tn(lhs_ref[:, half_lanes(side)], gp)
            keep[...] = full_ref[pl.ds(pl.multiple_of(x * half, half), half), :].astype(BF)
            send[...] = full_ref[pl.ds(pl.multiple_of((1 - x) * half, half), half), :].astype(BF)

    @pl.when(y == 0)
    def _():
        term(xh_ref)

    @pl.when(y != 0)
    def _():
        term(agg_ref)


def scatter_kernel(
    pairs_ref, mine_ref, theirs_ref, tiles_ref,
    near_ref, own_ref, far_ref, src, acc,
):
    c, near = core_of(), near_part()
    half = mine_ref.shape[1]
    tiles = 2 * half // T
    ht = tiles // 2
    for i in range(ht):
        cut = slice(i * T, (i + 1) * T)
        src[c * ht + i] = mine_ref[:, cut]
        src[(1 - c) * ht + i] = theirs_ref[:, cut]
    src[tiles] = jnp.zeros((T, T), BF)
    acc[...] = jnp.zeros_like(acc)
    for p in range((tiles_ref.shape[0] - 1 + tiles) // 2):
        right = jnp.concatenate([tiles_ref[pairs_ref[1, p]], tiles_ref[pairs_ref[2, p]]], axis=1)
        prod = mm(src[pairs_ref[0, p]], right)
        acc[pairs_ref[3, p]] += prod[:, :T]
        acc[pairs_ref[4, p]] += prod[:, T:]
    for i in range(tiles):
        near_ref[i] = acc[near * tiles + i].astype(BF)
        own_ref[i] = acc[tiles + i]
        far_ref[i] = acc[(2 - near) * tiles + i].astype(BF)


def chip_kernel(own_ref, a_ref, b_ref, g0_ref, g1_ref, g2_ref, g3_ref, out_ref, weights_ref):
    tiles = own_ref.shape[0]
    out_ref[0:tiles] = (own_ref[...] + (a_ref[...].astype(F32) + b_ref[...].astype(F32))).astype(BF)
    near = g0_ref[...].astype(F32) + g1_ref[...].astype(F32)
    weights = (near + (g2_ref[...].astype(F32) + g3_ref[...].astype(F32))).astype(BF)
    half = T // 2
    for ref in (weights_ref, out_ref.at[tiles]):
        ref[:half, :] = weights[:, :T]
        ref[half:, :] = weights[:, T:]


def total_kernel(mine_ref, theirs_ref, keep_ref, recv_ref, near_ref, near_y_ref, out_ref):
    c, y, x = core_of(), y_of(), lax.rem(lax.axis_index("blk"), 2)
    tiles = mine_ref.shape[0] - 1
    ht = tiles // 2
    for i in range(ht):
        cut = slice(i * T, (i + 1) * T)
        for first, ref in ((c * ht, keep_ref), ((1 - c) * ht, recv_ref)):
            both = mine_ref[first + i].astype(F32) + theirs_ref[first + i].astype(F32)
            out_ref[first + i] = (ref[:, cut] + both).astype(BF)
    out_ref[tiles + 2 * y + x] = mine_ref[tiles]
    out_ref[tiles + 2 * y + 1 - x] = near_ref[...]
    out_ref[tiles + 2 * (1 - y) + x] = theirs_ref[tiles]
    out_ref[tiles + 2 * (1 - y) + 1 - x] = near_y_ref[...]


def restore_kernel(order_ref, own_ref, core_ref, out_ref, self_ref, neigh_ref, full):
    c = core_of()
    rows = out_ref.shape[0]
    half = T // 2
    for side, ref in ((c, own_ref), (1 - c, core_ref)):
        for x in range(2):
            at = pl.ds(pl.multiple_of(side * T + x * half, half), half)
            for i in range(2):
                cut = slice(i * T, (i + 1) * T)
                rows_of = slice(i * half, (i + 1) * half)
                self_ref[at, cut] = ref[rows // T + x, rows_of, :].astype(F32)
                neigh_ref[at, cut] = ref[rows // T + 2 + x, rows_of, :].astype(F32)
    for i in range(rows // T):
        cut = slice(i * T, (i + 1) * T)
        full[pl.ds(pl.multiple_of(c * T, T), T), cut] = own_ref[i]
        full[pl.ds(pl.multiple_of((1 - c) * T, T), T), cut] = core_ref[i]
    for j in range(rows // 256):
        hot = onehot_inverse(order_ref[...], j * 256, 256)
        out_ref[j * 256 : (j + 1) * 256, :] = mm_nt(hot, full[...]).astype(BF)


def output_kernel(order_ref, own_ref, core_ref, out_ref, full):
    c = core_of()
    half = own_ref.shape[0]
    rows = 2 * half
    full[pl.ds(pl.multiple_of(c * half, half), half), :] = own_ref[...]
    full[pl.ds(pl.multiple_of((1 - c) * half, half), half), :] = core_ref[...]
    for j in range(rows // 256):
        hot = onehot_inverse(order_ref[...], j * 256, 256)
        out_ref[j * 256 : (j + 1) * 256, :] = mm(hot, full[...]).astype(BF)


def call(kernel, outs, ins, spaces=None, scratch=(), name=None, out_spaces=None):
    spaces = dict(spaces or {})
    out_spaces = dict(out_spaces or {})
    specs = [pl.BlockSpec(memory_space=spaces.get(i, pltpu.VMEM)) for i in range(len(ins))]
    shapes = [jax.ShapeDtypeStruct(s, d) for s, d in outs]
    out_specs = [pl.BlockSpec(memory_space=out_spaces.get(i, pltpu.VMEM)) for i in range(len(outs))]
    single = len(outs) == 1
    return pl.pallas_call(
        kernel,
        out_shape=shapes[0] if single else shapes,
        in_specs=specs,
        out_specs=out_specs[0] if single else out_specs,
        scratch_shapes=list(scratch),
        name=name,
        compiler_params=pltpu.CompilerParams(vmem_limit_bytes=VMEM),
        cost_estimate=pl.CostEstimate(flops=0, bytes_accessed=0, transcendentals=0),
    )(*ins)


def shards(
    features, degree, order, tile_rows, tile_cols, tile_count, tile_values, w_self, w_neigh, out_grad
):
    rows, width = features.shape
    half = rows // 2
    tiles = rows // T
    ht = tiles // 2
    blocks = lax.axis_size("blk")
    reps = lax.axis_size("rep")
    assert reps == 4 and width == 2 * T

    def swap_near(x):
        return lax.ppermute(x, "blk", [(b, b ^ 1) for b in range(blocks)])

    def swap_far(x):
        return lax.ppermute(x, "blk", [(b, (b + 2 * (b % 2) - 1) % blocks) for b in range(blocks)])

    def swap_core(x):
        return lax.ppermute(x, "rep", [(r, r ^ 1) for r in range(reps)])

    def swap_y(x):
        return lax.ppermute(x, "rep", [(r, r ^ 2) for r in range(reps)])

    def swap_diag(x):
        return lax.ppermute(x, "rep", [(r, r ^ 3) for r in range(reps)])

    def stay(x):
        return pltpu.with_memory_space_constraint(x, pltpu.MemorySpace.HBM)

    order8 = stay(order.reshape(tiles, T))
    deg = stay(degree.reshape(1, rows))
    features, out_grad = stay(features), stay(out_grad)
    va = tile_values[0, 0]
    slots = va.shape[0]
    hbm = pltpu.MemorySpace.HBM
    smem = pltpu.SMEM
    dma = pltpu.SemaphoreType.DMA

    feats_c, mine = call(
        reorder_kernel,
        [((rows, T), BF), ((8, T), jnp.int32)],
        [order8, features, stay(tile_rows[0]), stay(tile_cols[0]), tile_count],
        spaces={0: hbm, 1: hbm, 2: hbm, 3: hbm, 4: smem},
        scratch=[
            pltpu.VMEM((tiles, T), jnp.int32),
            pltpu.VMEM((rows, T), BF),
            pltpu.VMEM((1, slots), jnp.int32),
            pltpu.VMEM((1, slots), jnp.int32),
            dma((4,)),
        ],
        name="reorder",
    )
    near = swap_near(feats_c)
    far = swap_far(feats_c)
    theirs = swap_core(mine)
    va, _ = lax.optimization_barrier((va, feats_c))
    vb = swap_core(va)
    va = stay(va)
    xh, gh, hs, sc, sr, both, pairs = call(
        prepare_kernel,
        [
            ((half, width), BF),
            ((half, width), BF),
            ((half, width), F32),
            ((half, T), F32),
            ((8, half), F32),
            ((2 * slots + 1, T, T), BF),
            ((8, T), jnp.int32),
        ],
        [mine, theirs, va, vb, order8, deg, features, out_grad, stay(w_self)],
        spaces={0: smem, 1: smem, 2: pl.ANY, 3: pl.ANY},
        out_spaces={6: smem},
        scratch=[pltpu.SMEM((2, 16), jnp.int32), dma((2,))],
        name="prepare",
    )
    here, other = call(
        gather_kernel,
        [((half, T), BF), ((half, T), BF)],
        [pairs, near, feats_c, far, both],
        spaces={0: smem},
        scratch=[pltpu.VMEM((3 * rows + T, T), BF), pltpu.VMEM((tiles + 1, T, T), F32)],
        name="gather",
    )
    from_y = swap_y(here)
    from_diag = swap_diag(other)
    from_core = swap_core(other)
    act, gp, agg, s_keep, s_send = call(
        dense_kernel,
        [((half, width), BF), ((half, width), BF), ((half, width), BF), ((T, half), BF), ((T, half), BF)],
        [here, from_core, from_y, from_diag, hs, gh, sc, sr, w_neigh],
        name="dense",
    )
    s_other = swap_core(s_send)
    d_keep, d_send, mine_near, mine_far, theirs_near, theirs_far = call(
        terms_kernel,
        [((T, half), F32), ((T, half), F32)] + [((T // 2, width), BF)] * 4,
        [xh, agg, gp, w_self],
        scratch=[pltpu.VMEM((T, width), F32)],
        name="terms",
    )
    def swap_pair(x, mask):
        pairs_of = [(b * reps + r, (b ^ 1) * reps + (r ^ mask)) for b in range(blocks) for r in range(reps)]
        return lax.ppermute(x, ("blk", "rep"), pairs_of)

    terms_in = [mine_near, swap_core(theirs_near), swap_pair(mine_far, 0), swap_pair(theirs_far, 1)]
    piece = (tiles, T, T)
    near, own, far = call(
        scatter_kernel,
        [(piece, BF), (piece, F32), (piece, BF)],
        [pairs, s_keep, s_other, both],
        spaces={0: smem},
        scratch=[pltpu.VMEM((tiles + 1, T, T), BF), pltpu.VMEM((3 * tiles + 1, T, T), F32)],
        name="scatter",
    )
    from_near = swap_near(near)
    from_far = swap_far(far)
    d_recv = swap_core(d_send)
    bits = blocks.bit_length() - 1
    assert blocks == 1 << bits and bits % 2 and bits > 1

    def four(p, q, r, s):
        near = p.astype(F32) + q.astype(F32)
        return (near + (r.astype(F32) + s.astype(F32))).astype(BF)

    parts = terms_in
    for at in range(1, bits, 2):
        g = four(*parts)
        parts = [g] + [
            lax.ppermute(g, "blk", [(b, b ^ (k << at)) for b in range(blocks)]) for k in (1, 2, 3)
        ]
    chip, w_own = call(chip_kernel, [((tiles + 1, T, T), BF), ((T, T), BF)], [own, from_near, from_far] + parts, name="chip")
    chip, act = lax.optimization_barrier((chip, act))
    chip_y = swap_y(chip)
    w_near = swap_pair(w_own, 0)
    w_near_y = swap_pair(w_own, 2)
    act_other = swap_core(act)
    output = call(
        output_kernel,
        [((rows, width), BF)],
        [order, act, act_other],
        scratch=[pltpu.VMEM((rows, width), BF)],
        name="output",
    )
    chip_y, output = lax.optimization_barrier((chip_y, output))
    total = call(total_kernel, [((tiles + 4, T, T), BF)], [chip, chip_y, d_keep, d_recv, w_near, w_near_y], name="total")
    total_core = swap_core(total)
    grad_features, grad_self, grad_neigh = call(
        restore_kernel,
        [((rows, width), BF), ((width, width), F32), ((width, width), F32)],
        [order, total, total_core],
        scratch=[pltpu.VMEM((width, rows), BF)],
        name="restore",
    )
    return output, grad_features, grad_self, grad_neigh


def solution(mesh):
    return jax.shard_map(
        shards,
        mesh=mesh,
        in_specs=(
            P("blk", None),
            P("blk"),
            P("blk", None),
            P("blk", "rep", None),
            P("blk", "rep", None),
            P("blk", "rep"),
            P("blk", "rep", None, None, None),
            P(),
            P(),
            P("blk", None),
        ),
        out_specs=(P("blk", None), P("blk", None), P(), P()),
        check_vma=False,
    )
```

```python
import jax
import jax.numpy as jnp
from jax import lax
from jax.experimental import pallas as pl
from jax.experimental.pallas import tpu as pltpu
from jax.sharding import PartitionSpec as P

BF = jnp.bfloat16
F32 = jnp.float32
T = 128
VMEM = 16 * 2**20


def mm(a, b):
    return jnp.dot(a, b, preferred_element_type=F32)


def mm_nt(a, b):
    return lax.dot_general(a, b, (((1,), (1,)), ((), ())), preferred_element_type=F32)


def mm_tn(a, b):
    return lax.dot_general(a, b, (((0,), (0,)), ((), ())), preferred_element_type=F32)


def core_of():
    return lax.rem(lax.axis_index("rep"), 2)


def y_of():
    return lax.div(lax.axis_index("rep"), 2)


def order_column(order_row):
    return jnp.transpose(jnp.broadcast_to(order_row, (T, T)))


def onehot_rows(column, count):
    lane = lax.broadcasted_iota(jnp.int32, (T, T), 1).astype(F32)
    cuts = [
        jnp.where(column == lane + float(j * T), 1.0, 0.0).astype(BF) for j in range(count // T)
    ]
    return jnp.concatenate(cuts, axis=1)


def onehot_inverse(order_row, first, rows):
    wide = (rows, order_row.shape[1])
    at = lax.broadcasted_iota(jnp.int32, wide, 0) + first
    return jnp.where(jnp.broadcast_to(order_row, wide) == at, 1.0, 0.0).astype(BF)


def half_lanes(index):
    return pl.ds(pl.multiple_of(index * T, T), T)


def reorder_kernel(order_hbm, x_hbm, out_ref, order, x, sems):
    total = out_ref.shape[0]
    first = pltpu.make_async_copy(order_hbm, order, sems.at[0])
    second = pltpu.make_async_copy(x_hbm.at[:, half_lanes(core_of())], x, sems.at[1])
    first.start()
    second.start()
    first.wait()
    columns = [order_column(order[i : i + 1, :].astype(F32)) for i in range(total // T)]
    second.wait()
    for i in range(total // T):
        out_ref[i * T : (i + 1) * T, :] = mm(onehot_rows(columns[i], total), x[...]).astype(BF)


def index_kernel(count_ref, rows_ref, cols_ref, after_ref, idx_ref):
    del after_ref
    slots = rows_ref.shape[1]
    idx_ref[...] = jnp.zeros_like(idx_ref)
    idx_ref[0:1, 0:slots] = rows_ref[...]
    idx_ref[1:2, 0:slots] = cols_ref[...]
    idx_ref[2:3, :] = jnp.full((1, T), count_ref[0, 0], jnp.int32)


def pair_slots(mine, theirs, slots, row_tiles, pairs, out_ref, pending):
    dead = row_tiles
    nothing = 2 * slots
    beyond = 3 * row_tiles

    def clear(i, _):
        out_ref[0, i] = dead
        out_ref[1, i] = nothing
        out_ref[2, i] = nothing
        out_ref[3, i] = beyond
        out_ref[4, i] = beyond
        return 0

    lax.fori_loop(0, pairs, clear, 0)
    for r in range(row_tiles + 1):
        pending[0, r] = -1
        pending[1, r] = beyond

    def emit(n, r, a, b, col_a, col_b):
        out_ref[0, n] = r
        out_ref[1, n] = a
        out_ref[2, n] = b
        out_ref[3, n] = col_a
        out_ref[4, n] = col_b

    n = jnp.int32(0)
    for base, idx in ((0, mine), (slots, theirs)):
        count = idx[2, 0]

        def place(s, n, base=base, idx=idx, count=count):
            live = s < count
            r = jnp.where(live, idx[0, s], dead)
            col = jnp.where(live, idx[1, s], beyond)
            first = pending[0, r]
            whole = first >= 0

            @pl.when(whole)
            def _():
                emit(n, r, first, base + s, pending[1, r], col)
                pending[0, r] = -1

            @pl.when(jnp.logical_not(whole))
            def _():
                pending[0, r] = base + s
                pending[1, r] = col

            return n + whole.astype(jnp.int32)

        n = lax.fori_loop(0, slots, place, n)

    def rest(r, n):
        first = pending[0, r]
        left = first >= 0

        @pl.when(left)
        def _():
            emit(n, r, first, nothing, pending[1, r], beyond)

        return n + left.astype(jnp.int32)

    lax.fori_loop(0, row_tiles, rest, n)


def prepare_kernel(
    mine, theirs, va_any, vb_any, order_ref, degree_ref, x_ref, g_ref, w_ref,
    xh_ref, gh_ref, hs_ref, sc_ref, sr_ref, tiles_ref, pairs_ref, pending, sems,
):
    c = core_of()
    rows = x_ref.shape[0]
    slots = va_any.shape[0]
    copies = [
        pltpu.make_async_copy(va_any, tiles_ref.at[0:slots], sems.at[0]),
        pltpu.make_async_copy(vb_any, tiles_ref.at[slots : 2 * slots], sems.at[1]),
    ]
    for copy in copies:
        copy.start()
    tiles_ref[2 * slots] = jnp.zeros((T, T), BF)
    pair_slots(mine, theirs, slots, rows // T, slots + rows // T // 2, pairs_ref, pending)
    tiles = rows // T // 2
    deg = jnp.broadcast_to(degree_ref[...].astype(F32), (8, rows)).astype(BF)
    for i in range(tiles):
        column = order_column(order_ref[pl.ds(c * tiles + i, 1), :].astype(F32))
        hot = onehot_rows(column, rows)
        here = slice(i * T, (i + 1) * T)
        xt = mm(hot, x_ref[...]).astype(BF)
        xh_ref[here, :] = xt
        gh_ref[here, :] = mm(hot, g_ref[...]).astype(BF)
        hs_ref[here, :] = mm(xt, w_ref[...])
        scale = 1.0 / mm_nt(deg, hot)
        sr_ref[:, here] = scale
        sc_ref[here, :] = jnp.transpose(jnp.broadcast_to(scale[0:1, :], (T, T)))
    for copy in copies:
        copy.wait()


def near_part():
    return 2 - 2 * lax.rem(lax.axis_index("blk"), 2)


def gather_kernel(pairs_ref, near_ref, own_ref, far_ref, tiles_ref, here_ref, other_ref, win, acc):
    c, near = core_of(), near_part()
    rows = own_ref.shape[0]
    tiles = rows // T
    win[pl.ds(pl.multiple_of(near * rows, rows), rows), :] = near_ref[...]
    win[rows : 2 * rows, :] = own_ref[...]
    win[pl.ds(pl.multiple_of((2 - near) * rows, rows), rows), :] = far_ref[...]
    win[3 * rows : 3 * rows + T, :] = jnp.zeros((T, T), BF)
    acc[...] = jnp.zeros_like(acc)

    def window(col):
        return win[pl.ds(pl.multiple_of(col * T, T), T), :]

    for p in range((tiles_ref.shape[0] - 1 + tiles) // 2):
        left = jnp.concatenate([tiles_ref[pairs_ref[1, p]], tiles_ref[pairs_ref[2, p]]], axis=1)
        right = jnp.concatenate([window(pairs_ref[3, p]), window(pairs_ref[4, p])], axis=0)
        acc[pairs_ref[0, p]] += mm(left, right)
    for i in range(tiles // 2):
        here_ref[i * T : (i + 1) * T, :] = acc[c * (tiles // 2) + i].astype(BF)
        other_ref[i * T : (i + 1) * T, :] = acc[(1 - c) * (tiles // 2) + i].astype(BF)


def dense_kernel(
    own_ref, y_ref, diag_ref, core_ref, hs_ref, gh_ref, sc_ref, sr_ref, wn_ref,
    act_ref, gp_ref, agg_ref, keep_ref, send_ref,
):
    c = core_of()
    scale = sc_ref[...]
    agg_ref[:, half_lanes(c)] = (
        (own_ref[...].astype(F32) + y_ref[...].astype(F32)) * scale
    ).astype(BF)
    agg_ref[:, half_lanes(1 - c)] = (
        (core_ref[...].astype(F32) + diag_ref[...].astype(F32)) * scale
    ).astype(BF)
    h = hs_ref[...] + mm(agg_ref[...], wn_ref[...])
    sig = jax.nn.sigmoid(h)
    act_ref[...] = (h * sig).astype(BF)
    gp = (gh_ref[...].astype(F32) * (sig * (1.0 + h * (1.0 - sig)))).astype(BF)
    gp_ref[...] = gp
    row = sr_ref[0:1, :]
    keep_ref[...] = (mm_nt(wn_ref[pl.ds(pl.multiple_of(c * T, T), T), :], gp) * row).astype(BF)
    send_ref[...] = (mm_nt(wn_ref[pl.ds(pl.multiple_of((1 - c) * T, T), T), :], gp) * row).astype(BF)


def terms_kernel(xh_ref, agg_ref, gp_ref, ws_ref, keep_ref, send_ref, *refs):
    c, y = core_of(), y_of()
    term_refs, full_ref = refs[:4], refs[4]
    gp = gp_ref[...]
    keep_ref[...] = mm_nt(ws_ref[pl.ds(pl.multiple_of(c * T, T), T), :], gp)
    send_ref[...] = mm_nt(ws_ref[pl.ds(pl.multiple_of((1 - c) * T, T), T), :], gp)

    half = T // 2
    x = lax.rem(lax.axis_index("blk"), 2)

    def term(lhs_ref):
        for side, (keep, send) in ((c, term_refs[:2]), (1 - c, term_refs[2:])):
            full_ref[...] = mm_tn(lhs_ref[:, half_lanes(side)], gp)
            keep[...] = full_ref[pl.ds(pl.multiple_of(x * half, half), half), :].astype(BF)
            send[...] = full_ref[pl.ds(pl.multiple_of((1 - x) * half, half), half), :].astype(BF)

    @pl.when(y == 0)
    def _():
        term(xh_ref)

    @pl.when(y != 0)
    def _():
        term(agg_ref)


def scatter_kernel(
    pairs_ref, mine_ref, theirs_ref, tiles_ref,
    near_ref, own_ref, far_ref, src, acc,
):
    c, near = core_of(), near_part()
    half = mine_ref.shape[1]
    tiles = 2 * half // T
    ht = tiles // 2
    for i in range(ht):
        cut = slice(i * T, (i + 1) * T)
        src[c * ht + i] = mine_ref[:, cut]
        src[(1 - c) * ht + i] = theirs_ref[:, cut]
    src[tiles] = jnp.zeros((T, T), BF)
    acc[...] = jnp.zeros_like(acc)
    for p in range((tiles_ref.shape[0] - 1 + tiles) // 2):
        right = jnp.concatenate([tiles_ref[pairs_ref[1, p]], tiles_ref[pairs_ref[2, p]]], axis=1)
        prod = mm(src[pairs_ref[0, p]], right)
        acc[pairs_ref[3, p]] += prod[:, :T]
        acc[pairs_ref[4, p]] += prod[:, T:]
    for i in range(tiles):
        near_ref[i] = acc[near * tiles + i].astype(BF)
        own_ref[i] = acc[tiles + i]
        far_ref[i] = acc[(2 - near) * tiles + i].astype(BF)


def chip_kernel(own_ref, a_ref, b_ref, g0_ref, g1_ref, g2_ref, g3_ref, out_ref, weights_ref):
    tiles = own_ref.shape[0]
    out_ref[0:tiles] = (own_ref[...] + (a_ref[...].astype(F32) + b_ref[...].astype(F32))).astype(BF)
    near = g0_ref[...].astype(F32) + g1_ref[...].astype(F32)
    weights = (near + (g2_ref[...].astype(F32) + g3_ref[...].astype(F32))).astype(BF)
    half = T // 2
    for ref in (weights_ref, out_ref.at[tiles]):
        ref[:half, :] = weights[:, :T]
        ref[half:, :] = weights[:, T:]


def total_kernel(mine_ref, theirs_ref, keep_ref, recv_ref, near_ref, near_y_ref, out_ref):
    c, y, x = core_of(), y_of(), lax.rem(lax.axis_index("blk"), 2)
    tiles = mine_ref.shape[0] - 1
    ht = tiles // 2
    for i in range(ht):
        cut = slice(i * T, (i + 1) * T)
        for first, ref in ((c * ht, keep_ref), ((1 - c) * ht, recv_ref)):
            both = mine_ref[first + i].astype(F32) + theirs_ref[first + i].astype(F32)
            out_ref[first + i] = (ref[:, cut] + both).astype(BF)
    out_ref[tiles + 2 * y + x] = mine_ref[tiles]
    out_ref[tiles + 2 * y + 1 - x] = near_ref[...]
    out_ref[tiles + 2 * (1 - y) + x] = theirs_ref[tiles]
    out_ref[tiles + 2 * (1 - y) + 1 - x] = near_y_ref[...]


def restore_kernel(order_ref, own_ref, core_ref, out_hbm, self_hbm, neigh_hbm, full, out, self_sum, neigh_sum, sems):
    c = core_of()
    rows = out.shape[0]
    half = T // 2
    for side, ref in ((c, own_ref), (1 - c, core_ref)):
        for x in range(2):
            at = pl.ds(pl.multiple_of(side * T + x * half, half), half)
            for i in range(2):
                cut = slice(i * T, (i + 1) * T)
                rows_of = slice(i * half, (i + 1) * half)
                self_sum[at, cut] = ref[rows // T + x, rows_of, :].astype(F32)
                neigh_sum[at, cut] = ref[rows // T + 2 + x, rows_of, :].astype(F32)
    copies = [
        pltpu.make_async_copy(self_sum, self_hbm, sems.at[0]),
        pltpu.make_async_copy(neigh_sum, neigh_hbm, sems.at[1]),
    ]
    for copy in copies:
        copy.start()
    for i in range(rows // T):
        cut = slice(i * T, (i + 1) * T)
        full[pl.ds(pl.multiple_of(c * T, T), T), cut] = own_ref[i]
        full[pl.ds(pl.multiple_of((1 - c) * T, T), T), cut] = core_ref[i]
    for j in range(rows // 256):
        here = slice(j * 256, (j + 1) * 256)
        hot = onehot_inverse(order_ref[...], j * 256, 256)
        out[here, :] = mm_nt(hot, full[...]).astype(BF)
        copies.append(pltpu.make_async_copy(out.at[here], out_hbm.at[here], sems.at[2 + j]))
        copies[-1].start()
    for copy in copies:
        copy.wait()


def output_kernel(order_ref, own_ref, core_ref, out_ref, full):
    c = core_of()
    half = own_ref.shape[0]
    rows = 2 * half
    full[pl.ds(pl.multiple_of(c * half, half), half), :] = own_ref[...]
    full[pl.ds(pl.multiple_of((1 - c) * half, half), half), :] = core_ref[...]
    for j in range(rows // 256):
        hot = onehot_inverse(order_ref[...], j * 256, 256)
        out_ref[j * 256 : (j + 1) * 256, :] = mm(hot, full[...]).astype(BF)


def call(kernel, outs, ins, spaces=None, scratch=(), name=None, out_spaces=None):
    spaces = dict(spaces or {})
    out_spaces = dict(out_spaces or {})
    specs = [pl.BlockSpec(memory_space=spaces.get(i, pltpu.VMEM)) for i in range(len(ins))]
    shapes = [jax.ShapeDtypeStruct(s, d) for s, d in outs]
    out_specs = [pl.BlockSpec(memory_space=out_spaces.get(i, pltpu.VMEM)) for i in range(len(outs))]
    single = len(outs) == 1
    return pl.pallas_call(
        kernel,
        out_shape=shapes[0] if single else shapes,
        in_specs=specs,
        out_specs=out_specs[0] if single else out_specs,
        scratch_shapes=list(scratch),
        name=name,
        compiler_params=pltpu.CompilerParams(vmem_limit_bytes=VMEM),
        cost_estimate=pl.CostEstimate(flops=0, bytes_accessed=0, transcendentals=0),
    )(*ins)


def shards(
    features, degree, order, tile_rows, tile_cols, tile_count, tile_values, w_self, w_neigh, out_grad
):
    rows, width = features.shape
    half = rows // 2
    tiles = rows // T
    ht = tiles // 2
    blocks = lax.axis_size("blk")
    reps = lax.axis_size("rep")
    assert reps == 4 and width == 2 * T

    def swap_near(x):
        return lax.ppermute(x, "blk", [(b, b ^ 1) for b in range(blocks)])

    def swap_far(x):
        return lax.ppermute(x, "blk", [(b, (b + 2 * (b % 2) - 1) % blocks) for b in range(blocks)])

    def swap_core(x):
        return lax.ppermute(x, "rep", [(r, r ^ 1) for r in range(reps)])

    def swap_y(x):
        return lax.ppermute(x, "rep", [(r, r ^ 2) for r in range(reps)])

    def swap_diag(x):
        return lax.ppermute(x, "rep", [(r, r ^ 3) for r in range(reps)])

    def stay(x):
        return pltpu.with_memory_space_constraint(x, pltpu.MemorySpace.HBM)

    order8 = stay(order.reshape(tiles, T))
    deg = stay(degree.reshape(1, rows))
    features, out_grad = stay(features), stay(out_grad)
    va = tile_values[0, 0]
    slots = va.shape[0]
    hbm = pltpu.MemorySpace.HBM
    smem = pltpu.SMEM
    dma = pltpu.SemaphoreType.DMA

    feats_c = call(
        reorder_kernel,
        [((rows, T), BF)],
        [order8, features],
        spaces={0: hbm, 1: hbm},
        scratch=[pltpu.VMEM((tiles, T), jnp.int32), pltpu.VMEM((rows, T), BF), dma((2,))],
        name="reorder",
    )
    mine = call(
        index_kernel,
        [((8, T), jnp.int32)],
        [tile_count, stay(tile_rows[0]), stay(tile_cols[0]), feats_c],
        spaces={0: smem, 3: pl.ANY},
        name="index",
    )
    near = swap_near(feats_c)
    far = swap_far(feats_c)
    theirs = swap_core(mine)
    vb = swap_core(va)
    va = stay(va)
    xh, gh, hs, sc, sr, both, pairs = call(
        prepare_kernel,
        [
            ((half, width), BF),
            ((half, width), BF),
            ((half, width), F32),
            ((half, T), F32),
            ((8, half), F32),
            ((2 * slots + 1, T, T), BF),
            ((8, T), jnp.int32),
        ],
        [mine, theirs, va, vb, order8, deg, features, out_grad, stay(w_self)],
        spaces={0: smem, 1: smem, 2: pl.ANY, 3: pl.ANY},
        out_spaces={6: smem},
        scratch=[pltpu.SMEM((2, 16), jnp.int32), dma((2,))],
        name="prepare",
    )
    here, other = call(
        gather_kernel,
        [((half, T), BF), ((half, T), BF)],
        [pairs, near, feats_c, far, both],
        spaces={0: smem},
        scratch=[pltpu.VMEM((3 * rows + T, T), BF), pltpu.VMEM((tiles + 1, T, T), F32)],
        name="gather",
    )
    from_y = swap_y(here)
    from_diag = swap_diag(other)
    from_core = swap_core(other)
    act, gp, agg, s_keep, s_send = call(
        dense_kernel,
        [((half, width), BF), ((half, width), BF), ((half, width), BF), ((T, half), BF), ((T, half), BF)],
        [here, from_y, from_diag, from_core, hs, gh, sc, sr, w_neigh],
        name="dense",
    )
    s_other = swap_core(s_send)
    d_keep, d_send, mine_near, mine_far, theirs_near, theirs_far = call(
        terms_kernel,
        [((T, half), F32), ((T, half), F32)] + [((T // 2, width), BF)] * 4,
        [xh, agg, gp, w_self],
        scratch=[pltpu.VMEM((T, width), F32)],
        name="terms",
    )
    def swap_pair(x, mask):
        pairs_of = [(b * reps + r, (b ^ 1) * reps + (r ^ mask)) for b in range(blocks) for r in range(reps)]
        return lax.ppermute(x, ("blk", "rep"), pairs_of)

    terms_in = [mine_near, swap_core(theirs_near), swap_pair(mine_far, 0), swap_pair(theirs_far, 1)]
    piece = (tiles, T, T)
    near, own, far = call(
        scatter_kernel,
        [(piece, BF), (piece, F32), (piece, BF)],
        [pairs, s_keep, s_other, both],
        spaces={0: smem},
        scratch=[pltpu.VMEM((tiles + 1, T, T), BF), pltpu.VMEM((3 * tiles + 1, T, T), F32)],
        name="scatter",
    )
    from_near = swap_near(near)
    from_far = swap_far(far)
    d_recv = swap_core(d_send)
    bits = blocks.bit_length() - 1
    assert blocks == 1 << bits and bits % 2 and bits > 1

    def four(p, q, r, s):
        near = p.astype(F32) + q.astype(F32)
        return (near + (r.astype(F32) + s.astype(F32))).astype(BF)

    parts = terms_in
    for at in range(1, bits, 2):
        g = four(*parts)
        parts = [g] + [
            lax.ppermute(g, "blk", [(b, b ^ (k << at)) for b in range(blocks)]) for k in (1, 2, 3)
        ]
    chip, w_own = call(chip_kernel, [((tiles + 1, T, T), BF), ((T, T), BF)], [own, from_near, from_far] + parts, name="chip")
    chip, act = lax.optimization_barrier((chip, act))
    chip_y = swap_y(chip)
    w_near = swap_pair(w_own, 0)
    w_near_y = swap_pair(w_own, 2)
    act_other = swap_core(act)
    output = call(
        output_kernel,
        [((rows, width), BF)],
        [order, act, act_other],
        scratch=[pltpu.VMEM((rows, width), BF)],
        name="output",
    )
    chip_y, output = lax.optimization_barrier((chip_y, output))
    total = call(total_kernel, [((tiles + 4, T, T), BF)], [chip, chip_y, d_keep, d_recv, w_near, w_near_y], name="total")
    total_core = swap_core(total)
    grad_features, grad_self, grad_neigh = call(
        restore_kernel,
        [((rows, width), BF), ((width, width), F32), ((width, width), F32)],
        [order, total, total_core],
        out_spaces={i: pl.ANY for i in range(3)},
        scratch=[
            pltpu.VMEM((width, rows), BF),
            pltpu.VMEM((rows, width), BF),
            pltpu.VMEM((width, width), F32),
            pltpu.VMEM((width, width), F32),
            dma((2 + rows // 256,)),
        ],
        name="restore",
    )
    return output, grad_features, grad_self, grad_neigh


def solution(mesh):
    return jax.shard_map(
        shards,
        mesh=mesh,
        in_specs=(
            P("blk", None),
            P("blk"),
            P("blk", None),
            P("blk", "rep", None),
            P("blk", "rep", None),
            P("blk", "rep"),
            P("blk", "rep", None, None, None),
            P(),
            P(),
            P("blk", None),
        ),
        out_specs=(P("blk", None), P("blk", None), P(), P()),
        check_vma=False,
    )
```

```python
import jax
import jax.numpy as jnp
from jax import lax
from jax.experimental import pallas as pl
from jax.experimental.pallas import tpu as pltpu
from jax.sharding import PartitionSpec as P

BF = jnp.bfloat16
F32 = jnp.float32
T = 128
VMEM = 16 * 2**20


def mm(a, b):
    return jnp.dot(a, b, preferred_element_type=F32)


def mm_nt(a, b):
    return lax.dot_general(a, b, (((1,), (1,)), ((), ())), preferred_element_type=F32)


def mm_tn(a, b):
    return lax.dot_general(a, b, (((0,), (0,)), ((), ())), preferred_element_type=F32)


def core_of():
    return lax.rem(lax.axis_index("rep"), 2)


def y_of():
    return lax.div(lax.axis_index("rep"), 2)


def order_column(order_row):
    return jnp.transpose(jnp.broadcast_to(order_row, (T, T)))


def onehot_rows(column, count):
    lane = lax.broadcasted_iota(jnp.int32, (T, T), 1).astype(F32)
    cuts = [
        jnp.where(column == lane + float(j * T), 1.0, 0.0).astype(BF) for j in range(count // T)
    ]
    return jnp.concatenate(cuts, axis=1)


def onehot_inverse(order_row, first, rows):
    wide = (rows, order_row.shape[1])
    at = lax.broadcasted_iota(jnp.int32, wide, 0) + first
    return jnp.where(jnp.broadcast_to(order_row, wide) == at, 1.0, 0.0).astype(BF)


def half_lanes(index):
    return pl.ds(pl.multiple_of(index * T, T), T)


def reorder_kernel(order_hbm, x_hbm, out_ref, order, x, sems):
    total = out_ref.shape[0]
    first = pltpu.make_async_copy(order_hbm, order, sems.at[0])
    second = pltpu.make_async_copy(x_hbm.at[:, half_lanes(core_of())], x, sems.at[1])
    first.start()
    second.start()
    first.wait()
    columns = [order_column(order[i : i + 1, :].astype(F32)) for i in range(total // T)]
    second.wait()
    for i in range(total // T):
        out_ref[i * T : (i + 1) * T, :] = mm(onehot_rows(columns[i], total), x[...]).astype(BF)


def index_kernel(count_ref, rows_ref, cols_ref, after_ref, idx_ref):
    del after_ref
    slots = rows_ref.shape[1]
    idx_ref[...] = jnp.zeros_like(idx_ref)
    idx_ref[0:1, 0:slots] = rows_ref[...]
    idx_ref[1:2, 0:slots] = cols_ref[...]
    idx_ref[2:3, :] = jnp.full((1, T), count_ref[0, 0], jnp.int32)


def pair_slots(mine, theirs, slots, row_tiles, out_ref):
    lane = lax.broadcasted_iota(jnp.int32, mine.shape, 1)
    here = lane < slots
    theirs = pltpu.roll(theirs, slots, 1)
    both = jnp.where(here, mine, theirs)
    live = jnp.where(here, lane, lane - slots) < jnp.broadcast_to(both[2:3, :], lane.shape)
    live = jnp.logical_and(live, lane < 2 * slots)
    rows = jnp.where(live, jnp.broadcast_to(both[0:1, :], lane.shape), row_tiles).astype(F32)

    def along(x):
        return jnp.broadcast_to(x, (T, T))

    def down(x):
        return jnp.transpose(along(x))

    def parity(x):
        return x - 2.0 * jnp.floor(x * 0.5)

    def count(where):
        return jnp.sum(jnp.where(where, 1.0, 0.0), axis=0, keepdims=True)

    first = lax.broadcasted_iota(jnp.int32, (T, T), 0).astype(F32)
    second = lax.broadcasted_iota(jnp.int32, (T, T), 1).astype(F32)
    row_a, row_d = along(rows[0:1, :]), down(rows[0:1, :])
    rank = count(jnp.logical_and(row_a == row_d, first < second))
    rank_d = down(rank)
    odd = parity(rank_d) > 0.5
    before = count(jnp.logical_and(row_d < row_a, jnp.logical_not(odd)))
    place = jnp.where(rows[0:1, :] < row_tiles, before + jnp.floor(rank * 0.5), -1.0)
    hit = down(place) == second
    col_d = down(both[1:2, :].astype(F32))

    def pick(value, default, which):
        chosen = jnp.logical_and(hit, which)
        return (default + jnp.sum(jnp.where(chosen, value - default, 0.0), axis=0, keepdims=True)).astype(jnp.int32)

    even = jnp.logical_not(odd)
    out_ref[...] = jnp.zeros_like(out_ref)
    out_ref[0:1, :] = pick(row_d, float(row_tiles), even)
    out_ref[1:2, :] = pick(first, 2.0 * slots, even)
    out_ref[2:3, :] = pick(first, 2.0 * slots, odd)
    out_ref[3:4, :] = pick(col_d, 3.0 * row_tiles, even)
    out_ref[4:5, :] = pick(col_d, 3.0 * row_tiles, odd)


def prepare_kernel(
    mine, theirs, va_any, vb_any, order_ref, degree_ref, x_ref, g_ref, w_ref,
    xh_ref, gh_ref, hs_ref, sc_ref, sr_ref, tiles_ref, pairs_ref, sems,
):
    c = core_of()
    rows = x_ref.shape[0]
    slots = va_any.shape[0]
    copies = [
        pltpu.make_async_copy(va_any, tiles_ref.at[0:slots], sems.at[0]),
        pltpu.make_async_copy(vb_any, tiles_ref.at[slots : 2 * slots], sems.at[1]),
    ]
    for copy in copies:
        copy.start()
    tiles_ref[2 * slots] = jnp.zeros((T, T), BF)
    pair_slots(mine[...], theirs[...], slots, rows // T, pairs_ref)
    tiles = rows // T // 2
    deg = jnp.broadcast_to(degree_ref[...].astype(F32), (8, rows)).astype(BF)
    for i in range(tiles):
        column = order_column(order_ref[pl.ds(c * tiles + i, 1), :].astype(F32))
        hot = onehot_rows(column, rows)
        here = slice(i * T, (i + 1) * T)
        xt = mm(hot, x_ref[...]).astype(BF)
        xh_ref[here, :] = xt
        gh_ref[here, :] = mm(hot, g_ref[...]).astype(BF)
        hs_ref[here, :] = mm(xt, w_ref[...])
        scale = 1.0 / mm_nt(deg, hot)
        sr_ref[:, here] = scale
        sc_ref[here, :] = jnp.transpose(jnp.broadcast_to(scale[0:1, :], (T, T)))
    for copy in copies:
        copy.wait()


def near_part():
    return 2 - 2 * lax.rem(lax.axis_index("blk"), 2)


def gather_kernel(pairs_ref, near_ref, own_ref, far_ref, tiles_ref, here_ref, other_ref, win, acc):
    c, near = core_of(), near_part()
    rows = own_ref.shape[0]
    tiles = rows // T
    win[pl.ds(pl.multiple_of(near * rows, rows), rows), :] = near_ref[...]
    win[rows : 2 * rows, :] = own_ref[...]
    win[pl.ds(pl.multiple_of((2 - near) * rows, rows), rows), :] = far_ref[...]
    win[3 * rows : 3 * rows + T, :] = jnp.zeros((T, T), BF)
    acc[...] = jnp.zeros_like(acc)

    def window(col):
        return win[pl.ds(pl.multiple_of(col * T, T), T), :]

    for p in range((tiles_ref.shape[0] - 1 + tiles) // 2):
        left = jnp.concatenate([tiles_ref[pairs_ref[1, p]], tiles_ref[pairs_ref[2, p]]], axis=1)
        right = jnp.concatenate([window(pairs_ref[3, p]), window(pairs_ref[4, p])], axis=0)
        acc[pairs_ref[0, p]] += mm(left, right)
    for i in range(tiles // 2):
        here_ref[i * T : (i + 1) * T, :] = acc[c * (tiles // 2) + i].astype(BF)
        other_ref[i * T : (i + 1) * T, :] = acc[(1 - c) * (tiles // 2) + i].astype(BF)


def dense_kernel(
    own_ref, y_ref, diag_ref, core_ref, hs_ref, gh_ref, sc_ref, sr_ref, wn_ref,
    act_ref, gp_ref, agg_ref, keep_ref, send_ref,
):
    c = core_of()
    scale = sc_ref[...]
    agg_ref[:, half_lanes(c)] = (
        (own_ref[...].astype(F32) + y_ref[...].astype(F32)) * scale
    ).astype(BF)
    agg_ref[:, half_lanes(1 - c)] = (
        (core_ref[...].astype(F32) + diag_ref[...].astype(F32)) * scale
    ).astype(BF)
    h = hs_ref[...] + mm(agg_ref[...], wn_ref[...])
    sig = jax.nn.sigmoid(h)
    act_ref[...] = (h * sig).astype(BF)
    gp = (gh_ref[...].astype(F32) * (sig * (1.0 + h * (1.0 - sig)))).astype(BF)
    gp_ref[...] = gp
    row = sr_ref[0:1, :]
    keep_ref[...] = (mm_nt(wn_ref[pl.ds(pl.multiple_of(c * T, T), T), :], gp) * row).astype(BF)
    send_ref[...] = (mm_nt(wn_ref[pl.ds(pl.multiple_of((1 - c) * T, T), T), :], gp) * row).astype(BF)


def dself_kernel(gp_ref, ws_ref, keep_ref, send_ref):
    c = core_of()
    keep_ref[...] = mm_nt(ws_ref[pl.ds(pl.multiple_of(c * T, T), T), :], gp_ref[...])
    send_ref[...] = mm_nt(ws_ref[pl.ds(pl.multiple_of((1 - c) * T, T), T), :], gp_ref[...])


def terms_kernel(xh_ref, agg_ref, gp_ref, *refs):
    c, y = core_of(), y_of()
    term_refs, full_ref = refs[:4], refs[4]
    gp = gp_ref[...]

    half = T // 2
    x = lax.rem(lax.axis_index("blk"), 2)

    def term(lhs_ref):
        for side, (keep, send) in ((c, term_refs[:2]), (1 - c, term_refs[2:])):
            full_ref[...] = mm_tn(lhs_ref[:, half_lanes(side)], gp)
            keep[...] = full_ref[pl.ds(pl.multiple_of(x * half, half), half), :].astype(BF)
            send[...] = full_ref[pl.ds(pl.multiple_of((1 - x) * half, half), half), :].astype(BF)

    @pl.when(y == 0)
    def _():
        term(xh_ref)

    @pl.when(y != 0)
    def _():
        term(agg_ref)


def scatter_kernel(
    pairs_ref, mine_ref, theirs_ref, tiles_ref,
    near_ref, own_ref, far_ref, src, acc,
):
    c, near = core_of(), near_part()
    half = mine_ref.shape[1]
    tiles = 2 * half // T
    ht = tiles // 2
    for i in range(ht):
        cut = slice(i * T, (i + 1) * T)
        src[c * ht + i] = mine_ref[:, cut]
        src[(1 - c) * ht + i] = theirs_ref[:, cut]
    src[tiles] = jnp.zeros((T, T), BF)
    acc[...] = jnp.zeros_like(acc)
    for p in range((tiles_ref.shape[0] - 1 + tiles) // 2):
        right = jnp.concatenate([tiles_ref[pairs_ref[1, p]], tiles_ref[pairs_ref[2, p]]], axis=1)
        prod = mm(src[pairs_ref[0, p]], right)
        acc[pairs_ref[3, p]] += prod[:, :T]
        acc[pairs_ref[4, p]] += prod[:, T:]
    for i in range(tiles):
        near_ref[i] = acc[near * tiles + i].astype(BF)
        own_ref[i] = acc[tiles + i]
        far_ref[i] = acc[(2 - near) * tiles + i].astype(BF)


def chip_kernel(own_ref, a_ref, b_ref, g0_ref, g1_ref, g2_ref, g3_ref, out_ref, weights_ref):
    tiles = own_ref.shape[0]
    out_ref[0:tiles] = (own_ref[...] + (a_ref[...].astype(F32) + b_ref[...].astype(F32))).astype(BF)
    near = g0_ref[...].astype(F32) + g1_ref[...].astype(F32)
    weights = (near + (g2_ref[...].astype(F32) + g3_ref[...].astype(F32))).astype(BF)
    half = T // 2
    for ref in (weights_ref, out_ref.at[tiles]):
        ref[:half, :] = weights[:, :T]
        ref[half:, :] = weights[:, T:]


def total_kernel(mine_ref, theirs_ref, keep_ref, recv_ref, near_ref, near_y_ref, out_ref):
    c, y, x = core_of(), y_of(), lax.rem(lax.axis_index("blk"), 2)
    tiles = mine_ref.shape[0] - 1
    ht = tiles // 2
    for i in range(ht):
        cut = slice(i * T, (i + 1) * T)
        for first, ref in ((c * ht, keep_ref), ((1 - c) * ht, recv_ref)):
            both = mine_ref[first + i].astype(F32) + theirs_ref[first + i].astype(F32)
            out_ref[first + i] = (ref[:, cut] + both).astype(BF)
    out_ref[tiles + 2 * y + x] = mine_ref[tiles]
    out_ref[tiles + 2 * y + 1 - x] = near_ref[...]
    out_ref[tiles + 2 * (1 - y) + x] = theirs_ref[tiles]
    out_ref[tiles + 2 * (1 - y) + 1 - x] = near_y_ref[...]


def restore_kernel(order_ref, own_ref, core_ref, out_hbm, self_hbm, neigh_hbm, full, out, self_sum, neigh_sum, sems):
    c = core_of()
    rows = out.shape[0]
    half = T // 2
    for side, ref in ((c, own_ref), (1 - c, core_ref)):
        for x in range(2):
            at = pl.ds(pl.multiple_of(side * T + x * half, half), half)
            for i in range(2):
                cut = slice(i * T, (i + 1) * T)
                rows_of = slice(i * half, (i + 1) * half)
                self_sum[at, cut] = ref[rows // T + x, rows_of, :].astype(F32)
                neigh_sum[at, cut] = ref[rows // T + 2 + x, rows_of, :].astype(F32)
    copies = [
        pltpu.make_async_copy(self_sum, self_hbm, sems.at[0]),
        pltpu.make_async_copy(neigh_sum, neigh_hbm, sems.at[1]),
    ]
    for copy in copies:
        copy.start()
    for i in range(rows // T):
        cut = slice(i * T, (i + 1) * T)
        full[pl.ds(pl.multiple_of(c * T, T), T), cut] = own_ref[i]
        full[pl.ds(pl.multiple_of((1 - c) * T, T), T), cut] = core_ref[i]
    for j in range(rows // 256):
        here = slice(j * 256, (j + 1) * 256)
        hot = onehot_inverse(order_ref[...], j * 256, 256)
        out[here, :] = mm_nt(hot, full[...]).astype(BF)
        copies.append(pltpu.make_async_copy(out.at[here], out_hbm.at[here], sems.at[2 + j]))
        copies[-1].start()
    for copy in copies:
        copy.wait()


def output_kernel(order_ref, own_ref, core_ref, out_ref, full):
    c = core_of()
    half = own_ref.shape[0]
    rows = 2 * half
    full[pl.ds(pl.multiple_of(c * half, half), half), :] = own_ref[...]
    full[pl.ds(pl.multiple_of((1 - c) * half, half), half), :] = core_ref[...]
    for j in range(rows // 256):
        hot = onehot_inverse(order_ref[...], j * 256, 256)
        out_ref[j * 256 : (j + 1) * 256, :] = mm(hot, full[...]).astype(BF)


def call(kernel, outs, ins, spaces=None, scratch=(), name=None, out_spaces=None):
    spaces = dict(spaces or {})
    out_spaces = dict(out_spaces or {})
    specs = [pl.BlockSpec(memory_space=spaces.get(i, pltpu.VMEM)) for i in range(len(ins))]
    shapes = [jax.ShapeDtypeStruct(s, d) for s, d in outs]
    out_specs = [pl.BlockSpec(memory_space=out_spaces.get(i, pltpu.VMEM)) for i in range(len(outs))]
    single = len(outs) == 1
    return pl.pallas_call(
        kernel,
        out_shape=shapes[0] if single else shapes,
        in_specs=specs,
        out_specs=out_specs[0] if single else out_specs,
        scratch_shapes=list(scratch),
        name=name,
        compiler_params=pltpu.CompilerParams(vmem_limit_bytes=VMEM),
        cost_estimate=pl.CostEstimate(flops=0, bytes_accessed=0, transcendentals=0),
    )(*ins)


def shards(
    features, degree, order, tile_rows, tile_cols, tile_count, tile_values, w_self, w_neigh, out_grad
):
    rows, width = features.shape
    half = rows // 2
    tiles = rows // T
    ht = tiles // 2
    blocks = lax.axis_size("blk")
    reps = lax.axis_size("rep")
    assert reps == 4 and width == 2 * T

    def swap_near(x):
        return lax.ppermute(x, "blk", [(b, b ^ 1) for b in range(blocks)])

    def swap_far(x):
        return lax.ppermute(x, "blk", [(b, (b + 2 * (b % 2) - 1) % blocks) for b in range(blocks)])

    def swap_core(x):
        return lax.ppermute(x, "rep", [(r, r ^ 1) for r in range(reps)])

    def swap_y(x):
        return lax.ppermute(x, "rep", [(r, r ^ 2) for r in range(reps)])

    def swap_diag(x):
        return lax.ppermute(x, "rep", [(r, r ^ 3) for r in range(reps)])

    def stay(x):
        return pltpu.with_memory_space_constraint(x, pltpu.MemorySpace.HBM)

    order8 = stay(order.reshape(tiles, T))
    deg = stay(degree.reshape(1, rows))
    features, out_grad = stay(features), stay(out_grad)
    va = tile_values[0, 0]
    slots = va.shape[0]
    hbm = pltpu.MemorySpace.HBM
    smem = pltpu.SMEM
    dma = pltpu.SemaphoreType.DMA

    feats_c = call(
        reorder_kernel,
        [((rows, T), BF)],
        [order8, features],
        spaces={0: hbm, 1: hbm},
        scratch=[pltpu.VMEM((tiles, T), jnp.int32), pltpu.VMEM((rows, T), BF), dma((2,))],
        name="reorder",
    )
    mine = call(
        index_kernel,
        [((8, T), jnp.int32)],
        [tile_count, stay(tile_rows[0]), stay(tile_cols[0]), feats_c],
        spaces={0: smem, 3: pl.ANY},
        name="index",
    )
    near = swap_near(feats_c)
    far = swap_far(feats_c)
    theirs = swap_core(mine)
    vb = swap_core(va)
    va = stay(va)
    xh, gh, hs, sc, sr, both, pairs = call(
        prepare_kernel,
        [
            ((half, width), BF),
            ((half, width), BF),
            ((half, width), F32),
            ((half, T), F32),
            ((8, half), F32),
            ((2 * slots + 1, T, T), BF),
            ((8, T), jnp.int32),
        ],
        [mine, theirs, va, vb, order8, deg, features, out_grad, stay(w_self)],
        spaces={2: pl.ANY, 3: pl.ANY},
        scratch=[dma((2,))],
        name="prepare",
    )
    here, other = call(
        gather_kernel,
        [((half, T), BF), ((half, T), BF)],
        [pairs, near, feats_c, far, both],
        spaces={0: smem},
        scratch=[pltpu.VMEM((3 * rows + T, T), BF), pltpu.VMEM((tiles + 1, T, T), F32)],
        name="gather",
    )
    from_y = swap_y(here)
    from_diag = swap_diag(other)
    from_core = swap_core(other)
    act, gp, agg, s_keep, s_send = call(
        dense_kernel,
        [((half, width), BF), ((half, width), BF), ((half, width), BF), ((T, half), BF), ((T, half), BF)],
        [here, from_y, from_diag, from_core, hs, gh, sc, sr, w_neigh],
        name="dense",
    )
    s_other = swap_core(s_send)
    mine_near, mine_far, theirs_near, theirs_far = call(
        terms_kernel,
        [((T // 2, width), BF)] * 4,
        [xh, agg, gp],
        scratch=[pltpu.VMEM((T, width), F32)],
        name="terms",
    )
    def swap_pair(x, mask):
        pairs_of = [(b * reps + r, (b ^ 1) * reps + (r ^ mask)) for b in range(blocks) for r in range(reps)]
        return lax.ppermute(x, ("blk", "rep"), pairs_of)

    terms_in = [mine_near, swap_core(theirs_near), swap_pair(mine_far, 0), swap_pair(theirs_far, 1)]
    piece = (tiles, T, T)
    near, own, far = call(
        scatter_kernel,
        [(piece, BF), (piece, F32), (piece, BF)],
        [pairs, s_keep, s_other, both],
        spaces={0: smem},
        scratch=[pltpu.VMEM((tiles + 1, T, T), BF), pltpu.VMEM((3 * tiles + 1, T, T), F32)],
        name="scatter",
    )
    from_near = swap_near(near)
    from_far = swap_far(far)
    d_keep, d_send = call(dself_kernel, [((T, half), F32)] * 2, [gp, w_self], name="dself")
    d_recv = swap_core(d_send)
    bits = blocks.bit_length() - 1
    assert blocks == 1 << bits and bits % 2 and bits > 1

    def four(p, q, r, s):
        near = p.astype(F32) + q.astype(F32)
        return (near + (r.astype(F32) + s.astype(F32))).astype(BF)

    parts = terms_in
    for at in range(1, bits, 2):
        g = four(*parts)
        parts = [g] + [
            lax.ppermute(g, "blk", [(b, b ^ (k << at)) for b in range(blocks)]) for k in (1, 2, 3)
        ]
    chip, w_own = call(chip_kernel, [((tiles + 1, T, T), BF), ((T, T), BF)], [own, from_near, from_far] + parts, name="chip")
    chip, act = lax.optimization_barrier((chip, act))
    chip_y = swap_y(chip)
    w_near = swap_pair(w_own, 0)
    w_near_y = swap_pair(w_own, 2)
    act_other = swap_core(act)
    output = call(
        output_kernel,
        [((rows, width), BF)],
        [order, act, act_other],
        scratch=[pltpu.VMEM((rows, width), BF)],
        name="output",
    )
    chip_y, output = lax.optimization_barrier((chip_y, output))
    total = call(total_kernel, [((tiles + 4, T, T), BF)], [chip, chip_y, d_keep, d_recv, w_near, w_near_y], name="total")
    total_core = swap_core(total)
    grad_features, grad_self, grad_neigh = call(
        restore_kernel,
        [((rows, width), BF), ((width, width), F32), ((width, width), F32)],
        [order, total, total_core],
        out_spaces={i: pl.ANY for i in range(3)},
        scratch=[
            pltpu.VMEM((width, rows), BF),
            pltpu.VMEM((rows, width), BF),
            pltpu.VMEM((width, width), F32),
            pltpu.VMEM((width, width), F32),
            dma((2 + rows // 256,)),
        ],
        name="restore",
    )
    return output, grad_features, grad_self, grad_neigh


def solution(mesh):
    return jax.shard_map(
        shards,
        mesh=mesh,
        in_specs=(
            P("blk", None),
            P("blk"),
            P("blk", None),
            P("blk", "rep", None),
            P("blk", "rep", None),
            P("blk", "rep"),
            P("blk", "rep", None, None, None),
            P(),
            P(),
            P("blk", None),
        ),
        out_specs=(P("blk", None), P("blk", None), P(), P()),
        check_vma=False,
    )
```

```python
import jax
import jax.numpy as jnp
from jax import lax
from jax.experimental import pallas as pl
from jax.experimental.pallas import tpu as pltpu
from jax.sharding import PartitionSpec as P

BF = jnp.bfloat16
F32 = jnp.float32
T = 128
VMEM = 16 * 2**20


def mm(a, b):
    return jnp.dot(a, b, preferred_element_type=F32)


def mm_nt(a, b):
    return lax.dot_general(a, b, (((1,), (1,)), ((), ())), preferred_element_type=F32)


def mm_tn(a, b):
    return lax.dot_general(a, b, (((0,), (0,)), ((), ())), preferred_element_type=F32)


def core_of():
    return lax.rem(lax.axis_index("rep"), 2)


def y_of():
    return lax.div(lax.axis_index("rep"), 2)


def order_column(order_row):
    return jnp.transpose(jnp.broadcast_to(order_row, (T, T)))


def onehot_rows(column, count):
    lane = lax.broadcasted_iota(jnp.int32, (T, T), 1).astype(F32)
    cuts = [
        jnp.where(column == lane + float(j * T), 1.0, 0.0).astype(BF) for j in range(count // T)
    ]
    return jnp.concatenate(cuts, axis=1)


def onehot_inverse(order_row, first, rows):
    wide = (rows, order_row.shape[1])
    at = lax.broadcasted_iota(jnp.int32, wide, 0) + first
    return jnp.where(jnp.broadcast_to(order_row, wide) == at, 1.0, 0.0).astype(BF)


def half_lanes(index):
    return pl.ds(pl.multiple_of(index * T, T), T)


def reorder_kernel(order_hbm, x_hbm, out_ref, order, x, sems):
    total = out_ref.shape[0]
    first = pltpu.make_async_copy(order_hbm, order, sems.at[0])
    second = pltpu.make_async_copy(x_hbm.at[:, half_lanes(core_of())], x, sems.at[1])
    first.start()
    second.start()
    first.wait()
    columns = [order_column(order[i : i + 1, :].astype(F32)) for i in range(total // T)]
    second.wait()
    for i in range(total // T):
        out_ref[i * T : (i + 1) * T, :] = mm(onehot_rows(columns[i], total), x[...]).astype(BF)


def index_kernel(count_ref, rows_ref, cols_ref, after_ref, idx_ref):
    del after_ref
    slots = rows_ref.shape[1]
    idx_ref[...] = jnp.zeros_like(idx_ref)
    idx_ref[0:1, 0:slots] = rows_ref[...]
    idx_ref[1:2, 0:slots] = cols_ref[...]
    idx_ref[2:3, :] = jnp.full((1, T), count_ref[0, 0], jnp.int32)


def pair_slots(mine, theirs, slots, row_tiles, out_ref):
    lane = lax.broadcasted_iota(jnp.int32, mine.shape, 1)
    here = lane < slots
    theirs = pltpu.roll(theirs, slots, 1)
    both = jnp.where(here, mine, theirs)
    live = jnp.where(here, lane, lane - slots) < jnp.broadcast_to(both[2:3, :], lane.shape)
    live = jnp.logical_and(live, lane < 2 * slots)
    rows = jnp.where(live, jnp.broadcast_to(both[0:1, :], lane.shape), row_tiles).astype(F32)

    def along(x):
        return jnp.broadcast_to(x, (T, T))

    def down(x):
        return jnp.transpose(along(x))

    def parity(x):
        return x - 2.0 * jnp.floor(x * 0.5)

    def count(where):
        return jnp.sum(jnp.where(where, 1.0, 0.0), axis=0, keepdims=True)

    first = lax.broadcasted_iota(jnp.int32, (T, T), 0).astype(F32)
    second = lax.broadcasted_iota(jnp.int32, (T, T), 1).astype(F32)
    cols = both[1:2, :].astype(F32)
    own = jnp.logical_and(cols >= row_tiles, cols < 2 * row_tiles)
    key = rows[0:1, :] + jnp.where(own, 64.0, 0.0)
    key_a, key_d = along(key), down(key)
    row_d, col_d = down(rows[0:1, :]), down(cols)
    own_a, own_d = along(jnp.where(own, 1.0, 0.0)), down(jnp.where(own, 1.0, 0.0))
    rank = count(jnp.logical_and(key_a == key_d, first < second))
    rank_d = down(rank)
    odd = parity(rank_d) > 0.5
    even = jnp.logical_not(odd)
    lower = jnp.logical_and(key_d < key_a, own_d == own_a)
    before = count(jnp.logical_and(lower, even))
    place = jnp.where(rows[0:1, :] < row_tiles, before + jnp.floor(rank * 0.5), -1.0)
    hit = down(place) == second
    alive = row_d < row_tiles

    def pick(value, default, which):
        return (default + jnp.sum(jnp.where(which, value - default, 0.0), axis=0, keepdims=True)).astype(jnp.int32)

    out_ref[...] = jnp.zeros_like(out_ref)
    for base, mark in ((0, 0.0), (8, 1.0)):
        of_class = own_d == mark
        chosen = jnp.logical_and(hit, of_class)
        one, two = jnp.logical_and(chosen, even), jnp.logical_and(chosen, odd)
        out_ref[base : base + 1, :] = pick(row_d, float(row_tiles), one)
        out_ref[base + 1 : base + 2, :] = pick(first, 2.0 * slots, one)
        out_ref[base + 2 : base + 3, :] = pick(first, 2.0 * slots, two)
        out_ref[base + 3 : base + 4, :] = pick(col_d, 3.0 * row_tiles, one)
        out_ref[base + 4 : base + 5, :] = pick(col_d, 3.0 * row_tiles, two)
        pairs = count(jnp.logical_and(jnp.logical_and(of_class, alive), even))
        out_ref[base + 5 : base + 6, :] = pairs.astype(jnp.int32)


def for_pairs(pairs_ref, base, most, body):
    size = (most + 3) // 4
    for start in range(0, most, size):

        @pl.when(pairs_ref[base + 5, 0] > start)
        def _(start=start):
            for p in range(start, min(start + size, most)):
                body(p)


def prepare_kernel(
    mine, theirs, va_any, vb_any, order_ref, degree_ref, x_ref, g_ref, w_ref,
    xh_ref, gh_ref, hs_ref, sc_ref, sr_ref, tiles_ref, pairs_ref, sems,
):
    c = core_of()
    rows = x_ref.shape[0]
    slots = va_any.shape[0]
    copies = [
        pltpu.make_async_copy(va_any, tiles_ref.at[0:slots], sems.at[0]),
        pltpu.make_async_copy(vb_any, tiles_ref.at[slots : 2 * slots], sems.at[1]),
    ]
    for copy in copies:
        copy.start()
    tiles_ref[2 * slots] = jnp.zeros((T, T), BF)
    pair_slots(mine[...], theirs[...], slots, rows // T, pairs_ref)
    tiles = rows // T // 2
    deg = jnp.broadcast_to(degree_ref[...].astype(F32), (8, rows)).astype(BF)
    for i in range(tiles):
        column = order_column(order_ref[pl.ds(c * tiles + i, 1), :].astype(F32))
        hot = onehot_rows(column, rows)
        here = slice(i * T, (i + 1) * T)
        xt = mm(hot, x_ref[...]).astype(BF)
        xh_ref[here, :] = xt
        gh_ref[here, :] = mm(hot, g_ref[...]).astype(BF)
        hs_ref[here, :] = mm(xt, w_ref[...])
        scale = 1.0 / mm_nt(deg, hot)
        sr_ref[:, here] = scale
        sc_ref[here, :] = jnp.transpose(jnp.broadcast_to(scale[0:1, :], (T, T)))
    for copy in copies:
        copy.wait()


def near_part():
    return 2 - 2 * lax.rem(lax.axis_index("blk"), 2)


def gather_pair(pairs_ref, base, p, tiles_ref, window, acc):
    left = jnp.concatenate([tiles_ref[pairs_ref[base + 1, p]], tiles_ref[pairs_ref[base + 2, p]]], axis=1)
    right = jnp.concatenate([window(pairs_ref[base + 3, p]), window(pairs_ref[base + 4, p])], axis=0)
    acc[pairs_ref[base, p]] += mm(left, right)


def gather_own_kernel(pairs_ref, own_ref, tiles_ref, acc, win):
    rows = own_ref.shape[0]
    tiles = rows // T
    win[0:rows, :] = own_ref[...]
    win[rows : rows + T, :] = jnp.zeros((T, T), BF)
    acc[...] = jnp.zeros_like(acc)

    def window(col):
        return win[pl.ds(pl.multiple_of(jnp.minimum(col - tiles, tiles) * T, T), T), :]

    most = (tiles_ref.shape[0] - 1 + tiles) // 2
    for_pairs(pairs_ref, 8, most, lambda p: gather_pair(pairs_ref, 8, p, tiles_ref, window, acc))


def gather_kernel(pairs_ref, near_ref, start_ref, far_ref, tiles_ref, here_ref, other_ref, win, acc):
    c, near = core_of(), near_part()
    rows = near_ref.shape[0]
    tiles = rows // T
    win[pl.ds(pl.multiple_of(near * rows, rows), rows), :] = near_ref[...]
    win[pl.ds(pl.multiple_of((2 - near) * rows, rows), rows), :] = far_ref[...]
    win[3 * rows : 3 * rows + T, :] = jnp.zeros((T, T), BF)
    acc[...] = start_ref[...]

    def window(col):
        return win[pl.ds(pl.multiple_of(col * T, T), T), :]

    most = (tiles_ref.shape[0] - 1 + tiles) // 2
    for_pairs(pairs_ref, 0, most, lambda p: gather_pair(pairs_ref, 0, p, tiles_ref, window, acc))
    for i in range(tiles // 2):
        here_ref[i * T : (i + 1) * T, :] = acc[c * (tiles // 2) + i].astype(BF)
        other_ref[i * T : (i + 1) * T, :] = acc[(1 - c) * (tiles // 2) + i].astype(BF)


def dense_kernel(
    own_ref, y_ref, diag_ref, core_ref, hs_ref, gh_ref, sc_ref, sr_ref, wn_ref,
    act_ref, gp_ref, agg_ref, keep_ref, send_ref,
):
    c = core_of()
    scale = sc_ref[...]
    agg_ref[:, half_lanes(c)] = (
        (own_ref[...].astype(F32) + y_ref[...].astype(F32)) * scale
    ).astype(BF)
    agg_ref[:, half_lanes(1 - c)] = (
        (core_ref[...].astype(F32) + diag_ref[...].astype(F32)) * scale
    ).astype(BF)
    h = hs_ref[...] + mm(agg_ref[...], wn_ref[...])
    sig = jax.nn.sigmoid(h)
    act_ref[...] = (h * sig).astype(BF)
    gp = (gh_ref[...].astype(F32) * (sig * (1.0 + h * (1.0 - sig)))).astype(BF)
    gp_ref[...] = gp
    row = sr_ref[0:1, :]
    keep_ref[...] = (mm_nt(wn_ref[pl.ds(pl.multiple_of(c * T, T), T), :], gp) * row).astype(BF)
    send_ref[...] = (mm_nt(wn_ref[pl.ds(pl.multiple_of((1 - c) * T, T), T), :], gp) * row).astype(BF)


def dself_kernel(gp_ref, ws_ref, keep_ref, send_ref):
    c = core_of()
    keep_ref[...] = mm_nt(ws_ref[pl.ds(pl.multiple_of(c * T, T), T), :], gp_ref[...])
    send_ref[...] = mm_nt(ws_ref[pl.ds(pl.multiple_of((1 - c) * T, T), T), :], gp_ref[...])


def terms_kernel(xh_ref, agg_ref, gp_ref, *refs):
    c, y = core_of(), y_of()
    term_refs, full_ref = refs[:4], refs[4]
    gp = gp_ref[...]

    half = T // 2
    x = lax.rem(lax.axis_index("blk"), 2)

    def term(lhs_ref):
        for side, (keep, send) in ((c, term_refs[:2]), (1 - c, term_refs[2:])):
            full_ref[...] = mm_tn(lhs_ref[:, half_lanes(side)], gp)
            keep[...] = full_ref[pl.ds(pl.multiple_of(x * half, half), half), :].astype(BF)
            send[...] = full_ref[pl.ds(pl.multiple_of((1 - x) * half, half), half), :].astype(BF)

    @pl.when(y == 0)
    def _():
        term(xh_ref)

    @pl.when(y != 0)
    def _():
        term(agg_ref)


def scatter_pairs(pairs_ref, base, mine_ref, theirs_ref, tiles_ref, src, acc, at):
    c = core_of()
    half = mine_ref.shape[1]
    tiles = 2 * half // T
    ht = tiles // 2
    for i in range(ht):
        cut = slice(i * T, (i + 1) * T)
        src[c * ht + i] = mine_ref[:, cut]
        src[(1 - c) * ht + i] = theirs_ref[:, cut]
    src[tiles] = jnp.zeros((T, T), BF)
    acc[...] = jnp.zeros_like(acc)

    def body(p):
        right = jnp.concatenate(
            [tiles_ref[pairs_ref[base + 1, p]], tiles_ref[pairs_ref[base + 2, p]]], axis=1
        )
        prod = mm(src[pairs_ref[base, p]], right)
        acc[at(pairs_ref[base + 3, p])] += prod[:, :T]
        acc[at(pairs_ref[base + 4, p])] += prod[:, T:]

    for_pairs(pairs_ref, base, (tiles_ref.shape[0] - 1 + tiles) // 2, body)


def scatter_kernel(pairs_ref, mine_ref, theirs_ref, tiles_ref, near_ref, far_ref, src, acc):
    near = near_part()
    tiles = near_ref.shape[0]
    scatter_pairs(pairs_ref, 0, mine_ref, theirs_ref, tiles_ref, src, acc, lambda col: col)
    for i in range(tiles):
        near_ref[i] = acc[near * tiles + i].astype(BF)
        far_ref[i] = acc[(2 - near) * tiles + i].astype(BF)


def scatter_own_kernel(pairs_ref, mine_ref, theirs_ref, tiles_ref, after_ref, own_ref, src, acc):
    del after_ref
    tiles = own_ref.shape[0]
    scatter_pairs(
        pairs_ref, 8, mine_ref, theirs_ref, tiles_ref, src, acc, lambda col: jnp.minimum(col - tiles, tiles)
    )
    own_ref[...] = acc[0:tiles]


def chip_kernel(own_ref, a_ref, b_ref, g0_ref, g1_ref, g2_ref, g3_ref, out_ref, weights_ref):
    tiles = own_ref.shape[0]
    out_ref[0:tiles] = (own_ref[...] + (a_ref[...].astype(F32) + b_ref[...].astype(F32))).astype(BF)
    near = g0_ref[...].astype(F32) + g1_ref[...].astype(F32)
    weights = (near + (g2_ref[...].astype(F32) + g3_ref[...].astype(F32))).astype(BF)
    half = T // 2
    for ref in (weights_ref, out_ref.at[tiles]):
        ref[:half, :] = weights[:, :T]
        ref[half:, :] = weights[:, T:]


def total_kernel(mine_ref, theirs_ref, keep_ref, recv_ref, near_ref, near_y_ref, out_ref):
    c, y, x = core_of(), y_of(), lax.rem(lax.axis_index("blk"), 2)
    tiles = mine_ref.shape[0] - 1
    ht = tiles // 2
    for i in range(ht):
        cut = slice(i * T, (i + 1) * T)
        for first, ref in ((c * ht, keep_ref), ((1 - c) * ht, recv_ref)):
            both = mine_ref[first + i].astype(F32) + theirs_ref[first + i].astype(F32)
            out_ref[first + i] = (ref[:, cut] + both).astype(BF)
    out_ref[tiles + 2 * y + x] = mine_ref[tiles]
    out_ref[tiles + 2 * y + 1 - x] = near_ref[...]
    out_ref[tiles + 2 * (1 - y) + x] = theirs_ref[tiles]
    out_ref[tiles + 2 * (1 - y) + 1 - x] = near_y_ref[...]


def restore_kernel(order_ref, own_ref, core_ref, out_hbm, self_hbm, neigh_hbm, full, out, self_sum, neigh_sum, sems):
    c = core_of()
    rows = out.shape[0]
    half = T // 2
    for side, ref in ((c, own_ref), (1 - c, core_ref)):
        for x in range(2):
            at = pl.ds(pl.multiple_of(side * T + x * half, half), half)
            for i in range(2):
                cut = slice(i * T, (i + 1) * T)
                rows_of = slice(i * half, (i + 1) * half)
                self_sum[at, cut] = ref[rows // T + x, rows_of, :].astype(F32)
                neigh_sum[at, cut] = ref[rows // T + 2 + x, rows_of, :].astype(F32)
    copies = [
        pltpu.make_async_copy(self_sum, self_hbm, sems.at[0]),
        pltpu.make_async_copy(neigh_sum, neigh_hbm, sems.at[1]),
    ]
    for copy in copies:
        copy.start()
    for i in range(rows // T):
        cut = slice(i * T, (i + 1) * T)
        full[pl.ds(pl.multiple_of(c * T, T), T), cut] = own_ref[i]
        full[pl.ds(pl.multiple_of((1 - c) * T, T), T), cut] = core_ref[i]
    for j in range(rows // 256):
        here = slice(j * 256, (j + 1) * 256)
        hot = onehot_inverse(order_ref[...], j * 256, 256)
        out[here, :] = mm_nt(hot, full[...]).astype(BF)
        copies.append(pltpu.make_async_copy(out.at[here], out_hbm.at[here], sems.at[2 + j]))
        copies[-1].start()
    for copy in copies:
        copy.wait()


def output_kernel(order_ref, own_ref, core_ref, out_ref, full):
    c = core_of()
    half = own_ref.shape[0]
    rows = 2 * half
    full[pl.ds(pl.multiple_of(c * half, half), half), :] = own_ref[...]
    full[pl.ds(pl.multiple_of((1 - c) * half, half), half), :] = core_ref[...]
    for j in range(rows // 256):
        hot = onehot_inverse(order_ref[...], j * 256, 256)
        out_ref[j * 256 : (j + 1) * 256, :] = mm(hot, full[...]).astype(BF)


def call(kernel, outs, ins, spaces=None, scratch=(), name=None, out_spaces=None):
    spaces = dict(spaces or {})
    out_spaces = dict(out_spaces or {})
    specs = [pl.BlockSpec(memory_space=spaces.get(i, pltpu.VMEM)) for i in range(len(ins))]
    shapes = [jax.ShapeDtypeStruct(s, d) for s, d in outs]
    out_specs = [pl.BlockSpec(memory_space=out_spaces.get(i, pltpu.VMEM)) for i in range(len(outs))]
    single = len(outs) == 1
    return pl.pallas_call(
        kernel,
        out_shape=shapes[0] if single else shapes,
        in_specs=specs,
        out_specs=out_specs[0] if single else out_specs,
        scratch_shapes=list(scratch),
        name=name,
        compiler_params=pltpu.CompilerParams(vmem_limit_bytes=VMEM),
        cost_estimate=pl.CostEstimate(flops=0, bytes_accessed=0, transcendentals=0),
    )(*ins)


def shards(
    features, degree, order, tile_rows, tile_cols, tile_count, tile_values, w_self, w_neigh, out_grad
):
    rows, width = features.shape
    half = rows // 2
    tiles = rows // T
    ht = tiles // 2
    blocks = lax.axis_size("blk")
    reps = lax.axis_size("rep")
    assert reps == 4 and width == 2 * T

    def swap_near(x):
        return lax.ppermute(x, "blk", [(b, b ^ 1) for b in range(blocks)])

    def swap_far(x):
        return lax.ppermute(x, "blk", [(b, (b + 2 * (b % 2) - 1) % blocks) for b in range(blocks)])

    def swap_core(x):
        return lax.ppermute(x, "rep", [(r, r ^ 1) for r in range(reps)])

    def swap_y(x):
        return lax.ppermute(x, "rep", [(r, r ^ 2) for r in range(reps)])

    def swap_diag(x):
        return lax.ppermute(x, "rep", [(r, r ^ 3) for r in range(reps)])

    def stay(x):
        return pltpu.with_memory_space_constraint(x, pltpu.MemorySpace.HBM)

    order8 = stay(order.reshape(tiles, T))
    deg = stay(degree.reshape(1, rows))
    features, out_grad = stay(features), stay(out_grad)
    va = tile_values[0, 0]
    slots = va.shape[0]
    hbm = pltpu.MemorySpace.HBM
    smem = pltpu.SMEM
    dma = pltpu.SemaphoreType.DMA

    feats_c = call(
        reorder_kernel,
        [((rows, T), BF)],
        [order8, features],
        spaces={0: hbm, 1: hbm},
        scratch=[pltpu.VMEM((tiles, T), jnp.int32), pltpu.VMEM((rows, T), BF), dma((2,))],
        name="reorder",
    )
    mine = call(
        index_kernel,
        [((8, T), jnp.int32)],
        [tile_count, stay(tile_rows[0]), stay(tile_cols[0]), feats_c],
        spaces={0: smem, 3: pl.ANY},
        name="index",
    )
    near = swap_near(feats_c)
    far = swap_far(feats_c)
    theirs = swap_core(mine)
    vb = swap_core(va)
    va = stay(va)
    xh, gh, hs, sc, sr, both, pairs = call(
        prepare_kernel,
        [
            ((half, width), BF),
            ((half, width), BF),
            ((half, width), F32),
            ((half, T), F32),
            ((8, half), F32),
            ((2 * slots + 1, T, T), BF),
            ((16, T), jnp.int32),
        ],
        [mine, theirs, va, vb, order8, deg, features, out_grad, stay(w_self)],
        spaces={2: pl.ANY, 3: pl.ANY},
        scratch=[dma((2,))],
        name="prepare",
    )
    part = call(
        gather_own_kernel,
        [((tiles + 1, T, T), F32)],
        [pairs, feats_c, both],
        spaces={0: smem},
        scratch=[pltpu.VMEM((rows + T, T), BF)],
        name="gather_own",
    )
    here, other = call(
        gather_kernel,
        [((half, T), BF), ((half, T), BF)],
        [pairs, near, part, far, both],
        spaces={0: smem},
        scratch=[pltpu.VMEM((3 * rows + T, T), BF), pltpu.VMEM((tiles + 1, T, T), F32)],
        name="gather",
    )
    from_y = swap_y(here)
    from_diag = swap_diag(other)
    from_core = swap_core(other)
    act, gp, agg, s_keep, s_send = call(
        dense_kernel,
        [((half, width), BF), ((half, width), BF), ((half, width), BF), ((T, half), BF), ((T, half), BF)],
        [here, from_y, from_diag, from_core, hs, gh, sc, sr, w_neigh],
        name="dense",
    )
    s_other = swap_core(s_send)
    mine_near, mine_far, theirs_near, theirs_far = call(
        terms_kernel,
        [((T // 2, width), BF)] * 4,
        [xh, agg, gp],
        scratch=[pltpu.VMEM((T, width), F32)],
        name="terms",
    )
    def swap_pair(x, mask):
        pairs_of = [(b * reps + r, (b ^ 1) * reps + (r ^ mask)) for b in range(blocks) for r in range(reps)]
        return lax.ppermute(x, ("blk", "rep"), pairs_of)

    terms_in = [mine_near, swap_core(theirs_near), swap_pair(mine_far, 0), swap_pair(theirs_far, 1)]
    piece = (tiles, T, T)
    near, far = call(
        scatter_kernel,
        [(piece, BF)] * 2,
        [pairs, s_keep, s_other, both],
        spaces={0: smem},
        scratch=[pltpu.VMEM((tiles + 1, T, T), BF), pltpu.VMEM((3 * tiles + 1, T, T), F32)],
        name="scatter",
    )
    own = call(
        scatter_own_kernel,
        [(piece, F32)],
        [pairs, s_keep, s_other, both, near],
        spaces={0: smem, 4: pl.ANY},
        scratch=[pltpu.VMEM((tiles + 1, T, T), BF), pltpu.VMEM((tiles + 1, T, T), F32)],
        name="scatter_own",
    )
    from_near = swap_near(near)
    from_far = swap_far(far)
    d_keep, d_send = call(dself_kernel, [((T, half), F32)] * 2, [gp, w_self], name="dself")
    d_recv = swap_core(d_send)
    bits = blocks.bit_length() - 1
    assert blocks == 1 << bits and bits % 2 and bits > 1

    def four(p, q, r, s):
        near = p.astype(F32) + q.astype(F32)
        return (near + (r.astype(F32) + s.astype(F32))).astype(BF)

    parts = terms_in
    for at in range(1, bits, 2):
        g = four(*parts)
        parts = [g] + [
            lax.ppermute(g, "blk", [(b, b ^ (k << at)) for b in range(blocks)]) for k in (1, 2, 3)
        ]
    chip, w_own = call(chip_kernel, [((tiles + 1, T, T), BF), ((T, T), BF)], [own, from_near, from_far] + parts, name="chip")
    chip, act = lax.optimization_barrier((chip, act))
    chip_y = swap_y(chip)
    w_near = swap_pair(w_own, 0)
    w_near_y = swap_pair(w_own, 2)
    act_other = swap_core(act)
    output = call(
        output_kernel,
        [((rows, width), BF)],
        [order, act, act_other],
        scratch=[pltpu.VMEM((rows, width), BF)],
        name="output",
    )
    chip_y, output = lax.optimization_barrier((chip_y, output))
    total = call(total_kernel, [((tiles + 4, T, T), BF)], [chip, chip_y, d_keep, d_recv, w_near, w_near_y], name="total")
    total_core = swap_core(total)
    grad_features, grad_self, grad_neigh = call(
        restore_kernel,
        [((rows, width), BF), ((width, width), F32), ((width, width), F32)],
        [order, total, total_core],
        out_spaces={i: pl.ANY for i in range(3)},
        scratch=[
            pltpu.VMEM((width, rows), BF),
            pltpu.VMEM((rows, width), BF),
            pltpu.VMEM((width, width), F32),
            pltpu.VMEM((width, width), F32),
            dma((2 + rows // 256,)),
        ],
        name="restore",
    )
    return output, grad_features, grad_self, grad_neigh


def solution(mesh):
    return jax.shard_map(
        shards,
        mesh=mesh,
        in_specs=(
            P("blk", None),
            P("blk"),
            P("blk", None),
            P("blk", "rep", None),
            P("blk", "rep", None),
            P("blk", "rep"),
            P("blk", "rep", None, None, None),
            P(),
            P(),
            P("blk", None),
        ),
        out_specs=(P("blk", None), P("blk", None), P(), P()),
        check_vma=False,
    )
```

```python
import jax
import jax.numpy as jnp
from jax import lax
from jax.experimental import pallas as pl
from jax.experimental.pallas import tpu as pltpu
from jax.sharding import PartitionSpec as P

BF = jnp.bfloat16
F32 = jnp.float32
T = 128
VMEM = 16 * 2**20


def mm(a, b):
    return jnp.dot(a, b, preferred_element_type=F32)


def mm_nt(a, b):
    return lax.dot_general(a, b, (((1,), (1,)), ((), ())), preferred_element_type=F32)


def mm_tn(a, b):
    return lax.dot_general(a, b, (((0,), (0,)), ((), ())), preferred_element_type=F32)


def core_of():
    return lax.rem(lax.axis_index("rep"), 2)


def y_of():
    return lax.div(lax.axis_index("rep"), 2)


def order_column(order_row):
    return jnp.transpose(jnp.broadcast_to(order_row, (T, T)))


def onehot_rows(column, count):
    lane = lax.broadcasted_iota(jnp.int32, (T, T), 1).astype(F32)
    cuts = [
        jnp.where(column == lane + float(j * T), 1.0, 0.0).astype(BF) for j in range(count // T)
    ]
    return jnp.concatenate(cuts, axis=1)


def onehot_inverse(order_row, first, rows):
    wide = (rows, order_row.shape[1])
    at = lax.broadcasted_iota(jnp.int32, wide, 0) + first
    return jnp.where(jnp.broadcast_to(order_row, wide) == at, 1.0, 0.0).astype(BF)


def half_lanes(index):
    return pl.ds(pl.multiple_of(index * T, T), T)


def reorder_kernel(order_hbm, x_hbm, out_ref, order, x, sems):
    total = out_ref.shape[0]
    first = pltpu.make_async_copy(order_hbm, order, sems.at[0])
    second = pltpu.make_async_copy(x_hbm.at[:, half_lanes(core_of())], x, sems.at[1])
    first.start()
    second.start()
    first.wait()
    columns = [order_column(order[i : i + 1, :].astype(F32)) for i in range(total // T)]
    second.wait()
    for i in range(total // T):
        out_ref[i * T : (i + 1) * T, :] = mm(onehot_rows(columns[i], total), x[...]).astype(BF)


def index_kernel(count_ref, rows_ref, cols_ref, after_ref, idx_ref):
    del after_ref
    slots = rows_ref.shape[1]
    idx_ref[...] = jnp.zeros_like(idx_ref)
    idx_ref[0:1, 0:slots] = rows_ref[...]
    idx_ref[1:2, 0:slots] = cols_ref[...]
    idx_ref[2:3, :] = jnp.full((1, T), count_ref[0, 0], jnp.int32)


def pair_slots(mine, theirs, slots, row_tiles, out_ref):
    lane = lax.broadcasted_iota(jnp.int32, mine.shape, 1)
    here = lane < slots
    theirs = pltpu.roll(theirs, slots, 1)
    both = jnp.where(here, mine, theirs)
    live = jnp.where(here, lane, lane - slots) < jnp.broadcast_to(both[2:3, :], lane.shape)
    live = jnp.logical_and(live, lane < 2 * slots)
    rows = jnp.where(live, jnp.broadcast_to(both[0:1, :], lane.shape), row_tiles).astype(F32)

    def along(x):
        return jnp.broadcast_to(x, (T, T))

    def down(x):
        return jnp.transpose(along(x))

    def parity(x):
        return x - 2.0 * jnp.floor(x * 0.5)

    def count(where):
        return jnp.sum(jnp.where(where, 1.0, 0.0), axis=0, keepdims=True)

    first = lax.broadcasted_iota(jnp.int32, (T, T), 0).astype(F32)
    second = lax.broadcasted_iota(jnp.int32, (T, T), 1).astype(F32)
    cols = both[1:2, :].astype(F32)
    own = jnp.logical_and(cols >= row_tiles, cols < 2 * row_tiles)
    key = rows[0:1, :] + jnp.where(own, 64.0, 0.0)
    key_a, key_d = along(key), down(key)
    row_d, col_d = down(rows[0:1, :]), down(cols)
    own_a, own_d = along(jnp.where(own, 1.0, 0.0)), down(jnp.where(own, 1.0, 0.0))
    rank = count(jnp.logical_and(key_a == key_d, first < second))
    rank_d = down(rank)
    odd = parity(rank_d) > 0.5
    even = jnp.logical_not(odd)
    lower = jnp.logical_and(key_d < key_a, own_d == own_a)
    before = count(jnp.logical_and(lower, even))
    place = jnp.where(rows[0:1, :] < row_tiles, before + jnp.floor(rank * 0.5), -1.0)
    hit = down(place) == second
    alive = row_d < row_tiles

    def pick(value, default, which):
        return (default + jnp.sum(jnp.where(which, value - default, 0.0), axis=0, keepdims=True)).astype(jnp.int32)

    out_ref[...] = jnp.zeros_like(out_ref)
    for base, mark in ((0, 0.0), (8, 1.0)):
        of_class = own_d == mark
        chosen = jnp.logical_and(hit, of_class)
        one, two = jnp.logical_and(chosen, even), jnp.logical_and(chosen, odd)
        out_ref[base : base + 1, :] = pick(row_d, float(row_tiles), one)
        out_ref[base + 1 : base + 2, :] = pick(first, 2.0 * slots, one)
        out_ref[base + 2 : base + 3, :] = pick(first, 2.0 * slots, two)
        out_ref[base + 3 : base + 4, :] = pick(col_d, 3.0 * row_tiles, one)
        out_ref[base + 4 : base + 5, :] = pick(col_d, 3.0 * row_tiles, two)
        pairs = count(jnp.logical_and(jnp.logical_and(of_class, alive), even))
        out_ref[base + 5 : base + 6, :] = pairs.astype(jnp.int32)


def for_pairs(pairs_ref, base, usual, most, body):
    for p in range(usual):
        body(p)

    @pl.when(pairs_ref[base + 5, 0] > usual)
    def _():
        for p in range(usual, most):
            body(p)


def prepare_kernel(
    mine, theirs, va_any, vb_any, order_ref, degree_ref, x_ref, g_ref, w_ref,
    xh_ref, gh_ref, hs_ref, sc_ref, sr_ref, tiles_ref, pairs_ref, sems,
):
    c = core_of()
    rows = x_ref.shape[0]
    slots = va_any.shape[0]
    copies = [
        pltpu.make_async_copy(va_any, tiles_ref.at[0:slots], sems.at[0]),
        pltpu.make_async_copy(vb_any, tiles_ref.at[slots : 2 * slots], sems.at[1]),
    ]
    for copy in copies:
        copy.start()
    tiles_ref[2 * slots] = jnp.zeros((T, T), BF)
    pair_slots(mine[...], theirs[...], slots, rows // T, pairs_ref)
    tiles = rows // T // 2
    deg = jnp.broadcast_to(degree_ref[...].astype(F32), (8, rows)).astype(BF)
    for i in range(tiles):
        column = order_column(order_ref[pl.ds(c * tiles + i, 1), :].astype(F32))
        hot = onehot_rows(column, rows)
        here = slice(i * T, (i + 1) * T)
        xt = mm(hot, x_ref[...]).astype(BF)
        xh_ref[here, :] = xt
        gh_ref[here, :] = mm(hot, g_ref[...]).astype(BF)
        hs_ref[here, :] = mm(xt, w_ref[...])
        scale = 1.0 / mm_nt(deg, hot)
        sr_ref[:, here] = scale
        sc_ref[here, :] = jnp.transpose(jnp.broadcast_to(scale[0:1, :], (T, T)))
    for copy in copies:
        copy.wait()


def near_part():
    return 2 - 2 * lax.rem(lax.axis_index("blk"), 2)


def gather_pair(pairs_ref, base, p, tiles_ref, window, acc):
    left = jnp.concatenate([tiles_ref[pairs_ref[base + 1, p]], tiles_ref[pairs_ref[base + 2, p]]], axis=1)
    right = jnp.concatenate([window(pairs_ref[base + 3, p]), window(pairs_ref[base + 4, p])], axis=0)
    acc[pairs_ref[base, p]] += mm(left, right)


def gather_own_kernel(pairs_ref, own_ref, tiles_ref, acc, win):
    rows = own_ref.shape[0]
    tiles = rows // T
    win[0:rows, :] = own_ref[...]
    win[rows : rows + T, :] = jnp.zeros((T, T), BF)
    acc[...] = jnp.zeros_like(acc)

    def window(col):
        return win[pl.ds(pl.multiple_of(jnp.minimum(col - tiles, tiles) * T, T), T), :]

    most = (tiles_ref.shape[0] - 1 + tiles) // 2
    for_pairs(pairs_ref, 8, most // 2, most, lambda p: gather_pair(pairs_ref, 8, p, tiles_ref, window, acc))


def gather_kernel(pairs_ref, near_ref, start_ref, far_ref, tiles_ref, here_ref, other_ref, win, acc):
    c, near = core_of(), near_part()
    rows = near_ref.shape[0]
    tiles = rows // T
    win[pl.ds(pl.multiple_of(near * rows, rows), rows), :] = near_ref[...]
    win[pl.ds(pl.multiple_of((2 - near) * rows, rows), rows), :] = far_ref[...]
    win[3 * rows : 3 * rows + T, :] = jnp.zeros((T, T), BF)
    acc[...] = start_ref[...]

    def window(col):
        return win[pl.ds(pl.multiple_of(col * T, T), T), :]

    most = (tiles_ref.shape[0] - 1 + tiles) // 2
    for_pairs(pairs_ref, 0, most * 3 // 4, most, lambda p: gather_pair(pairs_ref, 0, p, tiles_ref, window, acc))
    for i in range(tiles // 2):
        here_ref[i * T : (i + 1) * T, :] = acc[c * (tiles // 2) + i].astype(BF)
        other_ref[i * T : (i + 1) * T, :] = acc[(1 - c) * (tiles // 2) + i].astype(BF)


def dense_kernel(
    own_ref, y_ref, diag_ref, core_ref, hs_ref, gh_ref, sc_ref, sr_ref, wn_ref,
    act_ref, gp_ref, agg_ref, keep_ref, send_ref,
):
    c = core_of()
    scale = sc_ref[...]
    agg_ref[:, half_lanes(c)] = (
        (own_ref[...].astype(F32) + y_ref[...].astype(F32)) * scale
    ).astype(BF)
    agg_ref[:, half_lanes(1 - c)] = (
        (core_ref[...].astype(F32) + diag_ref[...].astype(F32)) * scale
    ).astype(BF)
    h = hs_ref[...] + mm(agg_ref[...], wn_ref[...])
    sig = jax.nn.sigmoid(h)
    act_ref[...] = (h * sig).astype(BF)
    gp = (gh_ref[...].astype(F32) * (sig * (1.0 + h * (1.0 - sig)))).astype(BF)
    gp_ref[...] = gp
    row = sr_ref[0:1, :]
    keep_ref[...] = (mm_nt(wn_ref[pl.ds(pl.multiple_of(c * T, T), T), :], gp) * row).astype(BF)
    send_ref[...] = (mm_nt(wn_ref[pl.ds(pl.multiple_of((1 - c) * T, T), T), :], gp) * row).astype(BF)


def dself_kernel(gp_ref, ws_ref, keep_ref, send_ref):
    c = core_of()
    keep_ref[...] = mm_nt(ws_ref[pl.ds(pl.multiple_of(c * T, T), T), :], gp_ref[...])
    send_ref[...] = mm_nt(ws_ref[pl.ds(pl.multiple_of((1 - c) * T, T), T), :], gp_ref[...])


def terms_kernel(xh_ref, agg_ref, gp_ref, *refs):
    c, y = core_of(), y_of()
    term_refs, full_ref = refs[:4], refs[4]
    gp = gp_ref[...]

    half = T // 2
    x = lax.rem(lax.axis_index("blk"), 2)

    def term(lhs_ref):
        for side, (keep, send) in ((c, term_refs[:2]), (1 - c, term_refs[2:])):
            full_ref[...] = mm_tn(lhs_ref[:, half_lanes(side)], gp)
            keep[...] = full_ref[pl.ds(pl.multiple_of(x * half, half), half), :].astype(BF)
            send[...] = full_ref[pl.ds(pl.multiple_of((1 - x) * half, half), half), :].astype(BF)

    @pl.when(y == 0)
    def _():
        term(xh_ref)

    @pl.when(y != 0)
    def _():
        term(agg_ref)


def scatter_pairs(pairs_ref, base, mine_ref, theirs_ref, tiles_ref, src, acc, at):
    c = core_of()
    half = mine_ref.shape[1]
    tiles = 2 * half // T
    ht = tiles // 2
    for i in range(ht):
        cut = slice(i * T, (i + 1) * T)
        src[c * ht + i] = mine_ref[:, cut]
        src[(1 - c) * ht + i] = theirs_ref[:, cut]
    src[tiles] = jnp.zeros((T, T), BF)
    acc[...] = jnp.zeros_like(acc)

    def body(p):
        right = jnp.concatenate(
            [tiles_ref[pairs_ref[base + 1, p]], tiles_ref[pairs_ref[base + 2, p]]], axis=1
        )
        prod = mm(src[pairs_ref[base, p]], right)
        acc[at(pairs_ref[base + 3, p])] += prod[:, :T]
        acc[at(pairs_ref[base + 4, p])] += prod[:, T:]

    most = (tiles_ref.shape[0] - 1 + tiles) // 2
    for_pairs(pairs_ref, base, most // 2 if base else most * 3 // 4, most, body)


def scatter_kernel(pairs_ref, mine_ref, theirs_ref, tiles_ref, near_ref, far_ref, src, acc):
    near = near_part()
    tiles = near_ref.shape[0]
    scatter_pairs(pairs_ref, 0, mine_ref, theirs_ref, tiles_ref, src, acc, lambda col: col)
    for i in range(tiles):
        near_ref[i] = acc[near * tiles + i].astype(BF)
        far_ref[i] = acc[(2 - near) * tiles + i].astype(BF)


def scatter_own_kernel(pairs_ref, mine_ref, theirs_ref, tiles_ref, after_ref, own_ref, src, acc):
    del after_ref
    tiles = own_ref.shape[0]
    scatter_pairs(
        pairs_ref, 8, mine_ref, theirs_ref, tiles_ref, src, acc, lambda col: jnp.minimum(col - tiles, tiles)
    )
    own_ref[...] = acc[0:tiles]


def chip_kernel(own_ref, a_ref, b_ref, g0_ref, g1_ref, g2_ref, g3_ref, out_ref, weights_ref):
    tiles = own_ref.shape[0]
    out_ref[0:tiles] = (own_ref[...] + (a_ref[...].astype(F32) + b_ref[...].astype(F32))).astype(BF)
    near = g0_ref[...].astype(F32) + g1_ref[...].astype(F32)
    weights = (near + (g2_ref[...].astype(F32) + g3_ref[...].astype(F32))).astype(BF)
    half = T // 2
    for ref in (weights_ref, out_ref.at[tiles]):
        ref[:half, :] = weights[:, :T]
        ref[half:, :] = weights[:, T:]


def total_kernel(mine_ref, theirs_ref, keep_ref, recv_ref, near_ref, near_y_ref, out_ref):
    c, y, x = core_of(), y_of(), lax.rem(lax.axis_index("blk"), 2)
    tiles = mine_ref.shape[0] - 1
    ht = tiles // 2
    for i in range(ht):
        cut = slice(i * T, (i + 1) * T)
        for first, ref in ((c * ht, keep_ref), ((1 - c) * ht, recv_ref)):
            both = mine_ref[first + i].astype(F32) + theirs_ref[first + i].astype(F32)
            out_ref[first + i] = (ref[:, cut] + both).astype(BF)
    out_ref[tiles + 2 * y + x] = mine_ref[tiles]
    out_ref[tiles + 2 * y + 1 - x] = near_ref[...]
    out_ref[tiles + 2 * (1 - y) + x] = theirs_ref[tiles]
    out_ref[tiles + 2 * (1 - y) + 1 - x] = near_y_ref[...]


def restore_kernel(order_ref, own_ref, core_ref, out_hbm, self_hbm, neigh_hbm, full, out, self_sum, neigh_sum, sems):
    c = core_of()
    rows = out.shape[0]
    half = T // 2
    for side, ref in ((c, own_ref), (1 - c, core_ref)):
        for x in range(2):
            at = pl.ds(pl.multiple_of(side * T + x * half, half), half)
            for i in range(2):
                cut = slice(i * T, (i + 1) * T)
                rows_of = slice(i * half, (i + 1) * half)
                self_sum[at, cut] = ref[rows // T + x, rows_of, :].astype(F32)
                neigh_sum[at, cut] = ref[rows // T + 2 + x, rows_of, :].astype(F32)
    copies = [
        pltpu.make_async_copy(self_sum, self_hbm, sems.at[0]),
        pltpu.make_async_copy(neigh_sum, neigh_hbm, sems.at[1]),
    ]
    for copy in copies:
        copy.start()
    for i in range(rows // T):
        cut = slice(i * T, (i + 1) * T)
        full[pl.ds(pl.multiple_of(c * T, T), T), cut] = own_ref[i]
        full[pl.ds(pl.multiple_of((1 - c) * T, T), T), cut] = core_ref[i]
    for j in range(rows // 256):
        here = slice(j * 256, (j + 1) * 256)
        hot = onehot_inverse(order_ref[...], j * 256, 256)
        out[here, :] = mm_nt(hot, full[...]).astype(BF)
        copies.append(pltpu.make_async_copy(out.at[here], out_hbm.at[here], sems.at[2 + j]))
        copies[-1].start()
    for copy in copies:
        copy.wait()


def output_kernel(order_ref, own_ref, core_ref, out_ref, full):
    c = core_of()
    half = own_ref.shape[0]
    rows = 2 * half
    full[pl.ds(pl.multiple_of(c * half, half), half), :] = own_ref[...]
    full[pl.ds(pl.multiple_of((1 - c) * half, half), half), :] = core_ref[...]
    for j in range(rows // 256):
        hot = onehot_inverse(order_ref[...], j * 256, 256)
        out_ref[j * 256 : (j + 1) * 256, :] = mm(hot, full[...]).astype(BF)


def call(kernel, outs, ins, spaces=None, scratch=(), name=None, out_spaces=None):
    spaces = dict(spaces or {})
    out_spaces = dict(out_spaces or {})
    specs = [pl.BlockSpec(memory_space=spaces.get(i, pltpu.VMEM)) for i in range(len(ins))]
    shapes = [jax.ShapeDtypeStruct(s, d) for s, d in outs]
    out_specs = [pl.BlockSpec(memory_space=out_spaces.get(i, pltpu.VMEM)) for i in range(len(outs))]
    single = len(outs) == 1
    return pl.pallas_call(
        kernel,
        out_shape=shapes[0] if single else shapes,
        in_specs=specs,
        out_specs=out_specs[0] if single else out_specs,
        scratch_shapes=list(scratch),
        name=name,
        compiler_params=pltpu.CompilerParams(vmem_limit_bytes=VMEM),
        cost_estimate=pl.CostEstimate(flops=0, bytes_accessed=0, transcendentals=0),
    )(*ins)


def shards(
    features, degree, order, tile_rows, tile_cols, tile_count, tile_values, w_self, w_neigh, out_grad
):
    rows, width = features.shape
    half = rows // 2
    tiles = rows // T
    ht = tiles // 2
    blocks = lax.axis_size("blk")
    reps = lax.axis_size("rep")
    assert reps == 4 and width == 2 * T

    def swap_near(x):
        return lax.ppermute(x, "blk", [(b, b ^ 1) for b in range(blocks)])

    def swap_far(x):
        return lax.ppermute(x, "blk", [(b, (b + 2 * (b % 2) - 1) % blocks) for b in range(blocks)])

    def swap_core(x):
        return lax.ppermute(x, "rep", [(r, r ^ 1) for r in range(reps)])

    def swap_y(x):
        return lax.ppermute(x, "rep", [(r, r ^ 2) for r in range(reps)])

    def swap_diag(x):
        return lax.ppermute(x, "rep", [(r, r ^ 3) for r in range(reps)])

    def stay(x):
        return pltpu.with_memory_space_constraint(x, pltpu.MemorySpace.HBM)

    order8 = stay(order.reshape(tiles, T))
    deg = stay(degree.reshape(1, rows))
    features, out_grad = stay(features), stay(out_grad)
    va = tile_values[0, 0]
    slots = va.shape[0]
    hbm = pltpu.MemorySpace.HBM
    smem = pltpu.SMEM
    dma = pltpu.SemaphoreType.DMA

    feats_c = call(
        reorder_kernel,
        [((rows, T), BF)],
        [order8, features],
        spaces={0: hbm, 1: hbm},
        scratch=[pltpu.VMEM((tiles, T), jnp.int32), pltpu.VMEM((rows, T), BF), dma((2,))],
        name="reorder",
    )
    mine = call(
        index_kernel,
        [((8, T), jnp.int32)],
        [tile_count, stay(tile_rows[0]), stay(tile_cols[0]), feats_c],
        spaces={0: smem, 3: pl.ANY},
        name="index",
    )
    near = swap_near(feats_c)
    far = swap_far(feats_c)
    theirs = swap_core(mine)
    vb = swap_core(va)
    va = stay(va)
    xh, gh, hs, sc, sr, both, pairs = call(
        prepare_kernel,
        [
            ((half, width), BF),
            ((half, width), BF),
            ((half, width), F32),
            ((half, T), F32),
            ((8, half), F32),
            ((2 * slots + 1, T, T), BF),
            ((16, T), jnp.int32),
        ],
        [mine, theirs, va, vb, order8, deg, features, out_grad, stay(w_self)],
        spaces={2: pl.ANY, 3: pl.ANY},
        scratch=[dma((2,))],
        name="prepare",
    )
    part = call(
        gather_own_kernel,
        [((tiles + 1, T, T), F32)],
        [pairs, feats_c, both],
        spaces={0: smem},
        scratch=[pltpu.VMEM((rows + T, T), BF)],
        name="gather_own",
    )
    here, other = call(
        gather_kernel,
        [((half, T), BF), ((half, T), BF)],
        [pairs, near, part, far, both],
        spaces={0: smem},
        scratch=[pltpu.VMEM((3 * rows + T, T), BF), pltpu.VMEM((tiles + 1, T, T), F32)],
        name="gather",
    )
    from_y = swap_y(here)
    from_diag = swap_diag(other)
    from_core = swap_core(other)
    act, gp, agg, s_keep, s_send = call(
        dense_kernel,
        [((half, width), BF), ((half, width), BF), ((half, width), BF), ((T, half), BF), ((T, half), BF)],
        [here, from_y, from_diag, from_core, hs, gh, sc, sr, w_neigh],
        name="dense",
    )
    s_other = swap_core(s_send)
    mine_near, mine_far, theirs_near, theirs_far = call(
        terms_kernel,
        [((T // 2, width), BF)] * 4,
        [xh, agg, gp],
        scratch=[pltpu.VMEM((T, width), F32)],
        name="terms",
    )
    def swap_pair(x, mask):
        pairs_of = [(b * reps + r, (b ^ 1) * reps + (r ^ mask)) for b in range(blocks) for r in range(reps)]
        return lax.ppermute(x, ("blk", "rep"), pairs_of)

    terms_in = [mine_near, swap_core(theirs_near), swap_pair(mine_far, 0), swap_pair(theirs_far, 1)]
    piece = (tiles, T, T)
    near, far = call(
        scatter_kernel,
        [(piece, BF)] * 2,
        [pairs, s_keep, s_other, both],
        spaces={0: smem},
        scratch=[pltpu.VMEM((tiles + 1, T, T), BF), pltpu.VMEM((3 * tiles + 1, T, T), F32)],
        name="scatter",
    )
    own = call(
        scatter_own_kernel,
        [(piece, F32)],
        [pairs, s_keep, s_other, both, near],
        spaces={0: smem, 4: pl.ANY},
        scratch=[pltpu.VMEM((tiles + 1, T, T), BF), pltpu.VMEM((tiles + 1, T, T), F32)],
        name="scatter_own",
    )
    from_near = swap_near(near)
    from_far = swap_far(far)
    d_keep, d_send = call(dself_kernel, [((T, half), F32)] * 2, [gp, w_self], name="dself")
    d_recv = swap_core(d_send)
    bits = blocks.bit_length() - 1
    assert blocks == 1 << bits and bits % 2 and bits > 1

    def four(p, q, r, s):
        near = p.astype(F32) + q.astype(F32)
        return (near + (r.astype(F32) + s.astype(F32))).astype(BF)

    parts = terms_in
    for at in range(1, bits, 2):
        g = four(*parts)
        parts = [g] + [
            lax.ppermute(g, "blk", [(b, b ^ (k << at)) for b in range(blocks)]) for k in (1, 2, 3)
        ]
    chip, w_own = call(chip_kernel, [((tiles + 1, T, T), BF), ((T, T), BF)], [own, from_near, from_far] + parts, name="chip")
    chip, act = lax.optimization_barrier((chip, act))
    chip_y = swap_y(chip)
    w_near = swap_pair(w_own, 0)
    w_near_y = swap_pair(w_own, 2)
    act_other = swap_core(act)
    output = call(
        output_kernel,
        [((rows, width), BF)],
        [order, act, act_other],
        scratch=[pltpu.VMEM((rows, width), BF)],
        name="output",
    )
    chip_y, output = lax.optimization_barrier((chip_y, output))
    total = call(total_kernel, [((tiles + 4, T, T), BF)], [chip, chip_y, d_keep, d_recv, w_near, w_near_y], name="total")
    total_core = swap_core(total)
    grad_features, grad_self, grad_neigh = call(
        restore_kernel,
        [((rows, width), BF), ((width, width), F32), ((width, width), F32)],
        [order, total, total_core],
        out_spaces={i: pl.ANY for i in range(3)},
        scratch=[
            pltpu.VMEM((width, rows), BF),
            pltpu.VMEM((rows, width), BF),
            pltpu.VMEM((width, width), F32),
            pltpu.VMEM((width, width), F32),
            dma((2 + rows // 256,)),
        ],
        name="restore",
    )
    return output, grad_features, grad_self, grad_neigh


def solution(mesh):
    return jax.shard_map(
        shards,
        mesh=mesh,
        in_specs=(
            P("blk", None),
            P("blk"),
            P("blk", None),
            P("blk", "rep", None),
            P("blk", "rep", None),
            P("blk", "rep"),
            P("blk", "rep", None, None, None),
            P(),
            P(),
            P("blk", None),
        ),
        out_specs=(P("blk", None), P("blk", None), P(), P()),
        check_vma=False,
    )
```

```python
import jax
import jax.numpy as jnp
from jax import lax
from jax.experimental import pallas as pl
from jax.experimental.pallas import tpu as pltpu
from jax.sharding import PartitionSpec as P

BF = jnp.bfloat16
F32 = jnp.float32
T = 128
VMEM = 16 * 2**20


def mm(a, b):
    return jnp.dot(a, b, preferred_element_type=F32)


def mm_nt(a, b):
    return lax.dot_general(a, b, (((1,), (1,)), ((), ())), preferred_element_type=F32)


def mm_tn(a, b):
    return lax.dot_general(a, b, (((0,), (0,)), ((), ())), preferred_element_type=F32)


def core_of():
    return lax.rem(lax.axis_index("rep"), 2)


def y_of():
    return lax.div(lax.axis_index("rep"), 2)


def order_column(order_row):
    return jnp.transpose(jnp.broadcast_to(order_row, (T, T)))


def onehot_rows(column, count):
    lane = lax.broadcasted_iota(jnp.int32, (T, T), 1).astype(F32)
    cuts = [
        jnp.where(column == lane + float(j * T), 1.0, 0.0).astype(BF) for j in range(count // T)
    ]
    return jnp.concatenate(cuts, axis=1)


def onehot_inverse(order_row, first, rows):
    wide = (rows, order_row.shape[1])
    at = lax.broadcasted_iota(jnp.int32, wide, 0) + first
    return jnp.where(jnp.broadcast_to(order_row, wide) == at, 1.0, 0.0).astype(BF)


def half_lanes(index):
    return pl.ds(pl.multiple_of(index * T, T), T)


def reorder_kernel(order_hbm, x_hbm, out_ref, order, x, sems):
    total = out_ref.shape[0]
    first = pltpu.make_async_copy(order_hbm, order, sems.at[0])
    second = pltpu.make_async_copy(x_hbm.at[:, half_lanes(core_of())], x, sems.at[1])
    first.start()
    second.start()
    first.wait()
    columns = [order_column(order[i : i + 1, :].astype(F32)) for i in range(total // T)]
    second.wait()
    for i in range(total // T):
        out_ref[i * T : (i + 1) * T, :] = mm(onehot_rows(columns[i], total), x[...]).astype(BF)


def index_kernel(count_ref, rows_ref, cols_ref, after_ref, idx_ref):
    del after_ref
    slots = rows_ref.shape[1]
    idx_ref[...] = jnp.zeros_like(idx_ref)
    idx_ref[0:1, 0:slots] = rows_ref[...]
    idx_ref[1:2, 0:slots] = cols_ref[...]
    idx_ref[2:3, :] = jnp.full((1, T), count_ref[0, 0], jnp.int32)


def pair_slots(mine, theirs, slots, row_tiles, out_ref):
    lane = lax.broadcasted_iota(jnp.int32, mine.shape, 1)
    here = lane < slots
    theirs = pltpu.roll(theirs, slots, 1)
    both = jnp.where(here, mine, theirs)
    live = jnp.where(here, lane, lane - slots) < jnp.broadcast_to(both[2:3, :], lane.shape)
    live = jnp.logical_and(live, lane < 2 * slots)
    rows = jnp.where(live, jnp.broadcast_to(both[0:1, :], lane.shape), row_tiles).astype(F32)

    def along(x):
        return jnp.broadcast_to(x, (T, T))

    def down(x):
        return jnp.transpose(along(x))

    def parity(x):
        return x - 2.0 * jnp.floor(x * 0.5)

    def count(where):
        return jnp.sum(jnp.where(where, 1.0, 0.0), axis=0, keepdims=True)

    first = lax.broadcasted_iota(jnp.int32, (T, T), 0).astype(F32)
    second = lax.broadcasted_iota(jnp.int32, (T, T), 1).astype(F32)
    cols = both[1:2, :].astype(F32)
    own = jnp.logical_and(cols >= row_tiles, cols < 2 * row_tiles)
    key = rows[0:1, :] + jnp.where(own, 64.0, 0.0)
    key_a, key_d = along(key), down(key)
    row_d, col_d = down(rows[0:1, :]), down(cols)
    own_a, own_d = along(jnp.where(own, 1.0, 0.0)), down(jnp.where(own, 1.0, 0.0))
    rank = count(jnp.logical_and(key_a == key_d, first < second))
    rank_d = down(rank)
    odd = parity(rank_d) > 0.5
    even = jnp.logical_not(odd)
    lower = jnp.logical_and(key_d < key_a, own_d == own_a)
    before = count(jnp.logical_and(lower, even))
    place = jnp.where(rows[0:1, :] < row_tiles, before + jnp.floor(rank * 0.5), -1.0)
    hit = down(place) == second
    alive = row_d < row_tiles

    def pick(value, default, which):
        return (default + jnp.sum(jnp.where(which, value - default, 0.0), axis=0, keepdims=True)).astype(jnp.int32)

    out_ref[...] = jnp.zeros_like(out_ref)
    for base, mark in ((0, 0.0), (8, 1.0)):
        of_class = own_d == mark
        chosen = jnp.logical_and(hit, of_class)
        one, two = jnp.logical_and(chosen, even), jnp.logical_and(chosen, odd)
        out_ref[base : base + 1, :] = pick(row_d, float(row_tiles), one)
        out_ref[base + 1 : base + 2, :] = pick(first, 2.0 * slots, one)
        out_ref[base + 2 : base + 3, :] = pick(first, 2.0 * slots, two)
        out_ref[base + 3 : base + 4, :] = pick(col_d, 3.0 * row_tiles, one)
        out_ref[base + 4 : base + 5, :] = pick(col_d, 3.0 * row_tiles, two)
        pairs = count(jnp.logical_and(jnp.logical_and(of_class, alive), even))
        out_ref[base + 5 : base + 6, :] = pairs.astype(jnp.int32)


def for_pairs(pairs_ref, base, usual, most, body):
    for p in range(usual):
        body(p)

    @pl.when(pairs_ref[base + 5, 0] > usual)
    def _():
        for p in range(usual, most):
            body(p)


def prepare_kernel(
    mine, theirs, va_any, vb_any, order_ref, degree_ref, x_ref, g_ref, w_ref,
    xh_ref, gh_ref, hs_ref, sc_ref, sr_ref, tiles_ref, pairs_ref, sems,
):
    c = core_of()
    rows = x_ref.shape[0]
    slots = va_any.shape[0]
    copies = [
        pltpu.make_async_copy(va_any, tiles_ref.at[0:slots], sems.at[0]),
        pltpu.make_async_copy(vb_any, tiles_ref.at[slots : 2 * slots], sems.at[1]),
    ]
    for copy in copies:
        copy.start()
    tiles_ref[2 * slots] = jnp.zeros((T, T), BF)
    pair_slots(mine[...], theirs[...], slots, rows // T, pairs_ref)
    tiles = rows // T // 2
    deg = jnp.broadcast_to(degree_ref[...].astype(F32), (8, rows)).astype(BF)
    for i in range(tiles):
        column = order_column(order_ref[pl.ds(c * tiles + i, 1), :].astype(F32))
        hot = onehot_rows(column, rows)
        here = slice(i * T, (i + 1) * T)
        xt = mm(hot, x_ref[...]).astype(BF)
        xh_ref[here, :] = xt
        gh_ref[here, :] = mm(hot, g_ref[...]).astype(BF)
        hs_ref[here, :] = mm(xt, w_ref[...])
        scale = 1.0 / mm_nt(deg, hot)
        sr_ref[:, here] = scale
        sc_ref[here, :] = jnp.transpose(jnp.broadcast_to(scale[0:1, :], (T, T)))
    for copy in copies:
        copy.wait()


def near_part():
    return 2 - 2 * lax.rem(lax.axis_index("blk"), 2)


def gather_pair(pairs_ref, base, p, tiles_ref, window, acc):
    left = jnp.concatenate([tiles_ref[pairs_ref[base + 1, p]], tiles_ref[pairs_ref[base + 2, p]]], axis=1)
    right = jnp.concatenate([window(pairs_ref[base + 3, p]), window(pairs_ref[base + 4, p])], axis=0)
    acc[pairs_ref[base, p]] += mm(left, right)


def gather_own_kernel(pairs_ref, own_ref, tiles_ref, acc, win):
    rows = own_ref.shape[0]
    tiles = rows // T
    win[0:rows, :] = own_ref[...]
    win[rows : rows + T, :] = jnp.zeros((T, T), BF)
    acc[...] = jnp.zeros_like(acc)

    def window(col):
        return win[pl.ds(pl.multiple_of(jnp.minimum(col - tiles, tiles) * T, T), T), :]

    most = (tiles_ref.shape[0] - 1 + tiles) // 2
    for_pairs(pairs_ref, 8, most // 2, most, lambda p: gather_pair(pairs_ref, 8, p, tiles_ref, window, acc))


def gather_kernel(pairs_ref, near_ref, start_ref, far_ref, tiles_ref, here_ref, other_ref, win, acc):
    c, near = core_of(), near_part()
    rows = near_ref.shape[0]
    tiles = rows // T
    win[pl.ds(pl.multiple_of(near * rows, rows), rows), :] = near_ref[...]
    win[pl.ds(pl.multiple_of((2 - near) * rows, rows), rows), :] = far_ref[...]
    win[3 * rows : 3 * rows + T, :] = jnp.zeros((T, T), BF)
    acc[...] = start_ref[...]

    def window(col):
        return win[pl.ds(pl.multiple_of(col * T, T), T), :]

    most = (tiles_ref.shape[0] - 1 + tiles) // 2
    for_pairs(pairs_ref, 0, most * 5 // 6, most, lambda p: gather_pair(pairs_ref, 0, p, tiles_ref, window, acc))
    for i in range(tiles // 2):
        here_ref[i * T : (i + 1) * T, :] = acc[c * (tiles // 2) + i].astype(BF)
        other_ref[i * T : (i + 1) * T, :] = acc[(1 - c) * (tiles // 2) + i].astype(BF)


def dense_kernel(
    own_ref, y_ref, diag_ref, core_ref, hs_ref, gh_ref, sc_ref, sr_ref, wn_ref,
    act_ref, gp_ref, agg_ref, keep_ref, send_ref,
):
    c = core_of()
    scale = sc_ref[...]
    agg_ref[:, half_lanes(c)] = (
        (own_ref[...].astype(F32) + y_ref[...].astype(F32)) * scale
    ).astype(BF)
    agg_ref[:, half_lanes(1 - c)] = (
        (core_ref[...].astype(F32) + diag_ref[...].astype(F32)) * scale
    ).astype(BF)
    h = hs_ref[...] + mm(agg_ref[...], wn_ref[...])
    sig = jax.nn.sigmoid(h)
    act_ref[...] = (h * sig).astype(BF)
    gp = (gh_ref[...].astype(F32) * (sig * (1.0 + h * (1.0 - sig)))).astype(BF)
    gp_ref[...] = gp
    row = sr_ref[0:1, :]
    keep_ref[...] = (mm_nt(wn_ref[pl.ds(pl.multiple_of(c * T, T), T), :], gp) * row).astype(BF)
    send_ref[...] = (mm_nt(wn_ref[pl.ds(pl.multiple_of((1 - c) * T, T), T), :], gp) * row).astype(BF)


def dself_kernel(gp_ref, ws_ref, keep_ref, send_ref):
    c = core_of()
    keep_ref[...] = mm_nt(ws_ref[pl.ds(pl.multiple_of(c * T, T), T), :], gp_ref[...])
    send_ref[...] = mm_nt(ws_ref[pl.ds(pl.multiple_of((1 - c) * T, T), T), :], gp_ref[...])


def terms_kernel(xh_ref, agg_ref, gp_ref, *refs):
    c, y = core_of(), y_of()
    term_refs, full_ref = refs[:4], refs[4]
    gp = gp_ref[...]

    half = T // 2
    x = lax.rem(lax.axis_index("blk"), 2)

    def term(lhs_ref):
        for side, (keep, send) in ((c, term_refs[:2]), (1 - c, term_refs[2:])):
            full_ref[...] = mm_tn(lhs_ref[:, half_lanes(side)], gp)
            keep[...] = full_ref[pl.ds(pl.multiple_of(x * half, half), half), :].astype(BF)
            send[...] = full_ref[pl.ds(pl.multiple_of((1 - x) * half, half), half), :].astype(BF)

    @pl.when(y == 0)
    def _():
        term(xh_ref)

    @pl.when(y != 0)
    def _():
        term(agg_ref)


def scatter_pairs(pairs_ref, base, mine_ref, theirs_ref, tiles_ref, src, acc, at):
    c = core_of()
    half = mine_ref.shape[1]
    tiles = 2 * half // T
    ht = tiles // 2
    for i in range(ht):
        cut = slice(i * T, (i + 1) * T)
        src[c * ht + i] = mine_ref[:, cut]
        src[(1 - c) * ht + i] = theirs_ref[:, cut]
    src[tiles] = jnp.zeros((T, T), BF)
    acc[...] = jnp.zeros_like(acc)

    def body(p):
        right = jnp.concatenate(
            [tiles_ref[pairs_ref[base + 1, p]], tiles_ref[pairs_ref[base + 2, p]]], axis=1
        )
        prod = mm(src[pairs_ref[base, p]], right)
        acc[at(pairs_ref[base + 3, p])] += prod[:, :T]
        acc[at(pairs_ref[base + 4, p])] += prod[:, T:]

    most = (tiles_ref.shape[0] - 1 + tiles) // 2
    for_pairs(pairs_ref, base, most // 2 if base else most * 5 // 6, most, body)


def scatter_kernel(pairs_ref, mine_ref, theirs_ref, tiles_ref, near_ref, far_ref, src, acc):
    near = near_part()
    tiles = near_ref.shape[0]
    scatter_pairs(pairs_ref, 0, mine_ref, theirs_ref, tiles_ref, src, acc, lambda col: col)
    for i in range(tiles):
        near_ref[i] = acc[near * tiles + i].astype(BF)
        far_ref[i] = acc[(2 - near) * tiles + i].astype(BF)


def scatter_own_kernel(pairs_ref, mine_ref, theirs_ref, tiles_ref, after_ref, own_ref, src, acc):
    del after_ref
    tiles = own_ref.shape[0]
    scatter_pairs(
        pairs_ref, 8, mine_ref, theirs_ref, tiles_ref, src, acc, lambda col: jnp.minimum(col - tiles, tiles)
    )
    own_ref[...] = acc[0:tiles]


def chip_kernel(own_ref, a_ref, b_ref, g0_ref, g1_ref, g2_ref, g3_ref, out_ref, weights_ref):
    tiles = own_ref.shape[0]
    out_ref[0:tiles] = (own_ref[...] + (a_ref[...].astype(F32) + b_ref[...].astype(F32))).astype(BF)
    near = g0_ref[...].astype(F32) + g1_ref[...].astype(F32)
    weights = (near + (g2_ref[...].astype(F32) + g3_ref[...].astype(F32))).astype(BF)
    half = T // 2
    for ref in (weights_ref, out_ref.at[tiles]):
        ref[:half, :] = weights[:, :T]
        ref[half:, :] = weights[:, T:]


def total_kernel(mine_ref, theirs_ref, keep_ref, recv_ref, near_ref, near_y_ref, out_ref):
    c, y, x = core_of(), y_of(), lax.rem(lax.axis_index("blk"), 2)
    tiles = mine_ref.shape[0] - 1
    ht = tiles // 2
    for i in range(ht):
        cut = slice(i * T, (i + 1) * T)
        for first, ref in ((c * ht, keep_ref), ((1 - c) * ht, recv_ref)):
            both = mine_ref[first + i].astype(F32) + theirs_ref[first + i].astype(F32)
            out_ref[first + i] = (ref[:, cut] + both).astype(BF)
    out_ref[tiles + 2 * y + x] = mine_ref[tiles]
    out_ref[tiles + 2 * y + 1 - x] = near_ref[...]
    out_ref[tiles + 2 * (1 - y) + x] = theirs_ref[tiles]
    out_ref[tiles + 2 * (1 - y) + 1 - x] = near_y_ref[...]


def restore_kernel(order_ref, own_ref, core_ref, out_hbm, self_hbm, neigh_hbm, full, out, self_sum, neigh_sum, sems):
    c = core_of()
    rows = out.shape[0]
    half = T // 2
    for side, ref in ((c, own_ref), (1 - c, core_ref)):
        for x in range(2):
            at = pl.ds(pl.multiple_of(side * T + x * half, half), half)
            for i in range(2):
                cut = slice(i * T, (i + 1) * T)
                rows_of = slice(i * half, (i + 1) * half)
                self_sum[at, cut] = ref[rows // T + x, rows_of, :].astype(F32)
                neigh_sum[at, cut] = ref[rows // T + 2 + x, rows_of, :].astype(F32)
    copies = [
        pltpu.make_async_copy(self_sum, self_hbm, sems.at[0]),
        pltpu.make_async_copy(neigh_sum, neigh_hbm, sems.at[1]),
    ]
    for copy in copies:
        copy.start()
    for i in range(rows // T):
        cut = slice(i * T, (i + 1) * T)
        full[pl.ds(pl.multiple_of(c * T, T), T), cut] = own_ref[i]
        full[pl.ds(pl.multiple_of((1 - c) * T, T), T), cut] = core_ref[i]
    for j in range(rows // 256):
        here = slice(j * 256, (j + 1) * 256)
        hot = onehot_inverse(order_ref[...], j * 256, 256)
        out[here, :] = mm_nt(hot, full[...]).astype(BF)
        copies.append(pltpu.make_async_copy(out.at[here], out_hbm.at[here], sems.at[2 + j]))
        copies[-1].start()
    for copy in copies:
        copy.wait()


def output_kernel(order_ref, own_ref, core_ref, out_ref, full):
    c = core_of()
    half = own_ref.shape[0]
    rows = 2 * half
    full[pl.ds(pl.multiple_of(c * half, half), half), :] = own_ref[...]
    full[pl.ds(pl.multiple_of((1 - c) * half, half), half), :] = core_ref[...]
    for j in range(rows // 256):
        hot = onehot_inverse(order_ref[...], j * 256, 256)
        out_ref[j * 256 : (j + 1) * 256, :] = mm(hot, full[...]).astype(BF)


def call(kernel, outs, ins, spaces=None, scratch=(), name=None, out_spaces=None):
    spaces = dict(spaces or {})
    out_spaces = dict(out_spaces or {})
    specs = [pl.BlockSpec(memory_space=spaces.get(i, pltpu.VMEM)) for i in range(len(ins))]
    shapes = [jax.ShapeDtypeStruct(s, d) for s, d in outs]
    out_specs = [pl.BlockSpec(memory_space=out_spaces.get(i, pltpu.VMEM)) for i in range(len(outs))]
    single = len(outs) == 1
    return pl.pallas_call(
        kernel,
        out_shape=shapes[0] if single else shapes,
        in_specs=specs,
        out_specs=out_specs[0] if single else out_specs,
        scratch_shapes=list(scratch),
        name=name,
        compiler_params=pltpu.CompilerParams(vmem_limit_bytes=VMEM),
        cost_estimate=pl.CostEstimate(flops=0, bytes_accessed=0, transcendentals=0),
    )(*ins)


def shards(
    features, degree, order, tile_rows, tile_cols, tile_count, tile_values, w_self, w_neigh, out_grad
):
    rows, width = features.shape
    half = rows // 2
    tiles = rows // T
    ht = tiles // 2
    blocks = lax.axis_size("blk")
    reps = lax.axis_size("rep")
    assert reps == 4 and width == 2 * T

    def swap_near(x):
        return lax.ppermute(x, "blk", [(b, b ^ 1) for b in range(blocks)])

    def swap_far(x):
        return lax.ppermute(x, "blk", [(b, (b + 2 * (b % 2) - 1) % blocks) for b in range(blocks)])

    def swap_core(x):
        return lax.ppermute(x, "rep", [(r, r ^ 1) for r in range(reps)])

    def swap_y(x):
        return lax.ppermute(x, "rep", [(r, r ^ 2) for r in range(reps)])

    def swap_diag(x):
        return lax.ppermute(x, "rep", [(r, r ^ 3) for r in range(reps)])

    def stay(x):
        return pltpu.with_memory_space_constraint(x, pltpu.MemorySpace.HBM)

    order8 = stay(order.reshape(tiles, T))
    deg = stay(degree.reshape(1, rows))
    features, out_grad = stay(features), stay(out_grad)
    va = tile_values[0, 0]
    slots = va.shape[0]
    hbm = pltpu.MemorySpace.HBM
    smem = pltpu.SMEM
    dma = pltpu.SemaphoreType.DMA

    feats_c = call(
        reorder_kernel,
        [((rows, T), BF)],
        [order8, features],
        spaces={0: hbm, 1: hbm},
        scratch=[pltpu.VMEM((tiles, T), jnp.int32), pltpu.VMEM((rows, T), BF), dma((2,))],
        name="reorder",
    )
    mine = call(
        index_kernel,
        [((8, T), jnp.int32)],
        [tile_count, stay(tile_rows[0]), stay(tile_cols[0]), feats_c],
        spaces={0: smem, 3: pl.ANY},
        name="index",
    )
    near = swap_near(feats_c)
    far = swap_far(feats_c)
    theirs = swap_core(mine)
    vb = swap_core(va)
    va = stay(va)
    xh, gh, hs, sc, sr, both, pairs = call(
        prepare_kernel,
        [
            ((half, width), BF),
            ((half, width), BF),
            ((half, width), F32),
            ((half, T), F32),
            ((8, half), F32),
            ((2 * slots + 1, T, T), BF),
            ((16, T), jnp.int32),
        ],
        [mine, theirs, va, vb, order8, deg, features, out_grad, stay(w_self)],
        spaces={2: pl.ANY, 3: pl.ANY},
        scratch=[dma((2,))],
        name="prepare",
    )
    part = call(
        gather_own_kernel,
        [((tiles + 1, T, T), F32)],
        [pairs, feats_c, both],
        spaces={0: smem},
        scratch=[pltpu.VMEM((rows + T, T), BF)],
        name="gather_own",
    )
    here, other = call(
        gather_kernel,
        [((half, T), BF), ((half, T), BF)],
        [pairs, near, part, far, both],
        spaces={0: smem},
        scratch=[pltpu.VMEM((3 * rows + T, T), BF), pltpu.VMEM((tiles + 1, T, T), F32)],
        name="gather",
    )
    from_y = swap_y(here)
    from_diag = swap_diag(other)
    from_core = swap_core(other)
    act, gp, agg, s_keep, s_send = call(
        dense_kernel,
        [((half, width), BF), ((half, width), BF), ((half, width), BF), ((T, half), BF), ((T, half), BF)],
        [here, from_y, from_diag, from_core, hs, gh, sc, sr, w_neigh],
        name="dense",
    )
    s_other = swap_core(s_send)
    mine_near, mine_far, theirs_near, theirs_far = call(
        terms_kernel,
        [((T // 2, width), BF)] * 4,
        [xh, agg, gp],
        scratch=[pltpu.VMEM((T, width), F32)],
        name="terms",
    )
    def swap_pair(x, mask):
        pairs_of = [(b * reps + r, (b ^ 1) * reps + (r ^ mask)) for b in range(blocks) for r in range(reps)]
        return lax.ppermute(x, ("blk", "rep"), pairs_of)

    terms_in = [mine_near, swap_core(theirs_near), swap_pair(mine_far, 0), swap_pair(theirs_far, 1)]
    piece = (tiles, T, T)
    near, far = call(
        scatter_kernel,
        [(piece, BF)] * 2,
        [pairs, s_keep, s_other, both],
        spaces={0: smem},
        scratch=[pltpu.VMEM((tiles + 1, T, T), BF), pltpu.VMEM((3 * tiles + 1, T, T), F32)],
        name="scatter",
    )
    own = call(
        scatter_own_kernel,
        [(piece, F32)],
        [pairs, s_keep, s_other, both, near],
        spaces={0: smem, 4: pl.ANY},
        scratch=[pltpu.VMEM((tiles + 1, T, T), BF), pltpu.VMEM((tiles + 1, T, T), F32)],
        name="scatter_own",
    )
    from_near = swap_near(near)
    from_far = swap_far(far)
    d_keep, d_send = call(dself_kernel, [((T, half), F32)] * 2, [gp, w_self], name="dself")
    d_recv = swap_core(d_send)
    bits = blocks.bit_length() - 1
    assert blocks == 1 << bits and bits % 2 and bits > 1

    def four(p, q, r, s):
        near = p.astype(F32) + q.astype(F32)
        return (near + (r.astype(F32) + s.astype(F32))).astype(BF)

    parts = terms_in
    for at in range(1, bits, 2):
        g = four(*parts)
        parts = [g] + [
            lax.ppermute(g, "blk", [(b, b ^ (k << at)) for b in range(blocks)]) for k in (3, 2, 1)
        ]
    chip, w_own = call(chip_kernel, [((tiles + 1, T, T), BF), ((T, T), BF)], [own, from_near, from_far] + parts, name="chip")
    chip, act = lax.optimization_barrier((chip, act))
    chip_y = swap_y(chip)
    w_near = swap_pair(w_own, 0)
    w_near_y = swap_pair(w_own, 2)
    act_other = swap_core(act)
    output = call(
        output_kernel,
        [((rows, width), BF)],
        [order, act, act_other],
        scratch=[pltpu.VMEM((rows, width), BF)],
        name="output",
    )
    chip_y, output = lax.optimization_barrier((chip_y, output))
    total = call(total_kernel, [((tiles + 4, T, T), BF)], [chip, chip_y, d_keep, d_recv, w_near, w_near_y], name="total")
    total_core = swap_core(total)
    grad_features, grad_self, grad_neigh = call(
        restore_kernel,
        [((rows, width), BF), ((width, width), F32), ((width, width), F32)],
        [order, total, total_core],
        out_spaces={i: pl.ANY for i in range(3)},
        scratch=[
            pltpu.VMEM((width, rows), BF),
            pltpu.VMEM((rows, width), BF),
            pltpu.VMEM((width, width), F32),
            pltpu.VMEM((width, width), F32),
            dma((2 + rows // 256,)),
        ],
        name="restore",
    )
    return output, grad_features, grad_self, grad_neigh


def solution(mesh):
    return jax.shard_map(
        shards,
        mesh=mesh,
        in_specs=(
            P("blk", None),
            P("blk"),
            P("blk", None),
            P("blk", "rep", None),
            P("blk", "rep", None),
            P("blk", "rep"),
            P("blk", "rep", None, None, None),
            P(),
            P(),
            P("blk", None),
        ),
        out_specs=(P("blk", None), P("blk", None), P(), P()),
        check_vma=False,
    )
```
